32 devices in a mesh: row: 8 (over z, y), col: 4 (over x, core).
Axes of the slice: x: 2, y: 2, z: 4, core: 2. Of those that a mesh axis runs over, the one named last changes fastest.
Arguments:
- patches: bfloat16 [160, 480, 512], P('row', 'col'), may hold values from -6 to 6
- region_ids: int32 [160, 480], P('row', 'col'), may hold values from 0 to 8, as said below
- qkv_weight: float32 [512, 1536], replicated, may hold values from -0.25 to 0.25
- query_bias: float32 [512], replicated, may hold values from -3 to 3
- value_bias: float32 [512], replicated, may hold values from -3 to 3
- bias_table: float32 [361, 16], replicated, may hold values from -6 to 6
- proj_weight: float32 [512, 512], replicated, may hold values from -1.5 to 1.5
- proj_bias: float32 [512], replicated, may hold values from -3 to 3
- gain_one: float32 [512], replicated, may hold values from 0.1 to 1.9
- shift_one: float32 [512], replicated, may hold values from -3 to 3
- gain_two: float32 [512], replicated, may hold values from 0.1 to 1.9
- shift_two: float32 [512], replicated, may hold values from -3 to 3
- up_weight: float32 [512, 2048], replicated, may hold values from -0.25 to 0.25
- up_bias: float32 [2048], replicated, may hold values from -3 to 3
- down_weight: float32 [2048, 512], replicated, may hold values from -0.125 to 0.125
- down_bias: float32 [512], replicated, may hold values from -3 to 3
- cotangent: bfloat16 [160, 480, 512], P('row', 'col'), may hold values from -6 to 6
Outputs:
- block_out: bfloat16 [160, 480, 512], P('row', 'col')
- patches_grad: bfloat16 [160, 480, 512], P('row', 'col')
- qkv_weight_grad: float32 [512, 1536], replicated
- query_bias_grad: float32 [512], replicated
- value_bias_grad: float32 [512], replicated
- bias_table_grad: float32 [361, 16], replicated
- proj_weight_grad: float32 [512, 512], replicated
- proj_bias_grad: float32 [512], replicated
- gain_one_grad: float32 [512], replicated
- shift_one_grad: float32 [512], replicated
- gain_two_grad: float32 [512], replicated
- shift_two_grad: float32 [512], replicated
- up_weight_grad: float32 [512, 2048], replicated
- up_bias_grad: float32 [2048], replicated
- down_weight_grad: float32 [2048, 512], replicated
- down_bias_grad: float32 [512], replicated
The draws below stay inside these ranges and needn't reach their ends.
Inputs may be any that keep to these rules, and one draw needn't show every extreme that they name: `region_ids`: the grid is tiled by pages whose sides are multiples of 10, aligned to the windows of the shifted grid, all pages of one column group of 120 columns alike. Within a page of h rows and w columns, at row r' and column c' of the page, id = 3 * band(r', h) + band(c', w) with band(x, n) = 0 for x < n - 10, 1 for n - 10 <= x < n - 5, 2 otherwise, the usual shifted-window mask; no window holds patches of two pages. A patch attends only to patches of its own window with the same id.
All inputs are finite; a program needn't handle non-finite values.
Results may differ from the reference program's by a relative error of at most 0.012.
The reference program's roundings to bfloat16 on the way count: a program that leaves them out, or rounds other values in their place, can miss the bound.
Values may be sent and summed in bfloat16 or wider, within the bound.
No kernel may reach another device: no remote copies, remote signals or barrier semaphores. Data moves between devices by JAX's collectives and lax.ppermute only.
A program may use at most 256 MiB of HBM per device.

```python
import jax
import jax.numpy as jnp
from jax import lax

D = 512
HEADS = 16
HD = 32
FF = 2048
WIN = 10
SHIFT = 5
WCOLS = 12
GRID_ROWS = 160
GRID_COLS = 480
TABLE = 361


def band_of(place, extent):
    return jnp.where(place < extent - 2 * SHIFT, 0, jnp.where(place < extent - SHIFT, 1, 2)).astype(jnp.int32)


def draw_region_ids(key, part):
    key = jax.random.fold_in(key, 5)
    kind_key, offset_key = jax.random.split(key, 2)
    group_width = WIN * WCOLS
    groups = GRID_COLS // group_width
    large_kind = jax.random.randint(kind_key, (groups,), 0, 2).astype(jnp.int32)
    row_offset = (jax.random.randint(offset_key, (groups,), 0, 16) * WIN).astype(jnp.int32)
    width_large = group_width
    width_small = max(WIN, WIN * (WCOLS // 2))
    height_large = min(16 * WIN, GRID_ROWS)
    height_small = 8 * WIN
    columns = jnp.arange(GRID_COLS, dtype=jnp.int32)
    rows = jnp.arange(GRID_ROWS, dtype=jnp.int32)
    group = columns // group_width
    inside = columns % group_width
    is_large = large_kind[group] == 1
    width = jnp.where(is_large, width_large, width_small).astype(jnp.int32)
    height = jnp.where(is_large, height_large, height_small).astype(jnp.int32)
    offset = row_offset[group] % height
    col_place = inside % width
    row_place = (rows[:, None] - offset[None, :]) % height[None, :]
    return (3 * band_of(row_place, height[None, :]) + band_of(col_place, width)[None, :]).astype(jnp.int32)


def level_of(stream_key, shape, shards, smallest, largest):
    gain, own = 1.0, jax.random.fold_in(stream_key, 6)
    for position, parts in shards:
        heights = jnp.exp(jax.random.uniform(jax.random.fold_in(own, position), (parts,), jnp.float32, smallest / len(shards), largest / len(shards)))
        gain = gain * jnp.repeat(heights, shape[position] // parts).reshape([-1 if axis == position else 1 for axis in range(len(shape))])
    return gain


def noise(stream_key, shape, scale, limit, cuts=(), held_as=jnp.bfloat16):
    array = jax.random.normal(stream_key, shape, jnp.float32) * scale
    if len(cuts) > 0:
        array = level_of(stream_key, shape, cuts, -0.22, 0.18) * array
    return jnp.clip(array, min=-limit, max=limit).astype(held_as)


def setup_inputs(seed: int = 0) -> dict:
    keys = jax.random.split(jax.random.key(seed), 18)
    return {
        "patches": noise(keys[0], (GRID_ROWS, GRID_COLS, D), 1.0, 6.0, ((0, 8), (1, 4))),
        "region_ids": draw_region_ids(jax.random.fold_in(keys[17], 71), 0),
        "qkv_weight": noise(keys[2], (D, 3 * D), D ** -0.5, 0.25, (), jnp.float32),
        "query_bias": noise(keys[3], (D,), 0.5, 3.0, (), jnp.float32),
        "value_bias": noise(keys[4], (D,), 0.5, 3.0, (), jnp.float32),
        "bias_table": noise(keys[5], (TABLE, HEADS), 1.0, 6.0, (), jnp.float32),
        "proj_weight": noise(keys[6], (D, D), (D // 32) ** -0.5, 1.5, (), jnp.float32),
        "proj_bias": noise(keys[7], (D,), 0.5, 3.0, (), jnp.float32),
        "gain_one": jnp.clip(1.0 + 0.18 * jax.random.normal(keys[8], (D,), jnp.float32), 0.1, 1.9),
        "shift_one": noise(keys[9], (D,), 0.5, 3.0, (), jnp.float32),
        "gain_two": jnp.clip(1.0 + 0.18 * jax.random.normal(keys[10], (D,), jnp.float32), 0.1, 1.9),
        "shift_two": noise(keys[11], (D,), 0.5, 3.0, (), jnp.float32),
        "up_weight": noise(keys[12], (D, FF), D ** -0.5, 0.25, (), jnp.float32),
        "up_bias": noise(keys[13], (FF,), 0.5, 3.0, (), jnp.float32),
        "down_weight": noise(keys[14], (FF, D), FF ** -0.5, 0.125, (), jnp.float32),
        "down_bias": noise(keys[15], (D,), 0.5, 3.0, (), jnp.float32),
        "cotangent": noise(keys[16], (GRID_ROWS, GRID_COLS, D), 1.0, 6.0, ((0, 8), (1, 4))),
    }


norm_eps = 1e-05
far_below = -1000000000.0

@jax.custom_vjp
def low(v):
    return lax.optimization_barrier(v.astype(jnp.bfloat16)).astype(jnp.float32)

@jax.custom_vjp
def low_back(v):
    return v

def low_keep(v):
    return (low(v), None)

def low_pass(kept, grad):
    return (grad,)

def back_keep(v):
    return (v, None)

def back_low(kept, grad):
    return (low(grad),)
low.defvjp(low_keep, low_pass)
low_back.defvjp(back_keep, back_low)

def highest_dot(left, right):
    return jnp.dot(left, right, precision=lax.Precision.HIGHEST)

def layer_norm(values, gain_vec, offset):
    center = values - lax.optimization_barrier(jnp.mean(values, axis=-1, keepdims=True))
    spread = lax.optimization_barrier(jnp.mean(center * center, axis=-1, keepdims=True))
    return center * lax.rsqrt(spread + norm_eps) * gain_vec + offset

def relative_index(window):
    places = jnp.arange(window * window, dtype=jnp.int32)
    prow = places // window
    pcol = places % window
    return (prow[:, None] - prow[None, :] + window - 1) * (2 * window - 1) + (pcol[:, None] - pcol[None, :] + window - 1)

def to_windows(grid):
    trailing = grid.shape[2:]
    pieces = grid.reshape((GRID_ROWS // WIN, WIN, GRID_COLS // WIN, WIN) + trailing)
    ordering = (0, 2, 1, 3) + tuple(range(4, pieces.ndim))
    return pieces.transpose(ordering).reshape((GRID_ROWS // WIN, GRID_COLS // WIN, WIN * WIN) + trailing)

def from_windows(windows):
    trailing = windows.shape[3:]
    pieces = windows.reshape((GRID_ROWS // WIN, GRID_COLS // WIN, WIN, WIN) + trailing)
    ordering = (0, 2, 1, 3) + tuple(range(4, pieces.ndim))
    return pieces.transpose(ordering).reshape((GRID_ROWS, GRID_COLS) + trailing)

def attend_row(row_block, id_row, position_bias):
    model_width = row_block.shape[-1] // 3
    head_count = position_bias.shape[0]
    head_size = model_width // head_count
    shape_heads = (row_block.shape[0], row_block.shape[1], head_count, head_size)
    queries = row_block[..., :model_width].reshape(shape_heads)
    keys_all = row_block[..., model_width:2 * model_width].reshape(shape_heads)
    values_all = row_block[..., 2 * model_width:].reshape(shape_heads)
    raw = jnp.einsum('wqhd,wkhd->whqk', queries, keys_all, precision=lax.Precision.HIGHEST)
    raw = low_back(raw)
    scores = raw * HD ** (-0.5) + position_bias[None]
    same_region = id_row[:, None, :, None] == id_row[:, None, None, :]
    scores = jnp.where(same_region, scores, far_below)
    row_max = lax.optimization_barrier(jnp.max(scores, axis=-1, keepdims=True))
    exp_scores = jnp.exp(scores - row_max)
    probs = exp_scores / lax.optimization_barrier(jnp.sum(exp_scores, axis=-1, keepdims=True))
    mixed_heads = jnp.einsum('whqk,wkhd->wqhd', low(probs), values_all, precision=lax.Precision.HIGHEST)
    return mixed_heads.reshape(row_block.shape[0], row_block.shape[1], model_width)

def forward(patches, qkv_weight, query_bias, value_bias, bias_table, proj_weight, proj_bias, gain_one, shift_one, gain_two, shift_two, up_weight, up_bias, down_weight, down_bias, region_ids):
    shifted = jnp.roll(patches, (-SHIFT, -SHIFT), axis=(0, 1))
    windows = to_windows(shifted)
    labels = to_windows(region_ids)
    normed_one = layer_norm(windows, gain_one, shift_one)
    joined = highest_dot(low(normed_one), low(qkv_weight)) + jnp.concatenate((query_bias, jnp.zeros_like(query_bias), value_bias))
    joined = low(low_back(joined))
    position_bias = jnp.transpose(bias_table[relative_index(WIN)], (2, 0, 1))
    checked = jax.checkpoint(attend_row)
    mixed_heads = lax.map(lambda item_pair: checked(item_pair[0], item_pair[1], position_bias), (joined, labels))
    mixed_heads = low(low_back(mixed_heads))
    branch = low_back(highest_dot(mixed_heads, low(proj_weight)) + proj_bias)
    middle = windows + branch
    normed_two = layer_norm(middle, gain_two, shift_two)
    hidden = low_back(highest_dot(low(normed_two), low(up_weight)) + up_bias)
    active = low(jax.nn.gelu(hidden, approximate=False))
    result = middle + highest_dot(active, low(down_weight)) + down_bias
    return jnp.roll(from_windows(result), (SHIFT, SHIFT), axis=(0, 1))

def reference(patches, region_ids, qkv_weight, query_bias, value_bias, bias_table, proj_weight, proj_bias, gain_one, shift_one, gain_two, shift_two, up_weight, up_bias, down_weight, down_bias, cotangent):
    params = (patches.astype(jnp.float32), qkv_weight, query_bias, value_bias, bias_table, proj_weight, proj_bias, gain_one, shift_one, gain_two, shift_two, up_weight, up_bias, down_weight, down_bias)
    output, pull = jax.vjp(lambda *inner: forward(*inner, region_ids), *params)
    grads = pull(cotangent.astype(jnp.float32))
    return (output.astype(jnp.bfloat16), grads[0].astype(jnp.bfloat16), grads[1], grads[2], grads[3], grads[4], grads[5], grads[6], grads[7], grads[8], grads[9], grads[10], grads[11], grads[12], grads[13], grads[14])
```

```python
import functools

import jax
import jax.numpy as jnp
from jax import lax
from jax.experimental import pallas as pl
from jax.experimental.pallas import tpu as pltpu
from jax.sharding import PartitionSpec as P

WIN = 10
SHIFT = 5
PLACES = WIN * WIN
PAD = 104
GROUP = 4
ROWS = GROUP * PAD
SLAB = 32
FF_PARTS = 4

norm_eps = 1e-05
far_below = -1000000000.0
LOG2E = 1.4426950408889634
bf16 = jnp.bfloat16
f32 = jnp.float32


def dot(left, right, left_dim=1, right_dim=0):
    return lax.dot_general(
        left, right, (((left_dim,), (right_dim,)), ((), ())), preferred_element_type=f32
    )


def whole(array):
    count = len(array.shape)
    return pl.BlockSpec(array.shape, lambda *ids: (0,) * count)


def params():
    return pltpu.CompilerParams(vmem_limit_bytes=60 * 2**20)


def norm_parts(values):
    center = values - jnp.mean(values, axis=-1, keepdims=True)
    rstd = lax.rsqrt(jnp.mean(center * center, axis=-1, keepdims=True) + norm_eps)
    return center * rstd, rstd


def norm_pull(grad, unit, rstd, gain):
    scaled = grad * gain
    return rstd * (
        scaled
        - jnp.mean(scaled, axis=-1, keepdims=True)
        - unit * jnp.mean(scaled * unit, axis=-1, keepdims=True)
    )


def head_masks():
    lane = lax.broadcasted_iota(jnp.int32, (1, 128), 1) // 32
    return [(lane == head).astype(f32).astype(bf16) for head in range(4)]


def spread_heads(tile):
    return jnp.concatenate([tile * mask for mask in head_masks()], axis=0)


def gather_heads(stacked):
    lane = lax.broadcasted_iota(jnp.int32, (PAD, 128), 1) // 32
    out = stacked[0:PAD]
    for head in range(1, 4):
        out = jnp.where(lane == head, stacked[PAD * head : PAD * (head + 1)], out)
    return out


def window_rows(upper, lower, col, last_start):
    width = upper.shape[-1]
    first = col * WIN + SHIFT
    start = pl.multiple_of(jnp.minimum(first // 16 * 16, last_start), 16)
    offset = first - start
    half = upper.shape[0] * SLAB
    slab = jnp.concatenate(
        (
            upper[:, pl.ds(start, SLAB), :].reshape(half, width),
            lower[:, pl.ds(start, SLAB), :].reshape(half, width),
        ),
        axis=0,
    )
    place = lax.broadcasted_iota(jnp.int32, (PAD, 2 * half), 0)
    lane = lax.broadcasted_iota(jnp.int32, (PAD, 2 * half), 1)
    prow = (place * 205) >> 11
    target = place + (SLAB - WIN) * prow + offset
    hot = ((lane == target) & (place < PLACES)).astype(f32).astype(bf16)
    return dot(hot, slab)


def forward_kernel(
    last_start, upper, lower, label_row, label_col, bias, qkv, qkv_bias, proj, proj_bias, gain_one, shift_one,
    gain_two, shift_two, inputs, normed_one, joined, probs, mixed, middle, normed_two, rows_s, joined_s, mixed_s,
):
    part = pl.program_id(1)

    def load(window, _):
        at = pl.ds(pl.multiple_of(window * PAD, 8), PAD)
        rows_s[at, :] = window_rows(upper, lower, part * GROUP + window, last_start)
        return 0

    lax.fori_loop(0, GROUP, load, 0)
    rows = rows_s[...]
    inputs[...] = rows.astype(bf16)
    unit, _ = norm_parts(rows)
    normed = (unit * gain_one[...] + shift_one[...]).astype(bf16)
    normed_one[...] = normed
    joined_s[...] = dot(normed, qkv[...]) + qkv_bias[...]

    def attend(window, _):
        at = pl.ds(pl.multiple_of(window * PAD, 8), PAD)
        joined[window] = joined_s[at, :].astype(bf16)
        masked = jnp.where(label_col[window] == label_row[window], 0.0, far_below)
        for tile in range(4):
            lanes = 128 * tile
            queries = joined_s[at, lanes : lanes + 128].astype(bf16)
            keys = joined_s[at, 512 + lanes : 640 + lanes].astype(bf16)
            values = joined_s[at, 1024 + lanes : 1152 + lanes].astype(bf16)
            raw = dot(spread_heads(keys), queries, 1, 1)
            parts = []
            for head in range(4):
                scores = raw[PAD * head : PAD * (head + 1)] * (LOG2E * 32**-0.5) + (
                    bias[4 * tile + head] + masked
                )
                powers = jnp.exp2(scores - jnp.max(scores, axis=0, keepdims=True))
                total = jnp.sum(powers, axis=0, keepdims=True)
                parts.append((powers * (1.0 / total)).astype(bf16))
            stacked = jnp.concatenate(parts, axis=0)
            probs[window, 4 * PAD * tile : 4 * PAD * (tile + 1), :] = stacked
            mixed_s[at, lanes : lanes + 128] = dot(stacked, spread_heads(values), 0, 0)
        return 0

    lax.fori_loop(0, GROUP, attend, 0)
    mixed_low = mixed_s[...].astype(bf16)
    mixed[...] = mixed_low
    total = rows_s[...] + dot(mixed_low, proj[...]) + proj_bias[...]
    middle[...] = total
    unit, _ = norm_parts(total)
    normed_two[...] = (unit * gain_two[...] + shift_two[...]).astype(bf16)


def rows_kernel(last_start, upper, lower, out, total, rows_s):
    part = pl.program_id(1)

    @pl.when((pl.program_id(0) == 0) & (part == 0))
    def _():
        total[...] = jnp.zeros_like(total)

    def load(window, _):
        at = pl.ds(pl.multiple_of(window * PAD, 8), PAD)
        rows_s[at, :] = window_rows(upper, lower, part * GROUP + window, last_start)
        return 0

    lax.fori_loop(0, GROUP, load, 0)
    rows = rows_s[...]
    out[...] = rows.astype(bf16)
    total[...] += jnp.sum(rows, axis=0, keepdims=True)


def ff_kernel(normed, upstream, up, up_bias, down, active, hidden_grad, up_grad, down_grad, up_bias_grad):
    @pl.when(pl.program_id(0) == 0)
    def _():
        up_grad[...] = jnp.zeros_like(up_grad)
        down_grad[...] = jnp.zeros_like(down_grad)
        up_bias_grad[...] = jnp.zeros_like(up_bias_grad)

    hidden = dot(normed[...], up[...]) + up_bias[...]
    below = 0.5 + 0.5 * lax.erf(hidden * (2.0**-0.5))
    active_low = (hidden * below).astype(bf16)
    active[...] = active_low
    slope = below + hidden * (jnp.exp2(hidden * hidden * (-0.5 * LOG2E)) * 0.3989422804014327)
    grad_low = (slope * dot(upstream[...], down[...], 1, 1)).astype(bf16)
    hidden_grad[...] = grad_low
    up_bias_grad[...] += jnp.sum(grad_low.astype(f32), axis=0, keepdims=True)
    up_grad[...] += dot(normed[...], grad_low, 0, 0)
    down_grad[...] += dot(active_low, upstream[...], 0, 0)


def backward_kernel(*refs):
    count = FF_PARTS
    actives, hidden_grads = refs[:count], refs[count : 2 * count]
    (
        upstream, middle, mixed, inputs, normed_one, joined, probs, up, down, down_bias, proj, qkv, gain_one, gain_two,
        result, input_grad, qkv_grad, qkv_sums, bias_grad, proj_grad, proj_sums, gain_one_grad, shift_one_grad,
        gain_two_grad, shift_two_grad, mixed_grad_s, joined_s,
    ) = refs[2 * count :]

    @pl.when(pl.program_id(0) == 0)
    def _():
        for ref in (qkv_grad, qkv_sums, bias_grad, proj_grad, proj_sums, gain_one_grad, shift_one_grad,
                    gain_two_grad, shift_two_grad):
            ref[...] = jnp.zeros_like(ref)

    def column_sum(values):
        return jnp.sum(values, axis=0, keepdims=True)

    active = jnp.concatenate([ref[...] for ref in actives], axis=1)
    hidden_grad = jnp.concatenate([ref[...] for ref in hidden_grads], axis=1)
    result[...] = middle[...] + dot(active, down[...]) + down_bias[...]
    normed_grad = dot(hidden_grad, up[...], 1, 1)
    unit, rstd = norm_parts(middle[...])
    gain_two_grad[...] += column_sum(normed_grad * unit)
    shift_two_grad[...] += column_sum(normed_grad)
    middle_grad = norm_pull(normed_grad, unit, rstd, gain_two[...]) + upstream[...].astype(f32)
    input_grad[...] = middle_grad
    branch_low = middle_grad.astype(bf16)
    proj_sums[...] += column_sum(branch_low.astype(f32))
    proj_grad[...] += dot(mixed[...], branch_low, 0, 0)
    mixed_grad_s[...] = dot(branch_low, proj[...], 1, 1)

    def attend(window, _):
        at = pl.ds(pl.multiple_of(window * PAD, 8), PAD)
        for tile in range(4):
            lanes = 128 * tile
            queries = joined[window, :, lanes : lanes + 128]
            keys = joined[window, :, 512 + lanes : 640 + lanes]
            values = joined[window, :, 1024 + lanes : 1152 + lanes]
            grad = mixed_grad_s[at, lanes : lanes + 128].astype(bf16)
            probs_grad = dot(spread_heads(values), grad, 1, 1)
            probs_low = probs[window, 4 * PAD * tile : 4 * PAD * (tile + 1), :]
            parts = []
            for head in range(4):
                here = slice(PAD * head, PAD * (head + 1))
                prob = probs_low[here].astype(f32)
                product = prob * probs_grad[here]
                score_grad = product - prob * jnp.sum(product, axis=0, keepdims=True)
                bias_grad[4 * tile + head] += score_grad
                parts.append((score_grad * 32**-0.5).astype(bf16))
            draw = jnp.concatenate(parts, axis=0)
            joined_s[at, lanes : lanes + 128] = dot(draw, spread_heads(keys), 0, 0)
            joined_s[at, 512 + lanes : 640 + lanes] = gather_heads(dot(draw, queries))
            joined_s[at, 1024 + lanes : 1152 + lanes] = gather_heads(dot(probs_low, grad))
        return 0

    lax.fori_loop(0, GROUP, attend, 0)
    joined_low = joined_s[...].astype(bf16)
    qkv_sums[...] += column_sum(joined_low.astype(f32))
    qkv_grad[...] += dot(normed_one[...], joined_low, 0, 0)
    normed_grad = dot(joined_low, qkv[...], 1, 1)
    unit, rstd = norm_parts(inputs[...].astype(f32))
    gain_one_grad[...] += column_sum(normed_grad * unit)
    shift_one_grad[...] += column_sum(normed_grad)
    input_grad[...] += norm_pull(normed_grad, unit, rstd, gain_one[...])


def grid_kernel(windows, out):
    count, _, width = windows.shape
    for row in range(WIN):
        start = WIN * row // 8 * 8
        offset = WIN * row - start
        slab = windows[:, start : start + 16, :].reshape(count * 16, width).astype(bf16)
        col = lax.broadcasted_iota(jnp.int32, (count * WIN, count * 16), 0)
        lane = lax.broadcasted_iota(jnp.int32, (count * WIN, count * 16), 1)
        window = (col * 205) >> 11
        hot = (lane == col + (16 - WIN) * window + offset).astype(f32).astype(bf16)
        out[row] = dot(hot, slab).astype(bf16)


def from_behind(value, axis, steps):
    count = lax.axis_size(axis)
    pairs = [(source, (source + steps) % count) for source in range(count)]
    return lax.ppermute(value, axis, pairs)


def padded(grid):
    below = from_behind(grid[:SHIFT], "row", -1)
    grid = jnp.concatenate((grid, below), axis=0)
    right = from_behind(grid[:, :SHIFT], "col", -1)
    spare = -(grid.shape[1] + SHIFT) % 16
    zeros = jnp.zeros((grid.shape[0], spare, grid.shape[2]), grid.dtype)
    return jnp.concatenate((grid, right, zeros), axis=1)


def roll_out(grid):
    lower = from_behind(grid[-SHIFT:], "row", 1)
    grid = jnp.concatenate((lower, grid[:-SHIFT]), axis=0)
    rightmost = from_behind(grid[:, -SHIFT:], "col", 1)
    return jnp.concatenate((rightmost, grid[:, :-SHIFT]), axis=1)


def relative_index():
    places = jnp.arange(PLACES, dtype=jnp.int32)
    prow, pcol = places // WIN, places % WIN
    return (prow[None, :] - prow[:, None] + WIN - 1) * (2 * WIN - 1) + (pcol[None, :] - pcol[:, None] + WIN - 1)


def body(
    patches, region_ids, qkv_weight, query_bias, value_bias, bias_table, proj_weight, proj_bias, gain_one, shift_one,
    gain_two, shift_two, up_weight, up_bias, down_weight, down_bias, cotangent,
):
    local_rows, local_cols, width = patches.shape
    heads = bias_table.shape[1]
    hidden_units = up_weight.shape[1]
    wrows, wcols = local_rows // WIN, local_cols // WIN
    windows = wrows * wcols
    tokens = windows * PAD
    steps = wcols // GROUP
    padded_patches = padded(patches)
    padded_upstream = padded(cotangent)
    last_start = padded_patches.shape[1] - SLAB
    labels = region_ids.reshape(wrows, WIN, wcols, WIN).transpose(0, 2, 1, 3).reshape(windows, PLACES)
    labels = jnp.pad(labels, ((0, 0), (0, PAD - PLACES)), constant_values=-1)
    onehot = (
        relative_index().reshape(-1)[:, None] == jnp.arange(bias_table.shape[0], dtype=jnp.int32)[None, :]
    ).astype(f32)
    position_bias = jnp.dot(onehot, bias_table, precision=lax.Precision.HIGHEST)
    position_bias = position_bias.reshape(PLACES, PLACES, heads).transpose(2, 0, 1) * LOG2E
    position_bias = jnp.pad(position_bias, ((0, 0), (0, 0), (0, PAD - PLACES)))
    position_bias = jnp.pad(position_bias, ((0, 0), (0, PAD - PLACES), (0, 0)), constant_values=far_below)
    qkv_low, proj_low = qkv_weight.astype(bf16), proj_weight.astype(bf16)
    up_low, down_low = up_weight.astype(bf16), down_weight.astype(bf16)
    qkv_bias = jnp.concatenate((query_bias, jnp.zeros_like(query_bias), value_bias))[None]
    row = lambda vector: vector[None]

    def struct(shape, dtype):
        return jax.ShapeDtypeStruct(shape, dtype)

    def token_spec(columns):
        return pl.BlockSpec((ROWS, columns), lambda i, j: (i * steps + j, 0))

    halo_specs = [
        pl.BlockSpec((SHIFT,) + padded_patches.shape[1:], lambda i, j: (2 * i + 1, 0, 0)),
        pl.BlockSpec((SHIFT,) + padded_patches.shape[1:], lambda i, j: (2 * i + 2, 0, 0)),
    ]
    window_spec = lambda *shape: pl.BlockSpec((GROUP,) + shape, lambda i, j: (i * steps + j,) + (0,) * len(shape))
    operands = (
        position_bias, qkv_low, qkv_bias, proj_low, row(proj_bias), row(gain_one), row(shift_one), row(gain_two),
        row(shift_two),
    )
    inputs, normed_one, joined, probs, mixed, middle, normed_two = pl.pallas_call(
        functools.partial(forward_kernel, last_start),
        grid=(wrows, steps),
        in_specs=halo_specs + [window_spec(1, PAD), window_spec(PAD, 1)] + [whole(a) for a in operands],
        out_specs=[
            token_spec(width), token_spec(width), window_spec(PAD, 3 * width), window_spec(heads * PAD, PAD),
            token_spec(width), token_spec(width), token_spec(width),
        ],
        out_shape=[
            struct((tokens, width), bf16), struct((tokens, width), bf16), struct((windows, PAD, 3 * width), bf16),
            struct((windows, heads * PAD, PAD), bf16), struct((tokens, width), bf16), struct((tokens, width), f32),
            struct((tokens, width), bf16),
        ],
        scratch_shapes=[
            pltpu.VMEM((ROWS, width), f32), pltpu.VMEM((ROWS, 3 * width), f32), pltpu.VMEM((ROWS, width), f32),
        ],
        compiler_params=params(),
    )(padded_patches, padded_patches, labels[:, None, :], labels[:, :, None], *operands)
    upstream, down_bias_grad = pl.pallas_call(
        functools.partial(rows_kernel, last_start),
        grid=(wrows, steps),
        in_specs=halo_specs,
        out_specs=[token_spec(width), pl.BlockSpec((1, width), lambda i, j: (0, 0))],
        out_shape=[struct((tokens, width), bf16), struct((1, width), f32)],
        scratch_shapes=[pltpu.VMEM((ROWS, width), f32)],
        compiler_params=params(),
    )(padded_upstream, padded_upstream)
    part = hidden_units // FF_PARTS
    ff = []
    rows_of = lambda columns: pl.BlockSpec((ROWS, columns), lambda i: (i, 0))
    fixed = lambda *shape: pl.BlockSpec(shape, lambda i: (0,) * len(shape))
    for index in range(FF_PARTS):
        ff.append(
            pl.pallas_call(
                ff_kernel,
                grid=(tokens // ROWS,),
                in_specs=[
                    rows_of(width), rows_of(width),
                    pl.BlockSpec((width, part), lambda i, index=index: (0, index)),
                    pl.BlockSpec((1, part), lambda i, index=index: (0, index)),
                    pl.BlockSpec((part, width), lambda i, index=index: (index, 0)),
                ],
                out_specs=[rows_of(part), rows_of(part), fixed(width, part), fixed(part, width), fixed(1, part)],
                out_shape=[
                    struct((tokens, part), bf16), struct((tokens, part), bf16), struct((width, part), f32),
                    struct((part, width), f32), struct((1, part), f32),
                ],
                compiler_params=params(),
            )(normed_two, upstream, up_low, row(up_bias), down_low)
        )
    actives, hidden_grads, up_grads, down_grads, up_bias_grads = zip(*ff)
    operands = (up_low, down_low, row(down_bias), proj_low, qkv_low, row(gain_one), row(gain_two))
    win_of = lambda *shape: pl.BlockSpec((GROUP,) + shape, lambda i: (i,) + (0,) * len(shape))
    sums = [
        struct((width, 3 * width), f32), struct((1, 3 * width), f32), struct((heads, PAD, PAD), f32),
        struct((width, width), f32),
    ] + [struct((1, width), f32)] * 5
    result, input_grad, *sums = pl.pallas_call(
        backward_kernel,
        grid=(tokens // ROWS,),
        in_specs=[rows_of(part)] * (2 * FF_PARTS)
        + [rows_of(width)] * 5
        + [win_of(PAD, 3 * width), win_of(heads * PAD, PAD)]
        + [whole(a) for a in operands],
        out_specs=[rows_of(width)] * 2 + [whole(a) for a in sums],
        out_shape=[struct((tokens, width), f32)] * 2 + sums,
        scratch_shapes=[pltpu.VMEM((ROWS, width), f32), pltpu.VMEM((ROWS, 3 * width), f32)],
        compiler_params=params(),
    )(*actives, *hidden_grads, upstream, middle, mixed, inputs, normed_one, joined, probs, *operands)
    (qkv_grad, qkv_sums, bias_grad, proj_grad, proj_sums, gain_one_grad, shift_one_grad, gain_two_grad,
     shift_two_grad) = sums

    def to_grid(values):
        return pl.pallas_call(
            grid_kernel,
            grid=(wrows,),
            in_specs=[pl.BlockSpec((wcols, PAD, width), lambda i: (i, 0, 0))],
            out_specs=pl.BlockSpec((WIN, local_cols, width), lambda i: (i, 0, 0)),
            out_shape=struct((local_rows, local_cols, width), bf16),
            compiler_params=params(),
        )(values.reshape(windows, PAD, width))

    block_out = roll_out(to_grid(result))
    patches_grad = roll_out(to_grid(input_grad))
    terms = bias_grad[:, :PLACES, :PLACES].reshape(heads, -1)
    table_grad = lax.dot_general(
        onehot, terms, (((0,), (1,)), ((), ())), precision=lax.Precision.HIGHEST, preferred_element_type=f32
    )
    summed = lax.psum(
        (
            qkv_grad, qkv_sums[0, :width], qkv_sums[0, 2 * width :], table_grad, proj_grad, proj_sums[0],
            gain_one_grad[0], shift_one_grad[0], gain_two_grad[0], shift_two_grad[0],
            jnp.concatenate(up_grads, axis=1), jnp.concatenate(up_bias_grads, axis=1)[0],
            jnp.concatenate(down_grads, axis=0), down_bias_grad[0],
        ),
        ("row", "col"),
    )
    return (block_out, patches_grad) + tuple(summed)


def solution(mesh):
    grid = P("row", "col", None)
    return jax.shard_map(
        body,
        mesh=mesh,
        in_specs=(grid, P("row", "col")) + (P(),) * 14 + (grid,),
        out_specs=(grid, grid) + (P(),) * 14,
        check_vma=False,
    )
```

```python
import functools

import jax
import jax.numpy as jnp
from jax import lax
from jax.experimental import pallas as pl
from jax.experimental.pallas import tpu as pltpu
from jax.sharding import PartitionSpec as P

WIN = 10
SHIFT = 5
PLACES = WIN * WIN
PAD = 104
GROUP = 4
ROWS = GROUP * PAD
SLAB = 32
EDGE = 16
TILE = 128
TILES = 4

norm_eps = 1e-05
far_below = -1000000000.0
LOG2E = 1.4426950408889634
bf16 = jnp.bfloat16
f32 = jnp.float32


def dot(left, right, left_dim=1, right_dim=0):
    return lax.dot_general(
        left, right, (((left_dim,), (right_dim,)), ((), ())), preferred_element_type=f32
    )


def whole(array):
    count = len(array.shape)
    return pl.BlockSpec(array.shape, lambda *ids: (0,) * count)


def params():
    return pltpu.CompilerParams(vmem_limit_bytes=60 * 2**20)


def norm_parts(values):
    center = values - jnp.mean(values, axis=-1, keepdims=True)
    rstd = lax.rsqrt(jnp.mean(center * center, axis=-1, keepdims=True) + norm_eps)
    return center * rstd, rstd


def norm_pull(grad, unit, rstd, gain):
    scaled = grad * gain
    return rstd * (
        scaled
        - jnp.mean(scaled, axis=-1, keepdims=True)
        - unit * jnp.mean(scaled * unit, axis=-1, keepdims=True)
    )


def head_masks():
    lane = lax.broadcasted_iota(jnp.int32, (1, 128), 1) // 32
    return [(lane == head).astype(f32).astype(bf16) for head in range(4)]


def spread_heads(tile):
    return jnp.concatenate([tile * mask for mask in head_masks()], axis=0)


def gather_heads(stacked):
    lane = lax.broadcasted_iota(jnp.int32, (PAD, 128), 1) // 32
    out = stacked[0:PAD]
    for head in range(1, 4):
        out = jnp.where(lane == head, stacked[PAD * head : PAD * (head + 1)], out)
    return out


def prepare_kernel(*refs):
    for rows, cols, rows_out, cols_out, corner_out in (refs[0:2] + refs[4:7], refs[2:4] + refs[7:10]):
        rows_out[...] = rows[...]
        cols_out[...] = cols[...]
        corner_out[...] = cols[0:SHIFT]


def window_rows(refs, local, col):
    upper, lower, upper_right, lower_right = refs
    count, wide, width = upper.shape
    first = col * WIN + SHIFT
    start = pl.multiple_of(jnp.minimum(first // 16 * 16, wide - SLAB), 16)
    half, side = count * SLAB, count * EDGE
    cols = pl.ds(start, SLAB)
    inside = lax.broadcasted_iota(jnp.int32, (1, SLAB, width), 1) + start < local
    slab = jnp.concatenate(
        (
            jnp.where(inside, upper[:, cols, :], 0).reshape(half, width),
            jnp.where(inside, lower[:, cols, :], 0).reshape(half, width),
            upper_right[...].reshape(side, width),
            lower_right[...].reshape(side, width),
        ),
        axis=0,
    )
    place = lax.broadcasted_iota(jnp.int32, (PAD, 1), 0)
    prow = (place * 205) >> 11
    pcol = place - WIN * prow + first
    target = jnp.where(pcol < local, prow * SLAB + pcol - start, 2 * half + prow * EDGE + pcol - local)
    target = jnp.where(place < PLACES, target, -1)
    lane = lax.broadcasted_iota(jnp.int32, (PAD, 2 * (half + side)), 1)
    hot = (lane == target).astype(f32).astype(bf16)
    return dot(hot, slab)


def halo_specs(block_row, last, local_cols, width):
    wide, below = -(-local_cols // 16) * 16, 0 if last else block_row + 1
    return [
        pl.BlockSpec((SHIFT, columns, width), lambda i, at=at: (at, 0, 0))
        for columns in (wide, EDGE)
        for at in (block_row, below)
    ]


def forward_kernel(local, first, *refs):
    sources, grad_sources, refs = refs[0:4], refs[4:8], refs[8:]
    (
        label_row, label_col, bias, qkv, qkv_bias, proj, proj_bias, gain_one, shift_one, *refs
    ) = refs
    if not first:
        refs = refs[7:]
    inputs, normed_one, joined, probs, mixed, middle, upstream, upstream_sum, *refs = refs
    part = pl.program_id(0)
    if first:
        qkv_low, proj_low, *refs = refs

        @pl.when(part == 0)
        def _():
            for tile in range(TILES):
                for kind in range(3):
                    lanes = 3 * TILE * tile + TILE * kind
                    source = qkv.shape[0] * kind + TILE * tile
                    qkv_low[:, lanes : lanes + TILE] = qkv[:, source : source + TILE].astype(bf16)
            proj_low[...] = proj[...].astype(bf16)

    else:
        qkv_low, proj_low = qkv, proj
    rows_s, joined_s, mixed_s = refs

    @pl.when(part == 0)
    def _():
        upstream_sum[...] = jnp.zeros_like(upstream_sum)

    for window in range(GROUP):
        rows_s[PAD * window : PAD * (window + 1), :] = window_rows(sources, local, part * GROUP + window)
    rows = rows_s[...]
    inputs[...] = rows.astype(bf16)
    unit, _ = norm_parts(rows)
    normed = (unit * gain_one[...] + shift_one[...]).astype(bf16)
    normed_one[...] = normed
    joined_s[...] = dot(normed, qkv_low[...]) + qkv_bias[...]
    for window in range(GROUP):
        mixed_s[PAD * window : PAD * (window + 1), :] = window_rows(grad_sources, local, part * GROUP + window)
    upstream[...] = mixed_s[...].astype(bf16)
    upstream_sum[...] += column_sum(mixed_s[...])

    def attend(window, _):
        at = pl.ds(pl.multiple_of(window * PAD, 8), PAD)
        joined[window] = joined_s[at, :].astype(bf16)
        masked = jnp.where(label_col[window] == label_row[window], 0.0, far_below)
        for tile in range(TILES):
            lanes = 3 * TILE * tile
            queries = joined_s[at, lanes : lanes + TILE].astype(bf16)
            keys = joined_s[at, lanes + TILE : lanes + 2 * TILE].astype(bf16)
            values = joined_s[at, lanes + 2 * TILE : lanes + 3 * TILE].astype(bf16)
            raw = dot(spread_heads(keys), queries, 1, 1)
            parts = []
            for head in range(4):
                scores = raw[PAD * head : PAD * (head + 1)] * (LOG2E * 32**-0.5) + (
                    bias[4 * tile + head] + masked
                )
                powers = jnp.exp2(scores - jnp.max(scores, axis=0, keepdims=True))
                total = jnp.sum(powers, axis=0, keepdims=True)
                parts.append((powers * (1.0 / total)).astype(bf16))
            stacked = jnp.concatenate(parts, axis=0)
            probs[window, tile] = stacked
            mixed_s[at, TILE * tile : TILE * (tile + 1)] = dot(stacked, spread_heads(values), 0, 0)
        return 0

    lax.fori_loop(0, GROUP, attend, 0)
    mixed_low = mixed_s[...].astype(bf16)
    mixed[...] = mixed_low
    middle[...] = rows_s[...] + dot(mixed_low, proj_low[...]) + proj_bias[...]


def column_sum(values):
    return jnp.sum(values, axis=0, keepdims=True)


def store_halves(core, last, total, start, keep, send):
    half = total.shape[0] // 2
    at = slice(start, start + half)

    @pl.when(last & (core == 0))
    def _():
        keep[at, :] = total[0:half, :]
        send[at, :] = total[half : 2 * half, :].astype(bf16)

    @pl.when(last & (core != 0))
    def _():
        keep[at, :] = total[half : 2 * half, :]
        send[at, :] = total[0:half, :].astype(bf16)


def middle_kernel(
    core, upstream, middle, mixed, up_weight, up_bias, down_weight, down_bias, proj, gain, shift,
    out, below, edge, corner, middle_grad_out, mixed_grad, keep, send, up_bias_grad, proj_sums, gain_grad, shift_grad,
    windows_s, mixed_grad_s, up, down, ff_grad, proj_grad,
):
    part = pl.program_id(1)
    step = pl.program_id(0) * pl.num_programs(1) + part

    @pl.when(step == 0)
    def _():
        up[...] = up_weight[...].astype(bf16)
        down[...] = down_weight[...].astype(bf16)
        for ref in (ff_grad, proj_grad, up_bias_grad, proj_sums, gain_grad, shift_grad):
            ref[...] = jnp.zeros_like(ref)

    unit, rstd = norm_parts(middle[...])
    normed = (unit * gain[...] + shift[...]).astype(bf16)
    given = upstream[...]
    result = middle[...] + down_bias[...]
    normed_grad = 0.0
    width, units = up.shape
    for start in range(0, units, width):
        at = slice(start, start + width)
        down_at = slice(units + start, units + start + width)
        hidden = dot(normed, up[:, at]) + up_bias[:, at]
        under = 0.5 + 0.5 * lax.erf(hidden * (2.0**-0.5))
        active_low = (hidden * under).astype(bf16)
        slope = under + hidden * (jnp.exp2(hidden * hidden * (-0.5 * LOG2E)) * 0.3989422804014327)
        grad_low = (slope * dot(given, down[at, :], 1, 1)).astype(bf16)
        up_bias_grad[:, at] += column_sum(grad_low.astype(f32))
        ff_grad[at, :] += dot(normed, grad_low, 0, 0)
        ff_grad[down_at, :] += dot(active_low, given, 0, 0)
        result += dot(active_low, down[at, :])
        normed_grad += dot(grad_low, up[:, at], 1, 1)
    store_windows(windows_s, result, part)
    gain_grad[...] += column_sum(normed_grad * unit)
    shift_grad[...] += column_sum(normed_grad)
    middle_grad = norm_pull(normed_grad, unit, rstd, gain[...]) + given.astype(f32)
    middle_grad_out[...] = middle_grad
    branch_low = middle_grad.astype(bf16)
    proj_sums[...] += column_sum(branch_low.astype(f32))
    proj_grad[...] += dot(mixed[...], branch_low, 0, 0)
    mixed_grad_s[...] = dot(branch_low, proj[...], 1, 1)
    for window in range(GROUP):
        mixed_grad[window] = mixed_grad_s[PAD * window : PAD * (window + 1)].astype(bf16)
    windows_to_grid(windows_s, out, below, edge, corner)
    last = step == pl.num_programs(0) * pl.num_programs(1) - 1
    store_halves(core[0], last, ff_grad, 0, keep, send)
    store_halves(core[0], last, proj_grad, units, keep, send)


def attention_pull_kernel(
    core, normed_one, joined, probs, mixed_grad, joined_grad, keep, send, sums, bias_grad, joined_s, qkv_grad, bias_s
):
    @pl.when(pl.program_id(0) == 0)
    def _():
        for ref in (qkv_grad, sums, bias_s):
            ref[...] = jnp.zeros_like(ref)

    for window in range(GROUP):
        at = slice(PAD * window, PAD * (window + 1))
        queries = joined[window, :, 0:TILE]
        keys = joined[window, :, TILE : 2 * TILE]
        values = joined[window, :, 2 * TILE : 3 * TILE]
        grad = mixed_grad[window]
        probs_grad = dot(spread_heads(values), grad, 1, 1)
        probs_low = probs[window, 0]
        parts = []
        for head in range(4):
            here = slice(PAD * head, PAD * (head + 1))
            prob = probs_low[here].astype(f32)
            product = prob * probs_grad[here]
            score_grad = product - prob * column_sum(product)
            bias_s[window, head] += score_grad
            parts.append((score_grad * 32**-0.5).astype(bf16))
        draw = jnp.concatenate(parts, axis=0)
        joined_s[at, 0:TILE] = dot(draw, spread_heads(keys), 0, 0)
        joined_s[at, TILE : 2 * TILE] = gather_heads(dot(draw, queries))
        joined_s[at, 2 * TILE : 3 * TILE] = gather_heads(dot(probs_low, grad))
    joined_low = joined_s[...].astype(bf16)
    joined_grad[...] = joined_low
    sums[...] += column_sum(joined_low.astype(f32))
    qkv_grad[...] += dot(normed_one[...], joined_low, 0, 0)

    @pl.when(pl.program_id(0) == pl.num_programs(0) - 1)
    def _():
        for head in range(4):
            bias_grad[head] = (bias_s[0, head] + bias_s[1, head]) + (bias_s[2, head] + bias_s[3, head])

    store_halves(core[0], pl.program_id(0) == pl.num_programs(0) - 1, qkv_grad, 0, keep, send)


def windows_to_grid(windows, out, below, edge, corner):
    count, _, width = windows.shape
    cols = count * WIN
    window_row, last_row = pl.program_id(0), pl.num_programs(0) - 1

    @pl.when(pl.program_id(1) == pl.num_programs(1) - 1)
    def _():
        spot = lax.broadcasted_iota(jnp.int32, (cols + EDGE, 1), 0)
        col = spot - SHIFT
        window = (col * 205) >> 11
        valid = (col >= 0) & (col < cols)
        lane = lax.broadcasted_iota(jnp.int32, (cols + EDGE, count * 16), 1)
        for row in range(WIN):
            start = WIN * row // 8 * 8
            offset = WIN * row - start
            slab = windows[:, start : start + 16, :].reshape(count * 16, width).astype(bf16)
            target = jnp.where(valid, col + (16 - WIN) * window + offset, -1)
            moved_rows = dot((lane == target).astype(f32).astype(bf16), slab)
            main, side = moved_rows[0:cols].astype(bf16), moved_rows[cols : cols + EDGE].astype(bf16)
            at = WIN * window_row + row + SHIFT
            if row < WIN - SHIFT:
                out[at] = main
                edge[at] = side
            else:

                @pl.when(window_row < last_row)
                def _():
                    out[at] = main
                    edge[at] = side

                @pl.when(window_row == last_row)
                def _():
                    below[row - (WIN - SHIFT)] = main
                    corner[row - (WIN - SHIFT)] = side


def store_windows(windows_s, values, part):
    for window in range(GROUP):
        windows_s[part * GROUP + window] = values[PAD * window : PAD * (window + 1)]


def inputs_grad_kernel(*refs):
    grads = refs[:TILES]
    (
        inputs, middle_grad, qkv, gain, out, below, edge, corner, gain_grad, shift_grad, windows_s
    ) = refs[TILES:]
    part = pl.program_id(1)

    @pl.when((pl.program_id(0) == 0) & (part == 0))
    def _():
        gain_grad[...] = jnp.zeros_like(gain_grad)
        shift_grad[...] = jnp.zeros_like(shift_grad)

    normed_grad = dot(jnp.concatenate([ref[...] for ref in grads], axis=1), qkv[...], 1, 1)
    unit, rstd = norm_parts(inputs[...].astype(f32))
    gain_grad[...] += column_sum(normed_grad * unit)
    shift_grad[...] += column_sum(normed_grad)
    store_windows(windows_s, norm_pull(normed_grad, unit, rstd, gain[...]) + middle_grad[...], part)
    windows_to_grid(windows_s, out, below, edge, corner)


def flipped(value, row_bits, col_bits):
    rows, cols = lax.axis_size("row"), lax.axis_size("col")
    pairs = [(r * cols + c, (r ^ row_bits) * cols + (c ^ col_bits)) for r in range(rows) for c in range(cols)]
    return lax.ppermute(value, ("row", "col"), pairs)


def block(ref, index, rows):
    return ref[pl.ds(pl.multiple_of(index * rows, 8), rows), :]


def split_kernel(count, place, *refs):
    terms, total, outs = refs[: 2 * count], refs[-1], refs[2 * count : -1]
    start = 0
    for kept, got in zip(terms[:count], terms[count:]):
        rows = kept.shape[0]
        total[start : start + rows, :] = kept[...] + got[...].astype(f32)
        start += rows
    rows = outs[0].shape[0]
    outs[0][...] = block(total, place[0], rows)
    for other in range(1, 4):
        outs[other][...] = block(total, place[0] ^ other, rows).astype(bf16)


def split_again_kernel(place, kept, first, second, third, *refs):
    outs, total = refs[:-1], refs[-1]
    total[...] = kept[...] + first[...].astype(f32) + second[...].astype(f32) + third[...].astype(f32)
    rows = outs[0].shape[0]
    outs[0][...] = block(total, place[0], rows)
    for other in range(1, 4):
        outs[other][...] = block(total, place[0] ^ other, rows).astype(bf16)


def add_kernel(kept, first, second, third, out):
    out[...] = (kept[...] + first[...].astype(f32) + second[...].astype(f32) + third[...].astype(f32)).astype(out.dtype)


def join_kernel(place, *refs):
    pieces, out, joined_s = refs[:4], refs[4], refs[5]
    rows = pieces[0].shape[0]
    for other in range(4):
        at = pl.ds(pl.multiple_of((place[0] ^ other) * rows, 8), rows)
        joined_s[at, :] = pieces[other][...].astype(f32)
    out[...] = joined_s[...].astype(bf16)


def scalar_call(kernel, scalar, *operands, outs, scratch=()):
    return pl.pallas_call(
        kernel,
        grid_spec=pltpu.PrefetchScalarGridSpec(
            num_scalar_prefetch=1,
            grid=(1,),
            in_specs=[pl.BlockSpec(a.shape, lambda i, s, n=a.ndim: (0,) * n) for a in operands],
            out_specs=[pl.BlockSpec(a.shape, lambda i, s, n=len(a.shape): (0,) * n) for a in outs],
            scratch_shapes=list(scratch),
        ),
        out_shape=list(outs),
        compiler_params=params(),
    )(scalar, *operands)


def struct(shape, dtype):
    return jax.ShapeDtypeStruct(shape, dtype)


def places():
    row, col = lax.axis_index("row"), lax.axis_index("col")
    one = lambda value: jnp.reshape(value, (1,)).astype(jnp.int32)
    return one(col & 1), one(((col >> 1) & 1) | ((row & 1) << 1)), one((row >> 1) & 3)


class Order:
    def __init__(self):
        self.last = None

    def __call__(self, call, *operands):
        if self.last is not None:
            operands, _ = lax.optimization_barrier((operands, self.last))
        results = call(*operands)
        self.last = jax.tree.leaves(results)[0]
        return results


def sum_over_devices(order, kept, sent):
    _, plane, depth = places()
    plane_flips = ((0, 2), (1, 0), (1, 2))
    depth_flips = ((2, 0), (4, 0), (6, 0))
    got = [flipped(half, 0, 1) for half in sent]
    rows, width = sum(half.shape[0] for half in kept), kept[0].shape[1]
    quarter, small = rows // 4, rows // 16
    yield
    outs = [struct((quarter, width), f32)] + [struct((quarter, width), bf16)] * 3
    call = functools.partial(
        scalar_call, functools.partial(split_kernel, len(kept)), plane, outs=outs, scratch=[pltpu.VMEM((rows, width), f32)]
    )
    own, *sends = order(call, *kept, *got)
    got = [flipped(piece, *flip) for piece, flip in zip(sends, plane_flips)]
    yield
    outs = [struct((small, width), f32)] + [struct((small, width), bf16)] * 3
    call = functools.partial(
        scalar_call, split_again_kernel, depth, outs=outs, scratch=[pltpu.VMEM((quarter, width), f32)]
    )
    own, *sends = order(call, own, *got)
    got = [flipped(piece, *flip) for piece, flip in zip(sends, depth_flips)]
    yield
    further = []
    bit = 8
    while bit < lax.axis_size("row"):
        further.append(bit)
        bit *= 2
    done = order(pl.pallas_call(add_kernel, out_shape=struct((small, width), f32 if further else bf16)), own, *got)
    for bit in further:
        done = done + flipped(done.astype(bf16), bit, 0).astype(f32)
    done = done.astype(bf16)
    pieces = [done] + [flipped(done, *flip) for flip in depth_flips]
    yield
    call = functools.partial(
        scalar_call, join_kernel, depth, outs=[struct((quarter, width), bf16)], scratch=[pltpu.VMEM((quarter, width), f32)]
    )
    (mine,) = order(call, *pieces)
    mine = [mine] + [flipped(mine, *flip) for flip in plane_flips]
    yield
    pieces = mine + [flipped(piece, 0, 1) for piece in mine]
    yield pieces


def finish_kernel(count, write, plane, core, *refs):
    pieces, outs, total = refs[:8], refs[8 + count : -1], refs[-1]
    rows = pieces[0].shape[0]
    for other in range(4):
        at = pl.ds(pl.multiple_of((plane[0] ^ other) * rows, 8), rows)
        total[core[0], at, :] = pieces[other][...].astype(f32)
        total[1 - core[0], at, :] = pieces[4 + other][...].astype(f32)
    write(total, *outs)


def finish(order, pieces, write, specs, outs, given=()):
    core, plane, _ = places()
    rows, width = pieces[0].shape

    def call(*operands):
        return pl.pallas_call(
            functools.partial(finish_kernel, len(given), write),
            grid_spec=pltpu.PrefetchScalarGridSpec(
                num_scalar_prefetch=2,
                grid=(1,),
                in_specs=[pl.BlockSpec(a.shape, lambda i, s, t: (0, 0)) for a in pieces]
                + [pl.BlockSpec(memory_space=pl.ANY)] * len(given),
                out_specs=specs,
                scratch_shapes=[pltpu.VMEM((2, 4 * rows, width), f32)],
            ),
            out_shape=outs,
            input_output_aliases={10 + index: index for index in range(len(given))},
            compiler_params=params(),
        )(plane, core, *operands)

    return order(call, *pieces, *given)


def exchange_add(order, value):
    def add(*terms):
        def kernel(*refs):
            total = refs[0][...]
            for ref in refs[1:-1]:
                total = total + ref[...]
            refs[-1][...] = total

        return pl.pallas_call(kernel, out_shape=struct(terms[0].shape, f32))(*terms)

    value = order(add, value, flipped(value, 0, 1))
    yield
    value = order(add, value, *[flipped(value, *flip) for flip in ((0, 2), (1, 0), (1, 2))])
    yield
    value = order(add, value, *[flipped(value, *flip) for flip in ((2, 0), (4, 0), (6, 0))])
    bit = 8
    while bit < lax.axis_size("row"):
        value = value + flipped(value, bit, 0)
        bit *= 2
    yield value


def moved(value, row_step, col_step):
    rows, cols = lax.axis_size("row"), lax.axis_size("col")
    pairs = [
        (r * cols + c, ((r - row_step) % rows) * cols + (c - col_step) % cols) for r in range(rows) for c in range(cols)
    ]
    return lax.ppermute(value, ("row", "col"), pairs)


def relative_index():
    spots = jnp.arange(PLACES, dtype=jnp.int32)
    prow, pcol = spots // WIN, spots % WIN
    return (prow[None, :] - prow[:, None] + WIN - 1) * (2 * WIN - 1) + (pcol[None, :] - pcol[:, None] + WIN - 1)


def by_tile(array):
    return array.reshape(3, TILES, TILE).swapaxes(0, 1).reshape(1, 3 * TILES * TILE)


def thirds(values):
    terms = []
    for _ in range(3):
        term = lax.reduce_precision(values, 8, 7)
        terms.append(term.astype(bf16))
        values = values - term
    return jnp.concatenate(terms)


def exact_dot(values, onehot, dim):
    product = lax.dot_general(thirds(values), onehot, (((1,), (dim,)), ((), ())), preferred_element_type=f32)
    first, second, third = jnp.split(product, 3)
    return first + (second + third)


def body(
    patches, region_ids, qkv_weight, query_bias, value_bias, bias_table, proj_weight, proj_bias, gain_one, shift_one,
    gain_two, shift_two, up_weight, up_bias, down_weight, down_bias, cotangent,
):
    local_rows, local_cols, width = patches.shape
    heads = bias_table.shape[1]
    hidden_units = up_weight.shape[1]
    wrows, wcols = local_rows // WIN, local_cols // WIN
    windows = wrows * wcols
    tokens = windows * PAD
    steps = wcols // GROUP
    wide = -(-local_cols // 16) * 16
    row = lambda vector: vector[None]
    core, _, _ = places()
    order = Order()

    def prepare(first, second):
        rows_block = pl.BlockSpec((SHIFT, local_cols, width), lambda i: (0, 0, 0))
        cols_block = pl.BlockSpec((local_rows, EDGE, width), lambda i: (0, 0, 0))
        corner_block = pl.BlockSpec((SHIFT, EDGE, width), lambda i: (0, 0, 0))
        return pl.pallas_call(
            prepare_kernel,
            grid=(1,),
            in_specs=[rows_block, cols_block] * 2,
            out_specs=[rows_block, cols_block, corner_block] * 2,
            out_shape=[
                struct((SHIFT, local_cols, width), bf16), struct((local_rows, EDGE, width), bf16),
                struct((SHIFT, EDGE, width), bf16),
            ] * 2,
            compiler_params=params(),
        )(first, first, second, second)

    edges = order(prepare, patches, cotangent)
    right, right_grad = moved(edges[1], 0, 1), moved(edges[4], 0, 1)
    below, across = moved(edges[0], 1, 0), moved(edges[2], 1, 1)
    below_grad, across_grad = moved(edges[3], 1, 0), moved(edges[5], 1, 1)
    labels = region_ids.reshape(wrows, WIN, wcols, WIN).transpose(0, 2, 1, 3).reshape(windows, PLACES)
    labels = jnp.pad(labels, ((0, 0), (0, PAD - PLACES)), constant_values=-1)
    onehot = (
        relative_index().reshape(-1)[:, None] == jnp.arange(bias_table.shape[0], dtype=jnp.int32)[None, :]
    ).astype(bf16)
    position_bias = exact_dot(bias_table.T, onehot, 1).reshape(heads, PLACES, PLACES) * LOG2E
    position_bias = jnp.pad(position_bias, ((0, 0), (0, 0), (0, PAD - PLACES)))
    position_bias = jnp.pad(position_bias, ((0, 0), (0, PAD - PLACES), (0, 0)), constant_values=far_below)
    qkv_bias = by_tile(jnp.concatenate((query_bias, jnp.zeros_like(query_bias), value_bias)))

    token_arrays = [
        struct((tokens, width), bf16), struct((tokens, width), bf16), struct((windows, PAD, 3 * width), bf16),
        struct((windows, TILES, 4 * PAD, PAD), bf16), struct((tokens, width), bf16), struct((tokens, width), f32),
        struct((tokens, width), bf16),
    ]
    made, upstream_sums = [], []
    qkv_low, proj_low = qkv_weight, proj_weight
    labels = (labels[:, None, :], labels[:, :, None])
    for index in range(wrows):
        first, last = index == 0, index == wrows - 1
        block_of = lambda array: pl.BlockSpec(
            (array.shape[0] // (wrows * steps),) + array.shape[1:],
            lambda i, n=len(array.shape), index=index: (index * steps + i,) + (0,) * (n - 1),
        )
        specs = halo_specs(2 * index + 1, last, local_cols, width)
        operands = (
            position_bias, qkv_low, qkv_bias, proj_low, row(proj_bias), row(gain_one), row(shift_one),
        )
        lows = [struct(qkv_weight.shape, bf16), struct(proj_weight.shape, bf16)] if first else []
        call = pl.pallas_call(
            functools.partial(forward_kernel, local_cols, first),
            grid=(steps,),
            in_specs=specs * 2 + [block_of(a) for a in labels] + [whole(a) for a in operands]
            + [pl.BlockSpec(memory_space=pl.ANY)] * len(made),
            out_specs=[block_of(a) for a in token_arrays]
            + [pl.BlockSpec((1, width), lambda i: (0, 0))] + [whole(a) for a in lows],
            out_shape=token_arrays + [struct((1, width), f32)] + lows,
            input_output_aliases={17 + i: i for i in range(len(made))},
            scratch_shapes=[
                pltpu.VMEM((ROWS, width), f32), pltpu.VMEM((ROWS, 3 * width), f32), pltpu.VMEM((ROWS, width), f32),
            ],
            compiler_params=params(),
        )
        around = (patches, below if last else patches, right, across if last else right)
        around_grad = (cotangent, below_grad if last else cotangent, right_grad, across_grad if last else right_grad)
        outs = order(call, *around, *around_grad, *labels, *operands, *made)
        made, total = outs[: len(token_arrays)], outs[len(token_arrays)]
        if first:
            qkv_low, proj_low = outs[-2:]
        upstream_sums.append(total)
    inputs, normed_one, joined, probs, mixed, middle, upstream = made
    down_bias_grad = sum(upstream_sums)
    rows_of = lambda columns: pl.BlockSpec((ROWS, columns), lambda i, *_: (i, 0))
    win_of = lambda *shape: pl.BlockSpec((GROUP,) + shape, lambda i, *_: (i,) + (0,) * len(shape))
    fixed = lambda array: pl.BlockSpec(array.shape, lambda i, *_: (0,) * len(array.shape))

    def core_call(kernel, in_specs, out_specs, out_shape, scratch):
        return pl.pallas_call(
            kernel,
            grid_spec=pltpu.PrefetchScalarGridSpec(
                num_scalar_prefetch=1,
                grid=(tokens // ROWS,),
                in_specs=in_specs,
                out_specs=out_specs,
                scratch_shapes=scratch,
            ),
            out_shape=out_shape,
            compiler_params=params(),
        )

    def attention_pull(tile):
        outs = [
            struct((width // 2, 3 * TILE), f32), struct((width // 2, 3 * TILE), bf16), struct((1, 3 * TILE), f32),
            struct((heads // TILES, PAD, PAD), f32),
        ]
        call = core_call(
            attention_pull_kernel,
            [
                rows_of(width),
                pl.BlockSpec((GROUP, PAD, 3 * TILE), lambda i, s: (i, 0, tile)),
                pl.BlockSpec((GROUP, 1, 4 * PAD, PAD), lambda i, s: (i, tile, 0, 0)),
                pl.BlockSpec((GROUP, PAD, TILE), lambda i, s: (i, 0, tile)),
            ],
            [rows_of(3 * TILE)] + [fixed(a) for a in outs],
            [struct((tokens, 3 * TILE), bf16)] + outs,
            [
                pltpu.VMEM((ROWS, 3 * TILE), f32), pltpu.VMEM((width, 3 * TILE), f32),
                pltpu.VMEM((GROUP, heads // TILES, PAD, PAD), f32),
            ],
        )
        return order(call, core, normed_one, joined, probs, mixed_grad)

    def write_ff_proj(total, up_out, down_out, proj_out):
        for index in range(hidden_units // width):
            at = slice(width * index, width * (index + 1))
            up_out[:, at] = total[0, at, :]
        down_out[...] = total[1, 0:hidden_units, :]
        for side in range(2):
            proj_out[width // 2 * side : width // 2 * (side + 1), :] = total[side, hidden_units : hidden_units + width // 2, :]

    def write_qkv(total, out):
        rows = width // 2
        for side in range(2):
            for tile in range(TILES):
                for kind in range(3):
                    at = width * kind + TILE * tile
                    out[rows * side : rows * (side + 1), at : at + TILE] = (
                        total[side, rows * tile : rows * (tile + 1), TILE * kind : TILE * (kind + 1)]
                    )

    token_spec = lambda columns: pl.BlockSpec((ROWS, columns), lambda i, j, *_: (i * steps + j, 0))
    single = lambda array: pl.BlockSpec(
        array.shape, lambda *ids, n=len(array.shape): (0,) * n, pipeline_mode=pl.Buffered(1)
    )
    constant = lambda array: pl.BlockSpec(array.shape, lambda *ids, n=len(array.shape): (0,) * n)
    grid_outs = [
        struct((local_rows, local_cols, width), bf16), struct((SHIFT, local_cols, width), bf16),
        struct((local_rows, EDGE, width), bf16), struct((SHIFT, EDGE, width), bf16),
    ]
    vector = struct((1, width), f32)

    def edges_out(grid, below, edge, corner):
        return grid, moved(below, -1, 0), moved(edge, 0, -1), moved(corner, -1, -1)

    def place(grid, above, left, corner):
        spot = lax.broadcasted_iota(jnp.int32, (1, EDGE, 1), 1)
        rows = jnp.concatenate((jnp.where(spot < SHIFT, corner, above[:, :EDGE]), above[:, EDGE:]), axis=1)
        cols = jnp.where(spot < SHIFT, left[SHIFT:], grid[SHIFT:, :EDGE])
        return lax.dynamic_update_slice(lax.dynamic_update_slice(grid, rows, (0, 0, 0)), cols, (SHIFT, 0, 0))

    shared = hidden_units + width // 2
    outs = [
        struct((shared, width), f32), struct((shared, width), bf16), struct((1, hidden_units), f32), vector, vector,
        vector,
    ]
    call = pl.pallas_call(
        middle_kernel,
        grid_spec=pltpu.PrefetchScalarGridSpec(
            num_scalar_prefetch=1,
            grid=(wrows, steps),
            in_specs=[token_spec(width)] * 3
            + [single(up_weight), single(row(up_bias)), single(down_weight)]
            + [single(a) for a in (row(down_bias), proj_low, row(gain_two), row(shift_two))],
            out_specs=[single(a) for a in grid_outs]
            + [token_spec(width), pl.BlockSpec((GROUP, PAD, width), lambda i, j, s: (i * steps + j, 0, 0))]
            + [single(a) for a in outs],
            scratch_shapes=[
                pltpu.VMEM((wcols, PAD, width), f32), pltpu.VMEM((ROWS, width), f32), pltpu.VMEM(up_weight.shape, bf16),
                pltpu.VMEM(down_weight.shape, bf16), pltpu.VMEM((2 * hidden_units, width), f32),
                pltpu.VMEM((width, width), f32),
            ],
        ),
        out_shape=grid_outs + [struct((tokens, width), f32), struct((windows, PAD, width), bf16)] + outs,
        compiler_params=params(),
    )
    (
        *result_parts, middle_grad, mixed_grad, kept, sent, up_bias_grad, proj_sums, gain_two_grad, shift_two_grad,
    ) = order(
        call, core, upstream, middle, mixed, up_weight, row(up_bias), down_weight, row(down_bias), proj_low,
        row(gain_two), row(shift_two),
    )
    first_sum = sum_over_devices(order, (kept,), (sent,))
    next(first_sum)
    next(first_sum)
    result_parts = edges_out(*result_parts)
    tiles = [attention_pull(0), attention_pull(1)]
    next(first_sum)
    tiles.append(attention_pull(2))
    next(first_sum)
    tiles.append(attention_pull(3))
    next(first_sum)
    joined_grads, qkv_kept, qkv_sent, qkv_sums, bias_grads = zip(*tiles)
    second_sum = sum_over_devices(order, qkv_kept, qkv_sent)
    next(second_sum)
    next(second_sum)
    call = pl.pallas_call(
        inputs_grad_kernel,
        grid=(wrows, steps),
        in_specs=[token_spec(3 * TILE)] * TILES + [token_spec(width)] * 2 + [single(qkv_low), single(row(gain_one))],
        out_specs=[single(a) for a in grid_outs] + [single(vector)] * 2,
        out_shape=grid_outs + [vector] * 2,
        scratch_shapes=[pltpu.VMEM((wcols, PAD, width), f32)],
        compiler_params=params(),
    )
    *grad_parts, gain_one_grad, shift_one_grad = order(
        call, *joined_grads, inputs, middle_grad, qkv_low, row(gain_one)
    )
    grad_parts = edges_out(*grad_parts)
    next(second_sum)
    first_pieces = next(first_sum)
    terms = jnp.concatenate(bias_grads)[:, :PLACES, :PLACES].reshape(heads, -1)
    table_grad = exact_dot(terms, onehot, 0).T
    vectors = [
        jnp.concatenate(qkv_sums, axis=1)[0], proj_sums[0], gain_one_grad[0], shift_one_grad[0], gain_two_grad[0],
        shift_two_grad[0], up_bias_grad[0], down_bias_grad[0], table_grad.reshape(-1),
    ]
    packed = jnp.concatenate(vectors)
    packed = jnp.pad(packed, (0, -packed.size % 4096)).reshape(-1, width)
    small_sum = exchange_add(order, packed)
    next(second_sum)
    next(small_sum)
    constant_out = lambda *shape: pl.BlockSpec(shape, lambda i, s, t: (0,) * len(shape))
    up_total, down_total, proj_total = finish(
        order, first_pieces, write_ff_proj,
        [constant_out(width, hidden_units), constant_out(hidden_units, width), constant_out(width, width)],
        [struct((width, hidden_units), f32), struct((hidden_units, width), f32), struct((width, width), f32)],
    )
    next(small_sum)
    next(second_sum)
    small = next(small_sum).reshape(-1)
    result_out = place(*result_parts)
    grad_out = place(*grad_parts)
    qkv_pieces = next(second_sum)
    (qkv_total,) = finish(
        order, qkv_pieces, write_qkv, [constant_out(width, 3 * width)], [struct((width, 3 * width), f32)]
    )
    split, start = [], 0
    for value in vectors:
        split.append(small[start : start + value.size])
        start += value.size
    qkv_vector = split[0].reshape(TILES, 3, TILE).swapaxes(0, 1).reshape(3, width)
    return (
        result_out, grad_out, qkv_total, qkv_vector[0], qkv_vector[2], split[8].reshape(bias_table.shape), proj_total,
        split[1], split[2], split[3], split[4], split[5], up_total, split[6], down_total, split[7],
    )


def solution(mesh):
    grid = P("row", "col", None)
    return jax.shard_map(
        body,
        mesh=mesh,
        in_specs=(grid, P("row", "col")) + (P(),) * 14 + (grid,),
        out_specs=(grid, grid) + (P(),) * 14,
        check_vma=False,
    )
```

```python
import functools

import jax
import jax.numpy as jnp
from jax import lax
from jax.experimental import pallas as pl
from jax.experimental.pallas import tpu as pltpu
from jax.sharding import PartitionSpec as P

WIN = 10
SHIFT = 5
PLACES = WIN * WIN
PAD = 104
GROUP = 4
ROWS = GROUP * PAD
SLAB = 32
EDGE = 16
TILE = 128
TILES = 4

norm_eps = 1e-05
far_below = -1000000000.0
LOG2E = 1.4426950408889634
bf16 = jnp.bfloat16
f32 = jnp.float32


def dot(left, right, left_dim=1, right_dim=0):
    return lax.dot_general(
        left, right, (((left_dim,), (right_dim,)), ((), ())), preferred_element_type=f32
    )


def whole(array):
    count = len(array.shape)
    return pl.BlockSpec(array.shape, lambda *ids: (0,) * count)


SHORT = pl.CostEstimate(flops=1, bytes_accessed=1, transcendentals=0)


IN_VMEM = pl.BlockSpec(memory_space=pltpu.VMEM)


def params():
    return pltpu.CompilerParams(vmem_limit_bytes=60 * 2**20)


def norm_parts(values):
    center = values - jnp.mean(values, axis=-1, keepdims=True)
    rstd = lax.rsqrt(jnp.mean(center * center, axis=-1, keepdims=True) + norm_eps)
    return center * rstd, rstd


def norm_pull(grad, unit, rstd, gain):
    scaled = grad * gain
    return rstd * (
        scaled
        - jnp.mean(scaled, axis=-1, keepdims=True)
        - unit * jnp.mean(scaled * unit, axis=-1, keepdims=True)
    )


def head_masks():
    lane = lax.broadcasted_iota(jnp.int32, (1, 128), 1) // 32
    return [(lane == head).astype(f32).astype(bf16) for head in range(4)]


def spread_heads(tile):
    return jnp.concatenate([tile * mask for mask in head_masks()], axis=0)


def gather_heads(stacked):
    lane = lax.broadcasted_iota(jnp.int32, (PAD, 128), 1) // 32
    out = stacked[0:PAD]
    for head in range(1, 4):
        out = jnp.where(lane == head, stacked[PAD * head : PAD * (head + 1)], out)
    return out


def prepare_kernel(*refs):
    for rows, cols, rows_out, cols_out, corner_out in (refs[0:2] + refs[4:7], refs[2:4] + refs[7:10]):
        rows_out[...] = rows[...]
        cols_out[...] = cols[...]
        corner_out[...] = cols[0:SHIFT]


def window_rows(refs, local, col):
    upper, lower, upper_right, lower_right = refs
    count, wide, width = upper.shape
    first = col * WIN + SHIFT
    start = pl.multiple_of(jnp.minimum(first // 16 * 16, wide - SLAB), 16)
    half, side = count * SLAB, count * EDGE
    cols = pl.ds(start, SLAB)
    inside = lax.broadcasted_iota(jnp.int32, (1, SLAB, width), 1) + start < local
    slab = jnp.concatenate(
        (
            jnp.where(inside, upper[:, cols, :], 0).reshape(half, width),
            jnp.where(inside, lower[:, cols, :], 0).reshape(half, width),
            upper_right[...].reshape(side, width),
            lower_right[...].reshape(side, width),
        ),
        axis=0,
    )
    place = lax.broadcasted_iota(jnp.int32, (PAD, 1), 0)
    prow = (place * 205) >> 11
    pcol = place - WIN * prow + first
    target = jnp.where(pcol < local, prow * SLAB + pcol - start, 2 * half + prow * EDGE + pcol - local)
    target = jnp.where(place < PLACES, target, -1)
    lane = lax.broadcasted_iota(jnp.int32, (PAD, 2 * (half + side)), 1)
    hot = (lane == target).astype(f32).astype(bf16)
    return dot(hot, slab)


def halo_specs(block_row, last, local_cols, width):
    wide, below = -(-local_cols // 16) * 16, 0 if last else block_row + 1
    return [
        pl.BlockSpec((SHIFT, columns, width), lambda i, at=at: (at, 0, 0))
        for columns in (wide, EDGE)
        for at in (block_row, below)
    ]


def forward_kernel(local, first, *refs):
    sources, grad_sources, refs = refs[0:4], refs[4:8], refs[8:]
    (
        label_row, bias, qkv, qkv_bias, proj, proj_bias, gain_one, shift_one, *refs
    ) = refs
    if not first:
        refs = refs[7:]
    inputs, normed_one, joined, probs, mixed, middle, upstream, upstream_sum, *refs = refs
    part = pl.program_id(0)
    if first:
        qkv_low, proj_low, *refs = refs

        @pl.when(part == 0)
        def _():
            for tile in range(TILES):
                for kind in range(3):
                    lanes = 3 * TILE * tile + TILE * kind
                    source = qkv.shape[0] * kind + TILE * tile
                    qkv_low[:, lanes : lanes + TILE] = qkv[:, source : source + TILE].astype(bf16)
            proj_low[...] = proj[...].astype(bf16)

    else:
        qkv_low, proj_low = qkv, proj
    rows_s, joined_s, mixed_s = refs

    @pl.when(part == 0)
    def _():
        upstream_sum[...] = jnp.zeros_like(upstream_sum)

    for window in range(GROUP):
        rows_s[PAD * window : PAD * (window + 1), :] = window_rows(sources, local, part * GROUP + window)
    rows = rows_s[...]
    inputs[...] = rows.astype(bf16)
    unit, _ = norm_parts(rows)
    normed = (unit * gain_one[...] + shift_one[...]).astype(bf16)
    normed_one[...] = normed
    joined_s[...] = dot(normed, qkv_low[...]) + qkv_bias[...]
    for window in range(GROUP):
        mixed_s[PAD * window : PAD * (window + 1), :] = window_rows(grad_sources, local, part * GROUP + window)
    upstream[...] = mixed_s[...].astype(bf16)
    upstream_sum[...] += column_sum(mixed_s[...])

    def attend(window, _):
        at = pl.ds(pl.multiple_of(window * PAD, 8), PAD)
        joined[window] = joined_s[at, :].astype(bf16)
        labels = jnp.broadcast_to(label_row[window], (PAD, PAD))
        masked = jnp.where(labels.T == labels, 0.0, far_below)
        for tile in range(TILES):
            lanes = 3 * TILE * tile
            queries = joined_s[at, lanes : lanes + TILE].astype(bf16)
            keys = joined_s[at, lanes + TILE : lanes + 2 * TILE].astype(bf16)
            values = joined_s[at, lanes + 2 * TILE : lanes + 3 * TILE].astype(bf16)
            raw = dot(spread_heads(keys), queries, 1, 1)
            parts = []
            for head in range(4):
                scores = raw[PAD * head : PAD * (head + 1)] * (LOG2E * 32**-0.5) + (
                    bias[4 * tile + head] + masked
                )
                powers = jnp.exp2(scores - jnp.max(scores, axis=0, keepdims=True))
                total = jnp.sum(powers, axis=0, keepdims=True)
                parts.append((powers * (1.0 / total)).astype(bf16))
            stacked = jnp.concatenate(parts, axis=0)
            probs[window, tile] = stacked
            mixed_s[at, TILE * tile : TILE * (tile + 1)] = dot(stacked, spread_heads(values), 0, 0)
        return 0

    lax.fori_loop(0, GROUP, attend, 0)
    mixed_low = mixed_s[...].astype(bf16)
    mixed[...] = mixed_low
    middle[...] = rows_s[...] + dot(mixed_low, proj_low[...]) + proj_bias[...]


def column_sum(values):
    return jnp.sum(values, axis=0, keepdims=True)


def store_halves(core, last, total, start, keep, send):
    half = total.shape[0] // 2
    at = slice(start, start + half)

    @pl.when(last & (core == 0))
    def _():
        keep[at, :] = total[0:half, :]
        send[at, :] = total[half : 2 * half, :].astype(bf16)

    @pl.when(last & (core != 0))
    def _():
        keep[at, :] = total[half : 2 * half, :]
        send[at, :] = total[0:half, :].astype(bf16)


def store_mixed_halves(core, last, first, second, keep, send):
    sizes = [first.shape[0] // 8, second.shape[0] // 8]

    for side in range(2):

        @pl.when(last & (core == side))
        def _():
            start = 0
            for quarter in range(4):
                for total, size in ((first, sizes[0]), (second, sizes[1])):
                    mine = (4 * side + quarter) * size
                    other = (4 * (1 - side) + quarter) * size
                    keep[start : start + size, :] = total[mine : mine + size, :]
                    send[start : start + size, :] = total[other : other + size, :].astype(bf16)
                    start += size


def middle_kernel(
    core, upstream, middle, mixed, up_weight, up_bias, down_weight, down_bias, proj, gain, shift,
    out, below, edge, middle_grad_out, mixed_grad, keep, send, up_bias_grad, proj_sums, gain_grad, shift_grad,
    windows_s, mixed_grad_s, up, down, ff_grad, proj_grad,
):
    part = pl.program_id(1)
    step = pl.program_id(0) * pl.num_programs(1) + part

    @pl.when(step == 0)
    def _():
        up[...] = up_weight[...].astype(bf16)
        down[...] = down_weight[...].astype(bf16)
        for ref in (ff_grad, proj_grad, up_bias_grad, proj_sums, gain_grad, shift_grad):
            ref[...] = jnp.zeros_like(ref)

    unit, rstd = norm_parts(middle[...])
    normed = (unit * gain[...] + shift[...]).astype(bf16)
    given = upstream[...]
    result = middle[...] + down_bias[...]
    normed_grad = 0.0
    width, units = up.shape
    for start in range(0, units, width):
        at = slice(start, start + width)
        down_at = slice(units + start, units + start + width)
        hidden = dot(normed, up[:, at]) + up_bias[:, at]
        under = 0.5 + 0.5 * lax.erf(hidden * (2.0**-0.5))
        active_low = (hidden * under).astype(bf16)
        slope = under + hidden * (jnp.exp2(hidden * hidden * (-0.5 * LOG2E)) * 0.3989422804014327)
        grad_low = (slope * dot(given, down[at, :], 1, 1)).astype(bf16)
        up_bias_grad[:, at] += column_sum(grad_low.astype(f32))
        ff_grad[at, :] += dot(normed, grad_low, 0, 0)
        ff_grad[down_at, :] += dot(active_low, given, 0, 0)
        result += dot(active_low, down[at, :])
        normed_grad += dot(grad_low, up[:, at], 1, 1)
    store_windows(windows_s, result, part)
    gain_grad[...] += column_sum(normed_grad * unit)
    shift_grad[...] += column_sum(normed_grad)
    middle_grad = norm_pull(normed_grad, unit, rstd, gain[...]) + given.astype(f32)
    middle_grad_out[...] = middle_grad
    branch_low = middle_grad.astype(bf16)
    proj_sums[...] += column_sum(branch_low.astype(f32))
    proj_grad[...] += dot(mixed[...], branch_low, 0, 0)
    mixed_grad_s[...] = dot(branch_low, proj[...], 1, 1)
    for window in range(GROUP):
        mixed_grad[window] = mixed_grad_s[PAD * window : PAD * (window + 1)].astype(bf16)
    windows_to_grid(windows_s, out, below, edge)
    last = step == pl.num_programs(0) * pl.num_programs(1) - 1
    store_mixed_halves(core[0], last, ff_grad, proj_grad, keep, send)


def attention_pull_kernel(core, normed_one, joined, probs, mixed_grad, *refs):
    joined_grad, keep, send, sums, bias_grad, joined_s, qkv_grad, bias_s = refs[-8:]

    @pl.when(pl.program_id(0) == 0)
    def _():
        for ref in (qkv_grad, sums, bias_s):
            ref[...] = jnp.zeros_like(ref)

    for tile in range(probs.shape[1]):
        lanes = 3 * TILE * tile
        for window in range(GROUP):
            at = slice(PAD * window, PAD * (window + 1))
            queries = joined[window, :, lanes : lanes + TILE]
            keys = joined[window, :, lanes + TILE : lanes + 2 * TILE]
            values = joined[window, :, lanes + 2 * TILE : lanes + 3 * TILE]
            grad = mixed_grad[window, :, TILE * tile : TILE * (tile + 1)]
            probs_grad = dot(spread_heads(values), grad, 1, 1)
            probs_low = probs[window, tile]
            parts = []
            for head in range(4):
                here = slice(PAD * head, PAD * (head + 1))
                prob = probs_low[here].astype(f32)
                product = prob * probs_grad[here]
                score_grad = product - prob * column_sum(product)
                bias_s[window, 4 * tile + head] += score_grad
                parts.append((score_grad * 32**-0.5).astype(bf16))
            draw = jnp.concatenate(parts, axis=0)
            joined_s[at, lanes : lanes + TILE] = dot(draw, spread_heads(keys), 0, 0)
            joined_s[at, lanes + TILE : lanes + 2 * TILE] = gather_heads(dot(draw, queries))
            joined_s[at, lanes + 2 * TILE : lanes + 3 * TILE] = gather_heads(dot(probs_low, grad))
    joined_low = joined_s[...].astype(bf16)
    joined_grad[...] = joined_low
    sums[...] += column_sum(joined_low.astype(f32))
    qkv_grad[...] += dot(normed_one[...], joined_low, 0, 0)
    last = pl.program_id(0) == pl.num_programs(0) - 1

    @pl.when(last)
    def _():
        for head in range(bias_grad.shape[0]):
            bias_grad[head] = (bias_s[0, head] + bias_s[1, head]) + (bias_s[2, head] + bias_s[3, head])

    for tile in range(probs.shape[1]):
        columns = qkv_grad.at[:, 3 * TILE * tile : 3 * TILE * (tile + 1)]
        half = columns.shape[0] // 2
        store_halves(core[0], last, columns, half * tile, keep, send)


def windows_to_grid(windows, out, below, edge):
    count, _, width = windows.shape
    cols = count * WIN
    window_row, last_row = pl.program_id(0), pl.num_programs(0) - 1

    @pl.when(pl.program_id(1) == pl.num_programs(1) - 1)
    def _():
        spot = lax.broadcasted_iota(jnp.int32, (cols + EDGE, 1), 0)
        col = spot - SHIFT
        window = (col * 205) >> 11
        valid = (col >= 0) & (col < cols)
        lane = lax.broadcasted_iota(jnp.int32, (cols + EDGE, count * 16), 1)
        for row in range(WIN):
            start = WIN * row // 8 * 8
            offset = WIN * row - start
            slab = windows[:, start : start + 16, :].reshape(count * 16, width).astype(bf16)
            target = jnp.where(valid, col + (16 - WIN) * window + offset, -1)
            moved_rows = dot((lane == target).astype(f32).astype(bf16), slab)
            main, side = moved_rows[0:cols].astype(bf16), moved_rows[cols : cols + EDGE].astype(bf16)
            at = WIN * window_row + row + SHIFT
            if row < WIN - SHIFT:
                out[at] = main
                edge[at] = side
            else:

                @pl.when(window_row < last_row)
                def _():
                    out[at] = main
                    edge[at] = side

                @pl.when(window_row == last_row)
                def _():
                    below[row - (WIN - SHIFT)] = moved_rows.astype(bf16)


def place_kernel(given, above, left, out, rows_s, cols_s, semaphores):
    cols, count = rows_s.shape[1], cols_s.shape[0]
    edge = out.at[pl.ds(SHIFT, count), pl.ds(0, EDGE), :]
    fetch = pltpu.make_async_copy(edge, cols_s, semaphores.at[0])
    fetch.start()
    first = lax.broadcasted_iota(jnp.int32, (1, EDGE, 1), 1) < SHIFT
    rows_s[:, 0:EDGE, :] = jnp.where(first, left[0:SHIFT], above[:, 0:EDGE, :])
    rows_s[:, EDGE:cols, :] = above[:, EDGE:cols, :]
    rows = pltpu.make_async_copy(rows_s, out.at[pl.ds(0, SHIFT)], semaphores.at[1])
    rows.start()
    fetch.wait()
    cols_s[...] = jnp.where(first, left[SHIFT : SHIFT + count], cols_s[...])
    store = pltpu.make_async_copy(cols_s, edge, semaphores.at[2])
    store.start()
    rows.wait()
    store.wait()


def store_windows(windows_s, values, part):
    for window in range(GROUP):
        windows_s[part * GROUP + window] = values[PAD * window : PAD * (window + 1)]


def inputs_grad_kernel(
    joined_grad, inputs, middle_grad, qkv, gain, out, below, edge, gain_grad, shift_grad, windows_s
):
    part = pl.program_id(1)

    @pl.when((pl.program_id(0) == 0) & (part == 0))
    def _():
        gain_grad[...] = jnp.zeros_like(gain_grad)
        shift_grad[...] = jnp.zeros_like(shift_grad)

    normed_grad = dot(joined_grad[...], qkv[...], 1, 1)
    unit, rstd = norm_parts(inputs[...].astype(f32))
    gain_grad[...] += column_sum(normed_grad * unit)
    shift_grad[...] += column_sum(normed_grad)
    store_windows(windows_s, norm_pull(normed_grad, unit, rstd, gain[...]) + middle_grad[...], part)
    windows_to_grid(windows_s, out, below, edge)


def flipped(value, row_bits, col_bits):
    rows, cols = lax.axis_size("row"), lax.axis_size("col")
    pairs = [(r * cols + c, (r ^ row_bits) * cols + (c ^ col_bits)) for r in range(rows) for c in range(cols)]
    return lax.ppermute(value, ("row", "col"), pairs)


def block(ref, index, rows):
    return ref[pl.ds(pl.multiple_of(index * rows, 8), rows), :]


def split_kernel(place, kept, got, *outs):
    total = kept[...] + got[...].astype(f32)
    for other in range(4):

        @pl.when(pl.program_id(0) == other)
        def _():
            outs[other][...] = total.astype(outs[other].dtype)


def split_again_kernel(place, kept, first, second, third, *refs):
    outs, total = refs[:-1], refs[-1]
    total[...] = kept[...] + first[...].astype(f32) + second[...].astype(f32) + third[...].astype(f32)
    rows = outs[0].shape[0]
    outs[0][...] = block(total, place[0], rows)
    for other in range(1, 4):
        outs[other][...] = block(total, place[0] ^ other, rows).astype(bf16)


def add_kernel(kept, first, second, third, *refs):
    out, rows = refs[-1], kept.shape[0]
    total = kept[...] + first[...].astype(f32) + second[...].astype(f32) + third[...].astype(f32)
    out[0:rows, :] = total.astype(out.dtype)


def pack_rows(vectors):
    columns, spots, at = 3 * TILE, [], 0
    for index, vector in enumerate(vectors):
        if vector.shape[0] > 1:
            at = -(-at // 8) * 8
            spots.append((index, None, 0, at, columns))
            at += vector.shape[0]
            continue
        for start in range(0, vector.shape[1], columns):
            spots.append((index, 0, start, at, min(columns, vector.shape[1] - start)))
            at += 1
    return spots, -(-at // 8) * 8


def pack(vectors, packed):
    packed[...] = jnp.zeros_like(packed)
    for index, row, start, at, size in pack_rows(vectors)[0]:
        if row is None:
            packed[at : at + vectors[index].shape[0], :] = vectors[index][...]
        else:
            packed[at : at + 1, 0:size] = vectors[index][:, start : start + size]


def pack_kernel(*refs):
    pack(refs[:-1], refs[-1])


def add_and_pack_kernel(kept, first, second, third, *refs):
    *vectors, out, packed = refs
    add_kernel(kept, first, second, third, out)
    pack(vectors, packed)
    store_pair(out, kept.shape[0], packed[...])


def store_pair(out, start, values):
    size = values.shape[0]
    high = values.astype(bf16)
    out[start : start + size, :] = high
    out[start + size : start + 2 * size, :] = (values - high.astype(f32)).astype(bf16)


def pair_sum(refs, start, size):
    total = 0.0
    for ref in refs:
        total += ref[start : start + size, :].astype(f32) + ref[start + size : start + 2 * size, :].astype(f32)
    return total


def join_kernel(place, *refs):
    pieces, out, joined_s = refs[:4], refs[4], refs[5]
    rows = joined_s.shape[0] // 4
    for other in range(4):
        at = pl.ds(pl.multiple_of((place[0] ^ other) * rows, 8), rows)
        joined_s[at, :] = pieces[other][0:rows, :].astype(f32)
    out[0 : 4 * rows, :] = joined_s[...].astype(bf16)
    extra = (pieces[0].shape[0] - rows) // 2
    if extra:
        store_pair(out, 4 * rows, pair_sum(pieces, rows, extra))


def scalar_call(kernel, scalar, *operands, outs, scratch=()):
    return pl.pallas_call(
        kernel,
        grid_spec=pltpu.PrefetchScalarGridSpec(
            num_scalar_prefetch=1,
            grid=(1,),
            in_specs=[IN_VMEM] * len(operands),
            out_specs=[IN_VMEM] * len(outs),
            scratch_shapes=list(scratch),
        ),
        out_shape=list(outs),
        compiler_params=params(),
            cost_estimate=SHORT,
    )(scalar, *operands)


def struct(shape, dtype):
    return jax.ShapeDtypeStruct(shape, dtype)


def places():
    row, col = lax.axis_index("row"), lax.axis_index("col")
    one = lambda value: jnp.reshape(value, (1,)).astype(jnp.int32)
    return one(col & 1), one(((col >> 1) & 1) | ((row & 1) << 1)), one((row >> 1) & 3)


class Order:
    def __init__(self):
        self.last = []

    def __call__(self, call, *operands):
        if self.last:
            operands, _ = lax.optimization_barrier((operands, self.last))
        results = call(*operands)
        self.last = [jax.tree.leaves(results)[0]]
        return results

    def later(self, value):
        return lax.optimization_barrier((value, self.last))[0]

    def hold(self, *values):
        self.last.extend(values)


def sum_over_devices(order, kept, sent, small_vectors=None):
    _, plane, depth = places()
    plane_flips = ((0, 2), (1, 0), (1, 2))
    depth_flips = ((2, 0), (4, 0), (6, 0))
    got = flipped(sent, 0, 1)
    rows, width = kept.shape
    quarter, small = rows // 4, rows // 16
    yield
    outs = [struct((quarter, width), f32)] + [struct((quarter, width), bf16)] * 3

    def split(*operands):
        block = pl.BlockSpec((quarter, width), lambda i, s: (s[0] ^ i, 0))
        return pl.pallas_call(
            split_kernel,
            grid_spec=pltpu.PrefetchScalarGridSpec(
                num_scalar_prefetch=1,
                grid=(4,),
                in_specs=[block] * 2,
                out_specs=[pl.BlockSpec((quarter, width), lambda i, s: (0, 0), pipeline_mode=pl.Buffered(1))] * 4,
            ),
            out_shape=outs,
            compiler_params=params(),
            cost_estimate=SHORT,
        )(plane, *operands)

    own, *sends = order(split, kept, got)
    got = [flipped(piece, *flip) for piece, flip in zip(sends, plane_flips)]
    yield
    outs = [struct((small, width), f32)] + [struct((small, width), bf16)] * 3
    call = functools.partial(
        scalar_call, split_again_kernel, depth, outs=outs, scratch=[pltpu.VMEM((quarter, width), f32)]
    )
    own, *sends = order(call, own, *got)
    got = [flipped(piece, *flip) for piece, flip in zip(sends, depth_flips)]
    yield got
    vectors = [] if small_vectors is None else small_vectors()
    packed_rows = pack_rows(vectors)[1]
    ride = 2 * packed_rows
    further = []
    bit = 8
    while bit < lax.axis_size("row"):
        further.append(bit)
        bit *= 2
    if further:
        call = pl.pallas_call(add_kernel, out_shape=struct((small, width), f32), cost_estimate=SHORT)
        done = order(call, own, *got)
        extra = []
        if vectors:
            extra = [pl.pallas_call(pack_kernel, out_shape=struct((packed_rows, width), f32))(*vectors)]
        for bit in further:
            done = done + flipped(done.astype(bf16), bit, 0).astype(f32)
            extra = [value + flipped(value, bit, 0) for value in extra]
        done = done.astype(bf16)
        for value in extra:
            high = lax.reduce_precision(value, 8, 7)
            done = jnp.concatenate((done, high.astype(bf16), (value - high).astype(bf16)))
    else:
        call = pl.pallas_call(
            add_and_pack_kernel if vectors else add_kernel,
            out_shape=struct((small + ride, width), bf16),
            in_specs=[IN_VMEM] * (4 + len(vectors)),
            out_specs=IN_VMEM,
            scratch_shapes=[pltpu.VMEM((packed_rows, width), f32)] if vectors else [],
            cost_estimate=SHORT,
        )
        done = order(call, own, *got, *vectors)
    pieces = [done] + [flipped(done, *flip) for flip in depth_flips]
    yield pieces
    call = functools.partial(
        scalar_call, join_kernel, depth, outs=[struct((quarter + ride, width), bf16)],
        scratch=[pltpu.VMEM((quarter, width), f32)],
    )
    (mine,) = order(call, *pieces)
    if vectors:
        mine = [mine] + [flipped(mine, *flip) for flip in plane_flips]
    else:
        mine = [mine] + [flipped(mine, *flip) for flip in plane_flips[:2]]
        yield mine
        mine.append(flipped(order.later(mine[1]), *plane_flips[1]))
    yield mine
    pieces = mine + [flipped(piece if vectors else order.later(piece), 0, 1) for piece in mine]
    yield pieces


def finish_kernel(write, plane, core, *refs):
    pieces, out, small_outs, (total, packed) = refs[:8], refs[8], refs[9:-2], refs[-2:]
    rows = total.shape[1] // 4
    for other in range(4):
        at = pl.ds(pl.multiple_of((plane[0] ^ other) * rows, 8), rows)
        total[core[0], at, :] = pieces[other][0:rows, :].astype(f32)
        total[1 - core[0], at, :] = pieces[4 + other][0:rows, :].astype(f32)
    write(total, out)
    packed[...] = pair_sum(pieces, rows, packed.shape[0])
    query_out, value_out, *vector_outs, table_out = small_outs
    for tile in range(TILES):
        at = slice(TILE * tile, TILE * (tile + 1))
        query_out[:, at] = packed[tile : tile + 1, 0:TILE]
        value_out[:, at] = packed[tile : tile + 1, 2 * TILE : 3 * TILE]
    table_rows = struct((table_out.shape[0], 3 * TILE), f32)
    spots, _ = pack_rows([struct((1, 3 * TILE * TILES), f32), *vector_outs, table_rows])
    for index, row, start, at, size in spots:
        if row is None:
            table_out[...] = packed[at : at + table_rows.shape[0], 0 : table_out.shape[1]]
        elif index > 0:
            vector_outs[index - 1][:, start : start + size] = packed[at : at + 1, 0:size]


def finish(order, pieces, write, outs, small_outs):
    core, plane, _ = places()
    rows, width = pieces[0].shape
    table = struct((small_outs[-1].shape[0], width), f32)
    packed_rows = pack_rows([struct((1, width * TILES), f32), *small_outs[2:-1], table])[1]
    outs = outs + small_outs

    def call(*operands):
        return pl.pallas_call(
            functools.partial(finish_kernel, write),
            grid_spec=pltpu.PrefetchScalarGridSpec(
                num_scalar_prefetch=2,
                grid=(1,),
                in_specs=[IN_VMEM] * len(pieces),
                out_specs=[pl.BlockSpec(a.shape, lambda i, s, t: (0, 0)) for a in outs],
                scratch_shapes=[
                    pltpu.VMEM((2, 4 * (rows - 2 * packed_rows), width), f32), pltpu.VMEM((packed_rows, width), f32),
                ],
            ),
            out_shape=outs,
            compiler_params=params(),
            cost_estimate=SHORT,
        )(plane, core, *operands)

    return order(call, *pieces)


def finish_middle_kernel(plane, core, *refs):
    pieces, (up_out, down_out, proj_out) = refs[:8], refs[8:]
    size = up_out.shape[1]
    rest = pieces[0].shape[0] - size
    for other in range(4):
        for side in range(2):

            @pl.when((pl.program_id(0) == other) & (core[0] == side))
            def _():
                ups, downs = pieces[other + 4 * side], pieces[other + 4 * (1 - side)]
                up_out[...] = ups[0:size, :].astype(f32)
                down_out[...] = downs[0:size, :].astype(f32)
                at = pl.multiple_of((plane[0] ^ other) * rest, 8)
                proj_out[pl.ds(at, rest), :] = ups[size:, :].astype(f32)
                proj_out[pl.ds(at + 4 * rest, rest), :] = downs[size:, :].astype(f32)


def finish_middle(order, pieces, width, units):
    core, plane, _ = places()

    def call(*operands):
        return pl.pallas_call(
            finish_middle_kernel,
            grid_spec=pltpu.PrefetchScalarGridSpec(
                num_scalar_prefetch=2,
                grid=(4,),
                in_specs=[pl.BlockSpec(a.shape, lambda i, s, t: (0, 0), pipeline_mode=pl.Buffered(1)) for a in pieces],
                out_specs=[
                    pl.BlockSpec((width, units // 4), lambda i, s, t: (0, s[0] ^ i)),
                    pl.BlockSpec((units // 4, width), lambda i, s, t: (s[0] ^ i, 0)),
                    pl.BlockSpec((width, width), lambda i, s, t: (0, 0)),
                ],
            ),
            out_shape=[struct((width, units), f32), struct((units, width), f32), struct((width, width), f32)],
            compiler_params=params(),
            cost_estimate=SHORT,
        )(plane, core, *operands)

    return order(call, *pieces)


def moved(value, row_step, col_step):
    rows, cols = lax.axis_size("row"), lax.axis_size("col")
    pairs = [
        (r * cols + c, ((r - row_step) % rows) * cols + (c - col_step) % cols) for r in range(rows) for c in range(cols)
    ]
    return lax.ppermute(value, ("row", "col"), pairs)


def relative_index():
    spots = jnp.arange(PLACES, dtype=jnp.int32)
    prow, pcol = spots // WIN, spots % WIN
    return (prow[None, :] - prow[:, None] + WIN - 1) * (2 * WIN - 1) + (pcol[None, :] - pcol[:, None] + WIN - 1)


def by_tile(array):
    return array.reshape(3, TILES, TILE).swapaxes(0, 1).reshape(1, 3 * TILES * TILE)


def thirds(values):
    terms = []
    for _ in range(3):
        term = lax.reduce_precision(values, 8, 7)
        terms.append(term.astype(bf16))
        values = values - term
    return jnp.concatenate(terms)


def exact_dot(values, onehot, dim):
    product = lax.dot_general(thirds(values), onehot, (((1,), (dim,)), ((), ())), preferred_element_type=f32)
    first, second, third = jnp.split(product, 3)
    return first + (second + third)


def body(
    patches, region_ids, qkv_weight, query_bias, value_bias, bias_table, proj_weight, proj_bias, gain_one, shift_one,
    gain_two, shift_two, up_weight, up_bias, down_weight, down_bias, cotangent,
):
    local_rows, local_cols, width = patches.shape
    heads = bias_table.shape[1]
    hidden_units = up_weight.shape[1]
    wrows, wcols = local_rows // WIN, local_cols // WIN
    windows = wrows * wcols
    tokens = windows * PAD
    steps = wcols // GROUP
    wide = -(-local_cols // 16) * 16
    row = lambda vector: vector[None]
    core, _, _ = places()
    order = Order()

    def prepare(first, second):
        rows_block = pl.BlockSpec((SHIFT, local_cols, width), lambda i: (0, 0, 0))
        cols_block = pl.BlockSpec((local_rows, EDGE, width), lambda i: (0, 0, 0))
        corner_block = pl.BlockSpec((SHIFT, EDGE, width), lambda i: (0, 0, 0))
        return pl.pallas_call(
            prepare_kernel,
            grid=(1,),
            in_specs=[rows_block, cols_block] * 2,
            out_specs=[rows_block, cols_block, corner_block] * 2,
            out_shape=[
                struct((SHIFT, local_cols, width), bf16), struct((local_rows, EDGE, width), bf16),
                struct((SHIFT, EDGE, width), bf16),
            ] * 2,
            compiler_params=params(),
            cost_estimate=SHORT,
        )(first, first, second, second)

    edges = order(prepare, patches, cotangent)
    right, right_grad = moved(edges[1], 0, 1), moved(edges[4], 0, 1)
    below, across = moved(edges[0], 1, 0), moved(edges[2], 1, 1)
    below_grad, across_grad = moved(edges[3], 1, 0), moved(edges[5], 1, 1)
    labels = region_ids.reshape(wrows, WIN, wcols, WIN).transpose(0, 2, 1, 3).reshape(windows, PLACES)
    labels = jnp.pad(labels, ((0, 0), (0, PAD - PLACES)), constant_values=-1)
    entries = -(-bias_table.shape[0] // TILE) * TILE
    onehot = (relative_index().reshape(-1)[:, None] == jnp.arange(entries, dtype=jnp.int32)[None, :]).astype(bf16)
    table = jnp.pad(bias_table.T, ((0, 0), (0, entries - bias_table.shape[0])))
    position_bias = exact_dot(table, onehot, 1).reshape(heads, PLACES, PLACES) * LOG2E
    position_bias = jnp.pad(position_bias, ((0, 0), (0, 0), (0, PAD - PLACES)))
    position_bias = jnp.pad(position_bias, ((0, 0), (0, PAD - PLACES), (0, 0)), constant_values=far_below)
    qkv_bias = by_tile(jnp.concatenate((query_bias, jnp.zeros_like(query_bias), value_bias)))

    token_arrays = [
        struct((tokens, width), bf16), struct((tokens, width), bf16), struct((windows, PAD, 3 * width), bf16),
        struct((windows, TILES, 4 * PAD, PAD), bf16), struct((tokens, width), bf16), struct((tokens, width), f32),
        struct((tokens, width), bf16),
    ]
    made, upstream_sums = [], []
    qkv_low, proj_low = qkv_weight, proj_weight
    labels = labels[:, None, :].astype(f32)
    for index in range(wrows):
        first, last = index == 0, index == wrows - 1
        block_of = lambda array: pl.BlockSpec(
            (array.shape[0] // (wrows * steps),) + array.shape[1:],
            lambda i, n=len(array.shape), index=index: (index * steps + i,) + (0,) * (n - 1),
        )
        specs = halo_specs(2 * index + 1, last, local_cols, width)
        operands = (
            position_bias, qkv_low, qkv_bias, proj_low, row(proj_bias), row(gain_one), row(shift_one),
        )
        lows = [struct(qkv_weight.shape, bf16), struct(proj_weight.shape, bf16)] if first else []
        call = pl.pallas_call(
            functools.partial(forward_kernel, local_cols, first),
            grid=(steps,),
            in_specs=specs * 2 + [block_of(labels)] + [whole(a) for a in operands]
            + [pl.BlockSpec(memory_space=pl.ANY)] * len(made),
            out_specs=[block_of(a) for a in token_arrays]
            + [pl.BlockSpec((1, width), lambda i: (0, 0))] + [whole(a) for a in lows],
            out_shape=token_arrays + [struct((1, width), f32)] + lows,
            input_output_aliases={16 + i: i for i in range(len(made))},
            scratch_shapes=[
                pltpu.VMEM((ROWS, width), f32), pltpu.VMEM((ROWS, 3 * width), f32), pltpu.VMEM((ROWS, width), f32),
            ],
            compiler_params=params(),
            cost_estimate=SHORT,
        )
        around = (patches, below if last else patches, right, across if last else right)
        around_grad = (cotangent, below_grad if last else cotangent, right_grad, across_grad if last else right_grad)
        outs = order(call, *around, *around_grad, labels, *operands, *made)
        made, total = outs[: len(token_arrays)], outs[len(token_arrays)]
        if first:
            qkv_low, proj_low = outs[-2:]
        upstream_sums.append(total)
    inputs, normed_one, joined, probs, mixed, middle, upstream = made
    down_bias_grad = sum(upstream_sums)
    rows_of = lambda columns: pl.BlockSpec((ROWS, columns), lambda i, *_: (i, 0))
    win_of = lambda *shape: pl.BlockSpec((GROUP,) + shape, lambda i, *_: (i,) + (0,) * len(shape))
    fixed = lambda array: pl.BlockSpec(array.shape, lambda i, *_: (0,) * len(array.shape))

    def core_call(kernel, in_specs, out_specs, out_shape, scratch, aliases):
        return pl.pallas_call(
            kernel,
            grid_spec=pltpu.PrefetchScalarGridSpec(
                num_scalar_prefetch=1,
                grid=(tokens // ROWS,),
                in_specs=in_specs,
                out_specs=out_specs,
                scratch_shapes=scratch,
            ),
            out_shape=out_shape,
            input_output_aliases=aliases,
            compiler_params=params(),
            cost_estimate=SHORT,
        )

    def attention_pull(tile, count, *made):
        rows, columns, at = width // 2 * count, 3 * TILE * count, tile // count
        outs = [
            struct((tokens, 3 * width), bf16), struct((width // 2 * TILES, 3 * TILE), f32),
            struct((width // 2 * TILES, 3 * TILE), bf16), struct((1, 3 * width), f32), struct((heads, PAD, PAD), f32),
        ]
        part = heads // TILES * count
        call = core_call(
            attention_pull_kernel,
            [
                rows_of(width),
                pl.BlockSpec((GROUP, PAD, columns), lambda i, s: (i, 0, at)),
                pl.BlockSpec((GROUP, count, 4 * PAD, PAD), lambda i, s: (i, at, 0, 0)),
                pl.BlockSpec((GROUP, PAD, TILE * count), lambda i, s: (i, 0, at)),
            ]
            + [pl.BlockSpec(memory_space=pl.ANY)] * len(made),
            [
                pl.BlockSpec((ROWS, columns), lambda i, s: (i, at)),
                pl.BlockSpec((rows, 3 * TILE), lambda i, s: (at, 0)),
                pl.BlockSpec((rows, 3 * TILE), lambda i, s: (at, 0)),
                pl.BlockSpec((1, columns), lambda i, s: (0, at)),
                pl.BlockSpec((part, PAD, PAD), lambda i, s: (at, 0, 0)),
            ],
            outs,
            [
                pltpu.VMEM((ROWS, columns), f32), pltpu.VMEM((width, columns), f32),
                pltpu.VMEM((GROUP, part, PAD, PAD), f32),
            ],
            {5 + i: i for i in range(len(made))},
        )
        return order(call, core, normed_one, joined, probs, mixed_grad, *made)

    def write_qkv(total, out):
        rows = width // 2
        for side in range(2):
            for tile in range(TILES):
                for kind in range(3):
                    at = width * kind + TILE * tile
                    out[rows * side : rows * (side + 1), at : at + TILE] = (
                        total[side, rows * tile : rows * (tile + 1), TILE * kind : TILE * (kind + 1)]
                    )

    token_spec = lambda columns: pl.BlockSpec((ROWS, columns), lambda i, j, *_: (i * steps + j, 0))
    single = lambda array: pl.BlockSpec(
        array.shape, lambda *ids, n=len(array.shape): (0,) * n, pipeline_mode=pl.Buffered(1)
    )
    constant = lambda array: pl.BlockSpec(array.shape, lambda *ids, n=len(array.shape): (0,) * n)
    grid_outs = [
        struct((local_rows, local_cols, width), bf16), struct((SHIFT, local_cols + EDGE, width), bf16),
        struct((local_rows, EDGE, width), bf16),
    ]
    vector = struct((1, width), f32)

    def edge_out(above, edge):
        return moved(jnp.concatenate((above[:, local_cols:], edge[SHIFT:])), 0, -1)

    def place(grid, above, left):
        return order(
            pl.pallas_call(
                place_kernel,
                in_specs=[pl.BlockSpec(memory_space=pl.ANY), IN_VMEM, IN_VMEM],
                out_specs=pl.BlockSpec(memory_space=pl.ANY),
                out_shape=struct(grid.shape, grid.dtype),
                input_output_aliases={0: 0},
                scratch_shapes=[
                    pltpu.VMEM((SHIFT, local_cols, width), bf16), pltpu.VMEM((local_rows - SHIFT, EDGE, width), bf16),
                    pltpu.SemaphoreType.DMA((3,)),
                ],
                compiler_params=params(),
                cost_estimate=SHORT,
            ),
            grid, above, left,
        )

    shared = hidden_units + width // 2
    outs = [
        struct((shared, width), f32), struct((shared, width), bf16), struct((1, hidden_units), f32), vector, vector,
        vector,
    ]
    call = pl.pallas_call(
        middle_kernel,
        grid_spec=pltpu.PrefetchScalarGridSpec(
            num_scalar_prefetch=1,
            grid=(wrows, steps),
            in_specs=[token_spec(width)] * 3
            + [single(up_weight), single(row(up_bias)), single(down_weight)]
            + [single(a) for a in (row(down_bias), proj_low, row(gain_two), row(shift_two))],
            out_specs=[single(a) for a in grid_outs]
            + [token_spec(width), pl.BlockSpec((GROUP, PAD, width), lambda i, j, s: (i * steps + j, 0, 0))]
            + [single(a) for a in outs],
            scratch_shapes=[
                pltpu.VMEM((wcols, PAD, width), f32), pltpu.VMEM((ROWS, width), f32), pltpu.VMEM(up_weight.shape, bf16),
                pltpu.VMEM(down_weight.shape, bf16), pltpu.VMEM((2 * hidden_units, width), f32),
                pltpu.VMEM((width, width), f32),
            ],
        ),
        out_shape=grid_outs + [struct((tokens, width), f32), struct((windows, PAD, width), bf16)] + outs,
        compiler_params=params(),
            cost_estimate=SHORT,
    )
    (
        result_grid, result_below, result_edge, middle_grad, mixed_grad, kept, sent, up_bias_grad, proj_sums, gain_two_grad, shift_two_grad,
    ) = order(
        call, core, upstream, middle, mixed, up_weight, row(up_bias), down_weight, row(down_bias), proj_low,
        row(gain_two), row(shift_two),
    )
    result_above = moved(result_below, -1, 0)
    first_sum = sum_over_devices(order, kept, sent)
    next(first_sum)
    next(first_sum)
    tiles = attention_pull(0, 2)
    tiles = attention_pull(2, 1, *tiles)
    order.hold(result_above)
    in_flight = next(first_sum)
    result_left = edge_out(order.later(result_above), result_edge)
    joined_grad, qkv_kept, qkv_sent, qkv_sums, bias_grad = attention_pull(3, 1, *tiles)
    qkv_sent, _ = lax.optimization_barrier((qkv_sent, in_flight))
    second_sum = sum_over_devices(order, qkv_kept, qkv_sent, lambda: vectors)
    next(second_sum)
    next(first_sum)
    next(second_sum)
    call = pl.pallas_call(
        inputs_grad_kernel,
        grid=(wrows, steps),
        in_specs=[token_spec(3 * width)] + [token_spec(width)] * 2 + [single(qkv_low), single(row(gain_one))],
        out_specs=[single(a) for a in grid_outs] + [single(vector)] * 2,
        out_shape=grid_outs + [vector] * 2,
        scratch_shapes=[pltpu.VMEM((wcols, PAD, width), f32)],
        compiler_params=params(),
            cost_estimate=SHORT,
    )
    grad_grid, grad_below, grad_edge, gain_one_grad, shift_one_grad = order(
        call, joined_grad, inputs, middle_grad, qkv_low, row(gain_one)
    )
    ff_pieces = next(first_sum)
    order.hold(result_left)
    next(second_sum)
    terms = order.later(bias_grad)[:, :PLACES, :PLACES].reshape(heads, -1)
    table_grad = exact_dot(terms, onehot, 0)
    vectors = [
        qkv_sums, proj_sums, gain_one_grad, shift_one_grad, gain_two_grad, shift_two_grad, up_bias_grad, down_bias_grad,
        table_grad,
    ]
    next(second_sum)
    order.hold(ff_pieces[1])
    ff_pieces = next(first_sum)
    next(second_sum)
    first_pieces = next(first_sum)
    grad_above = moved(order.later(grad_below), -1, 0)
    up_total, down_total, proj_total = finish_middle(order, first_pieces, width, hidden_units)
    result_out = place(result_grid, result_above, result_left)
    qkv_pieces = next(second_sum)
    grad_left = edge_out(order.later(grad_above), grad_edge)
    grad_out = place(grad_grid, grad_above, grad_left)
    (qkv_total, *small) = finish(
        order, qkv_pieces, write_qkv, [struct((width, 3 * width), f32)],
        [struct((1, width), f32)] * 2 + [struct(vector.shape, f32) for vector in vectors[1:-1]] + [struct(bias_table.shape[::-1], f32)],
    )
    query_grad, value_grad, proj_sum, gain_one, shift_one, gain_two, shift_two, up_sum, down_sum = [
        vector[0] for vector in small[:-1]
    ]
    return (
        result_out, grad_out, qkv_total, query_grad, value_grad, small[-1].T, proj_total, proj_sum, gain_one, shift_one,
        gain_two, shift_two, up_total, up_sum, down_total, down_sum,
    )


def solution(mesh):
    grid = P("row", "col", None)
    return jax.shard_map(
        body,
        mesh=mesh,
        in_specs=(grid, P("row", "col")) + (P(),) * 14 + (grid,),
        out_specs=(grid, grid) + (P(),) * 14,
        check_vma=False,
    )
```

```python
import functools

import jax
import jax.numpy as jnp
from jax import lax
from jax.experimental import pallas as pl
from jax.experimental.pallas import tpu as pltpu
from jax.sharding import PartitionSpec as P

WIN = 10
SHIFT = 5
PLACES = WIN * WIN
PAD = 104
GROUP = 4
ROWS = GROUP * PAD
SLAB = 32
EDGE = 16
TILE = 128
TILES = 4

norm_eps = 1e-05
far_below = -1000000000.0
LOG2E = 1.4426950408889634
bf16 = jnp.bfloat16
f32 = jnp.float32


def dot(left, right, left_dim=1, right_dim=0):
    return lax.dot_general(
        left, right, (((left_dim,), (right_dim,)), ((), ())), preferred_element_type=f32
    )


def whole(array):
    count = len(array.shape)
    return pl.BlockSpec(array.shape, lambda *ids: (0,) * count)


SHORT = pl.CostEstimate(flops=1, bytes_accessed=1, transcendentals=0)


IN_VMEM = pl.BlockSpec(memory_space=pltpu.VMEM)


def params():
    return pltpu.CompilerParams(vmem_limit_bytes=60 * 2**20)


def norm_parts(values):
    center = values - jnp.mean(values, axis=-1, keepdims=True)
    rstd = lax.rsqrt(jnp.mean(center * center, axis=-1, keepdims=True) + norm_eps)
    return center * rstd, rstd


def norm_pull(grad, unit, rstd, gain):
    scaled = grad * gain
    return rstd * (
        scaled
        - jnp.mean(scaled, axis=-1, keepdims=True)
        - unit * jnp.mean(scaled * unit, axis=-1, keepdims=True)
    )


def head_masks():
    lane = lax.broadcasted_iota(jnp.int32, (1, 128), 1) // 32
    return [(lane == head).astype(f32).astype(bf16) for head in range(4)]


def spread_heads(tile):
    return jnp.concatenate([tile * mask for mask in head_masks()], axis=0)


def gather_heads(stacked):
    lane = lax.broadcasted_iota(jnp.int32, (PAD, 128), 1) // 32
    out = stacked[0:PAD]
    for head in range(1, 4):
        out = jnp.where(lane == head, stacked[PAD * head : PAD * (head + 1)], out)
    return out


def prepare_kernel(*refs):
    for rows, cols, rows_out, cols_out, corner_out in (refs[0:2] + refs[4:7], refs[2:4] + refs[7:10]):
        rows_out[...] = rows[...]
        cols_out[...] = cols[...]
        corner_out[...] = cols[0:SHIFT]


def window_rows(grids, local, col):
    count, wide, width = grids[0][0].shape
    first = col * WIN + SHIFT
    start = pl.multiple_of(jnp.minimum(first // 16 * 16, wide - SLAB), 16)
    half, side = count * SLAB, count * EDGE
    cols = pl.ds(start, SLAB)
    inside = lax.broadcasted_iota(jnp.int32, (1, SLAB, width), 1) + start < local
    place = lax.broadcasted_iota(jnp.int32, (PAD, 1), 0)
    prow = (place * 205) >> 11
    pcol = place - WIN * prow + first
    target = jnp.where(pcol < local, prow * SLAB + pcol - start, 2 * half + prow * EDGE + pcol - local)
    target = jnp.where(place < PLACES, target, -1)
    lane = lax.broadcasted_iota(jnp.int32, (PAD, 2 * (half + side)), 1)
    hot = (lane == target).astype(f32).astype(bf16)
    results = []
    for upper, lower, upper_right, lower_right in grids:
        slab = jnp.concatenate(
            (
                jnp.where(inside, upper[:, cols, :], 0).reshape(half, width),
                jnp.where(inside, lower[:, cols, :], 0).reshape(half, width),
                upper_right[...].reshape(side, width),
                lower_right[...].reshape(side, width),
            ),
            axis=0,
        )
        results.append(dot(hot, slab))
    return results


def halo_specs(block_row, last, local_cols, width):
    wide, below = -(-local_cols // 16) * 16, 0 if last else block_row + 1
    return [
        pl.BlockSpec((SHIFT, columns, width), lambda i, at=at: (at, 0, 0))
        for columns in (wide, EDGE)
        for at in (block_row, below)
    ]


def forward_kernel(local, first, *refs):
    sources, grad_sources, refs = refs[0:4], refs[4:8], refs[8:]
    (
        label_row, bias, qkv, qkv_bias, proj, proj_bias, gain_one, shift_one, *refs
    ) = refs
    if not first:
        refs = refs[7:]
    inputs, normed_one, joined, probs, mixed, middle, upstream, upstream_sum, *refs = refs
    part = pl.program_id(0)
    if first:
        qkv_low, proj_low, *refs = refs

        @pl.when(part == 0)
        def _():
            for tile in range(TILES):
                for kind in range(3):
                    lanes = 3 * TILE * tile + TILE * kind
                    source = qkv.shape[0] * kind + TILE * tile
                    qkv_low[:, lanes : lanes + TILE] = qkv[:, source : source + TILE].astype(bf16)
            proj_low[...] = proj[...].astype(bf16)

    else:
        qkv_low, proj_low = qkv, proj
    rows_s, joined_s, mixed_s = refs

    @pl.when(part == 0)
    def _():
        upstream_sum[...] = jnp.zeros_like(upstream_sum)

    for window in range(GROUP):
        at = slice(PAD * window, PAD * (window + 1))
        rows_s[at, :], mixed_s[at, :] = window_rows((sources, grad_sources), local, part * GROUP + window)
    upstream[...] = mixed_s[...].astype(bf16)
    upstream_sum[...] += column_sum(mixed_s[...])
    rows = rows_s[...]
    inputs[...] = rows.astype(bf16)
    unit, _ = norm_parts(rows)
    normed = (unit * gain_one[...] + shift_one[...]).astype(bf16)
    normed_one[...] = normed
    joined_s[...] = dot(normed, qkv_low[...]) + qkv_bias[...]

    def attend(window):
        at = pl.ds(pl.multiple_of(window * PAD, 8), PAD)
        joined[window] = joined_s[at, :].astype(bf16)
        labels = jnp.broadcast_to(label_row[window], (PAD, PAD))
        masked = jnp.where(labels.T == labels, 0.0, far_below)
        for tile in range(TILES):
            lanes = 3 * TILE * tile
            queries = joined_s[at, lanes : lanes + TILE].astype(bf16)
            keys = joined_s[at, lanes + TILE : lanes + 2 * TILE].astype(bf16)
            values = joined_s[at, lanes + 2 * TILE : lanes + 3 * TILE].astype(bf16).T
            raw = dot(spread_heads(keys), queries, 1, 1)
            outs = []
            for head in range(4):
                here = slice(PAD * head, PAD * (head + 1))
                scores = raw[here] * (LOG2E * 32**-0.5) + (bias[4 * tile + head] + masked)
                powers = jnp.exp2(scores - jnp.max(scores, axis=0, keepdims=True))
                total = jnp.sum(powers, axis=0, keepdims=True)
                probs_low = (powers * (1.0 / total)).astype(bf16)
                probs[window, tile, here, :] = probs_low
                outs.append(dot(values[32 * head : 32 * (head + 1)], probs_low))
            mixed_s[at, TILE * tile : TILE * (tile + 1)] = jnp.concatenate(outs, axis=0).T

    def attend_pair(pair, _):
        attend(2 * pair)
        attend(2 * pair + 1)
        return 0

    lax.fori_loop(0, GROUP // 2, attend_pair, 0)
    mixed_low = mixed_s[...].astype(bf16)
    mixed[...] = mixed_low
    middle[...] = rows_s[...] + dot(mixed_low, proj_low[...]) + proj_bias[...]


def column_sum(values):
    return jnp.sum(values, axis=0, keepdims=True)


def store_halves(core, last, total, start, keep, send):
    half = total.shape[0] // 2
    at = slice(start, start + half)

    @pl.when(last & (core == 0))
    def _():
        keep[at, :] = total[0:half, :]
        send[at, :] = total[half : 2 * half, :].astype(bf16)

    @pl.when(last & (core != 0))
    def _():
        keep[at, :] = total[half : 2 * half, :]
        send[at, :] = total[0:half, :].astype(bf16)


def store_mixed_halves(core, last, first, second, keep, send):
    sizes = [first.shape[0] // 8, second.shape[0] // 8]

    for side in range(2):

        @pl.when(last & (core == side))
        def _():
            start = 0
            for quarter in range(4):
                for total, size in ((first, sizes[0]), (second, sizes[1])):
                    mine = (4 * side + quarter) * size
                    other = (4 * (1 - side) + quarter) * size
                    keep[start : start + size, :] = total[mine : mine + size, :]
                    send[start : start + size, :] = total[other : other + size, :].astype(bf16)
                    start += size


def middle_kernel(
    core, upstream, middle, mixed, up_weight, up_bias, down_weight, down_bias, proj, gain, shift,
    out, below, edge, middle_grad_out, mixed_grad, keep, send, up_bias_grad, proj_sums, gain_grad, shift_grad,
    windows_s, mixed_grad_s, up, down, ff_grad, proj_grad,
):
    part = pl.program_id(1)
    step = pl.program_id(0) * pl.num_programs(1) + part

    @pl.when(step == 0)
    def _():
        up[...] = up_weight[...].astype(bf16)
        down[...] = down_weight[...].astype(bf16)
        for ref in (ff_grad, proj_grad, up_bias_grad, proj_sums, gain_grad, shift_grad):
            ref[...] = jnp.zeros_like(ref)

    unit, rstd = norm_parts(middle[...])
    normed = (unit * gain[...] + shift[...]).astype(bf16)
    given = upstream[...]
    result = middle[...] + down_bias[...]
    normed_grad = 0.0
    width, units = up.shape
    for start in range(0, units, width):
        at = slice(start, start + width)
        down_at = slice(units + start, units + start + width)
        hidden = dot(normed, up[:, at]) + up_bias[:, at]
        under = 0.5 + 0.5 * lax.erf(hidden * (2.0**-0.5))
        active_low = (hidden * under).astype(bf16)
        slope = under + hidden * (jnp.exp2(hidden * hidden * (-0.5 * LOG2E)) * 0.3989422804014327)
        grad_low = (slope * dot(given, down[at, :], 1, 1)).astype(bf16)
        up_bias_grad[:, at] += column_sum(grad_low.astype(f32))
        ff_grad[at, :] += dot(normed, grad_low, 0, 0)
        ff_grad[down_at, :] += dot(active_low, given, 0, 0)
        result += dot(active_low, down[at, :])
        normed_grad += dot(grad_low, up[:, at], 1, 1)
    store_windows(windows_s, result, part)
    gain_grad[...] += column_sum(normed_grad * unit)
    shift_grad[...] += column_sum(normed_grad)
    middle_grad = norm_pull(normed_grad, unit, rstd, gain[...]) + given.astype(f32)
    middle_grad_out[...] = middle_grad
    branch_low = middle_grad.astype(bf16)
    proj_sums[...] += column_sum(branch_low.astype(f32))
    proj_grad[...] += dot(mixed[...], branch_low, 0, 0)
    mixed_grad_s[...] = dot(branch_low, proj[...], 1, 1)
    for window in range(GROUP):
        mixed_grad[window] = mixed_grad_s[PAD * window : PAD * (window + 1)].astype(bf16)
    windows_to_grid(windows_s, out, below, edge)
    last = step == pl.num_programs(0) * pl.num_programs(1) - 1
    store_mixed_halves(core[0], last, ff_grad, proj_grad, keep, send)


def attention_pull_kernel(core, normed_one, joined, probs, mixed_grad, *refs):
    joined_grad, keep, send, sums, bias_grad, joined_s, qkv_grad, bias_s = refs[-8:]

    @pl.when(pl.program_id(0) == 0)
    def _():
        for ref in (qkv_grad, sums, bias_s):
            ref[...] = jnp.zeros_like(ref)

    for tile in range(probs.shape[1]):
        lanes = 3 * TILE * tile
        for window in range(GROUP):
            at = slice(PAD * window, PAD * (window + 1))
            queries = joined[window, :, lanes : lanes + TILE]
            keys = joined[window, :, lanes + TILE : lanes + 2 * TILE]
            values = joined[window, :, lanes + 2 * TILE : lanes + 3 * TILE]
            grad = mixed_grad[window, :, TILE * tile : TILE * (tile + 1)]
            probs_grad = dot(spread_heads(values), grad, 1, 1)
            probs_low = probs[window, tile]
            parts = []
            for head in range(4):
                here = slice(PAD * head, PAD * (head + 1))
                prob = probs_low[here].astype(f32)
                product = prob * probs_grad[here]
                score_grad = product - prob * column_sum(product)
                bias_s[window, 4 * tile + head] += score_grad
                parts.append((score_grad * 32**-0.5).astype(bf16))
            draw = jnp.concatenate(parts, axis=0)
            keys = keys.T
            outs = [dot(keys[32 * head : 32 * (head + 1)], parts[head]) for head in range(4)]
            joined_s[at, lanes : lanes + TILE] = jnp.concatenate(outs, axis=0).T
            joined_s[at, lanes + TILE : lanes + 2 * TILE] = gather_heads(dot(draw, queries))
            joined_s[at, lanes + 2 * TILE : lanes + 3 * TILE] = gather_heads(dot(probs_low, grad))
    joined_low = joined_s[...].astype(bf16)
    joined_grad[...] = joined_low
    sums[...] += column_sum(joined_low.astype(f32))
    qkv_grad[...] += dot(normed_one[...], joined_low, 0, 0)
    last = pl.program_id(0) == pl.num_programs(0) - 1

    @pl.when(last)
    def _():
        for head in range(bias_grad.shape[0]):
            bias_grad[head] = (bias_s[0, head] + bias_s[1, head]) + (bias_s[2, head] + bias_s[3, head])

    for tile in range(probs.shape[1]):
        columns = qkv_grad.at[:, 3 * TILE * tile : 3 * TILE * (tile + 1)]
        half = columns.shape[0] // 2
        store_halves(core[0], last, columns, half * tile, keep, send)


def windows_to_grid(windows, out, below, edge):
    count, _, width = windows.shape
    cols = count * WIN
    window_row, last_row = pl.program_id(0), pl.num_programs(0) - 1

    @pl.when(pl.program_id(1) == pl.num_programs(1) - 1)
    def _():
        spot = lax.broadcasted_iota(jnp.int32, (cols + EDGE, 1), 0)
        col = spot - SHIFT
        window = (col * 205) >> 11
        valid = (col >= 0) & (col < cols)
        lane = lax.broadcasted_iota(jnp.int32, (cols + EDGE, count * 16), 1)
        for row in range(WIN):
            start = WIN * row // 8 * 8
            offset = WIN * row - start
            slab = windows[:, start : start + 16, :].reshape(count * 16, width).astype(bf16)
            target = jnp.where(valid, col + (16 - WIN) * window + offset, -1)
            moved_rows = dot((lane == target).astype(f32).astype(bf16), slab)
            main, side = moved_rows[0:cols].astype(bf16), moved_rows[cols : cols + EDGE].astype(bf16)
            at = WIN * window_row + row + SHIFT
            if row < WIN - SHIFT:
                out[at] = main
                edge[at] = side
            else:

                @pl.when(window_row < last_row)
                def _():
                    out[at] = main
                    edge[at] = side

                @pl.when(window_row == last_row)
                def _():
                    below[row - (WIN - SHIFT)] = moved_rows.astype(bf16)


def place_kernel(given, above, left, out, rows_s, cols_s, semaphores):
    cols, count = rows_s.shape[1], cols_s.shape[0]
    edge = out.at[pl.ds(SHIFT, count), pl.ds(0, EDGE), :]
    fetch = pltpu.make_async_copy(edge, cols_s, semaphores.at[0])
    fetch.start()
    first = lax.broadcasted_iota(jnp.int32, (1, EDGE, 1), 1) < SHIFT
    rows_s[:, 0:EDGE, :] = jnp.where(first, left[0:SHIFT], above[:, 0:EDGE, :])
    rows_s[:, EDGE:cols, :] = above[:, EDGE:cols, :]
    rows = pltpu.make_async_copy(rows_s, out.at[pl.ds(0, SHIFT)], semaphores.at[1])
    rows.start()
    fetch.wait()
    cols_s[...] = jnp.where(first, left[SHIFT : SHIFT + count], cols_s[...])
    store = pltpu.make_async_copy(cols_s, edge, semaphores.at[2])
    store.start()
    rows.wait()
    store.wait()


def store_windows(windows_s, values, part):
    for window in range(GROUP):
        windows_s[part * GROUP + window] = values[PAD * window : PAD * (window + 1)]


def inputs_grad_kernel(
    joined_grad, inputs, middle_grad, qkv, gain, out, below, edge, gain_grad, shift_grad, windows_s
):
    part = pl.program_id(1)

    @pl.when((pl.program_id(0) == 0) & (part == 0))
    def _():
        gain_grad[...] = jnp.zeros_like(gain_grad)
        shift_grad[...] = jnp.zeros_like(shift_grad)

    normed_grad = dot(joined_grad[...], qkv[...], 1, 1)
    unit, rstd = norm_parts(inputs[...].astype(f32))
    gain_grad[...] += column_sum(normed_grad * unit)
    shift_grad[...] += column_sum(normed_grad)
    store_windows(windows_s, norm_pull(normed_grad, unit, rstd, gain[...]) + middle_grad[...], part)
    windows_to_grid(windows_s, out, below, edge)


def flipped(value, row_bits, col_bits):
    rows, cols = lax.axis_size("row"), lax.axis_size("col")
    pairs = [(r * cols + c, (r ^ row_bits) * cols + (c ^ col_bits)) for r in range(rows) for c in range(cols)]
    return lax.ppermute(value, ("row", "col"), pairs)


def block(ref, index, rows):
    return ref[pl.ds(pl.multiple_of(index * rows, 8), rows), :]


def split_kernel(place, kept, got, *outs):
    total = kept[...] + got[...].astype(f32)
    for other in range(4):

        @pl.when(pl.program_id(0) == other)
        def _():
            outs[other][...] = total.astype(outs[other].dtype)


def split_again_kernel(place, kept, first, second, third, *refs):
    outs, total = refs[:-1], refs[-1]
    total[...] = kept[...] + first[...].astype(f32) + second[...].astype(f32) + third[...].astype(f32)
    rows = outs[0].shape[0]
    outs[0][...] = block(total, place[0], rows)
    for other in range(1, 4):
        outs[other][...] = block(total, place[0] ^ other, rows).astype(bf16)


def add_kernel(kept, first, second, third, *refs):
    out, rows = refs[-1], kept.shape[0]
    total = kept[...] + first[...].astype(f32) + second[...].astype(f32) + third[...].astype(f32)
    out[0:rows, :] = total.astype(out.dtype)


def pack_rows(vectors):
    columns, spots, at = 3 * TILE, [], 0
    for index, vector in enumerate(vectors):
        if vector.shape[0] > 1:
            at = -(-at // 8) * 8
            spots.append((index, None, 0, at, columns))
            at += vector.shape[0]
            continue
        for start in range(0, vector.shape[1], columns):
            spots.append((index, 0, start, at, min(columns, vector.shape[1] - start)))
            at += 1
    return spots, -(-at // 8) * 8


def pack(vectors, packed):
    packed[...] = jnp.zeros_like(packed)
    for index, row, start, at, size in pack_rows(vectors)[0]:
        if row is None:
            packed[at : at + vectors[index].shape[0], :] = vectors[index][...]
        else:
            packed[at : at + 1, 0:size] = vectors[index][:, start : start + size]


def pack_kernel(*refs):
    pack(refs[:-1], refs[-1])


def add_and_pack_kernel(kept, first, second, third, *refs):
    *vectors, out, packed = refs
    add_kernel(kept, first, second, third, out)
    pack(vectors, packed)
    store_pair(out, kept.shape[0], packed[...])


def store_pair(out, start, values):
    size = values.shape[0]
    high = values.astype(bf16)
    out[start : start + size, :] = high
    out[start + size : start + 2 * size, :] = (values - high.astype(f32)).astype(bf16)


def pair_sum(refs, start, size):
    total = 0.0
    for ref in refs:
        total += ref[start : start + size, :].astype(f32) + ref[start + size : start + 2 * size, :].astype(f32)
    return total


def join_kernel(place, *refs):
    pieces, out, joined_s = refs[:4], refs[4], refs[5]
    rows = joined_s.shape[0] // 4
    for other in range(4):
        at = pl.ds(pl.multiple_of((place[0] ^ other) * rows, 8), rows)
        joined_s[at, :] = pieces[other][0:rows, :].astype(f32)
    out[0 : 4 * rows, :] = joined_s[...].astype(bf16)
    extra = (pieces[0].shape[0] - rows) // 2
    if extra:
        store_pair(out, 4 * rows, pair_sum(pieces, rows, extra))


def scalar_call(kernel, scalar, *operands, outs, scratch=()):
    return pl.pallas_call(
        kernel,
        grid_spec=pltpu.PrefetchScalarGridSpec(
            num_scalar_prefetch=1,
            grid=(1,),
            in_specs=[IN_VMEM] * len(operands),
            out_specs=[IN_VMEM] * len(outs),
            scratch_shapes=list(scratch),
        ),
        out_shape=list(outs),
        compiler_params=params(),
            cost_estimate=SHORT,
    )(scalar, *operands)


def struct(shape, dtype):
    return jax.ShapeDtypeStruct(shape, dtype)


def places():
    row, col = lax.axis_index("row"), lax.axis_index("col")
    one = lambda value: jnp.reshape(value, (1,)).astype(jnp.int32)
    return one(col & 1), one(((col >> 1) & 1) | ((row & 1) << 1)), one((row >> 1) & 3)


class Order:
    def __init__(self):
        self.last = []

    def __call__(self, call, *operands):
        if self.last:
            operands, _ = lax.optimization_barrier((operands, self.last))
        results = call(*operands)
        self.last = [jax.tree.leaves(results)[0]]
        return results

    def later(self, value):
        return lax.optimization_barrier((value, self.last))[0]

    def hold(self, *values):
        self.last.extend(values)


def sum_over_devices(order, kept, sent, small_vectors=None):
    _, plane, depth = places()
    plane_flips = ((0, 2), (1, 0), (1, 2))
    depth_flips = ((2, 0), (4, 0), (6, 0))
    got = flipped(sent, 0, 1)
    rows, width = kept.shape
    quarter, small = rows // 4, rows // 16
    yield
    outs = [struct((quarter, width), f32)] + [struct((quarter, width), bf16)] * 3

    def split(*operands):
        block = pl.BlockSpec((quarter, width), lambda i, s: (s[0] ^ i, 0))
        return pl.pallas_call(
            split_kernel,
            grid_spec=pltpu.PrefetchScalarGridSpec(
                num_scalar_prefetch=1,
                grid=(4,),
                in_specs=[block] * 2,
                out_specs=[pl.BlockSpec((quarter, width), lambda i, s: (0, 0), pipeline_mode=pl.Buffered(1))] * 4,
            ),
            out_shape=outs,
            compiler_params=params(),
            cost_estimate=SHORT,
        )(plane, *operands)

    own, *sends = order(split, kept, got)
    got = [flipped(piece, *flip) for piece, flip in zip(sends, plane_flips)]
    yield
    outs = [struct((small, width), f32)] + [struct((small, width), bf16)] * 3
    call = functools.partial(
        scalar_call, split_again_kernel, depth, outs=outs, scratch=[pltpu.VMEM((quarter, width), f32)]
    )
    own, *sends = order(call, own, *got)
    got = [flipped(piece, *flip) for piece, flip in zip(sends, depth_flips)]
    yield got
    vectors = [] if small_vectors is None else small_vectors()
    packed_rows = pack_rows(vectors)[1]
    ride = 2 * packed_rows
    further = []
    bit = 8
    while bit < lax.axis_size("row"):
        further.append(bit)
        bit *= 2
    if further:
        call = pl.pallas_call(add_kernel, out_shape=struct((small, width), f32), cost_estimate=SHORT)
        done = order(call, own, *got)
        extra = []
        if vectors:
            extra = [pl.pallas_call(pack_kernel, out_shape=struct((packed_rows, width), f32))(*vectors)]
        for bit in further:
            done = done + flipped(done.astype(bf16), bit, 0).astype(f32)
            extra = [value + flipped(value, bit, 0) for value in extra]
        done = done.astype(bf16)
        for value in extra:
            high = lax.reduce_precision(value, 8, 7)
            done = jnp.concatenate((done, high.astype(bf16), (value - high).astype(bf16)))
    else:
        call = pl.pallas_call(
            add_and_pack_kernel if vectors else add_kernel,
            out_shape=struct((small + ride, width), bf16),
            in_specs=[IN_VMEM] * (4 + len(vectors)),
            out_specs=IN_VMEM,
            scratch_shapes=[pltpu.VMEM((packed_rows, width), f32)] if vectors else [],
            cost_estimate=SHORT,
        )
        done = order(call, own, *got, *vectors)
    pieces = [done] + [flipped(done, *flip) for flip in depth_flips]
    yield pieces
    call = functools.partial(
        scalar_call, join_kernel, depth, outs=[struct((quarter + ride, width), bf16)],
        scratch=[pltpu.VMEM((quarter, width), f32)],
    )
    (mine,) = order(call, *pieces)
    if vectors:
        mine = [mine] + [flipped(mine, *flip) for flip in plane_flips]
    else:
        mine = [mine] + [flipped(mine, *flip) for flip in plane_flips[:2]]
        yield mine
        mine.append(flipped(order.later(mine[1]), *plane_flips[1]))
    yield mine
    pieces = mine + [flipped(piece if vectors else order.later(piece), 0, 1) for piece in mine]
    yield pieces


def finish_kernel(write, plane, core, *refs):
    pieces, out, small_outs, (total, packed) = refs[:8], refs[8], refs[9:-2], refs[-2:]
    rows = total.shape[1] // 4
    for other in range(4):
        at = pl.ds(pl.multiple_of((plane[0] ^ other) * rows, 8), rows)
        total[core[0], at, :] = pieces[other][0:rows, :].astype(f32)
        total[1 - core[0], at, :] = pieces[4 + other][0:rows, :].astype(f32)
    write(total, out)
    packed[...] = pair_sum(pieces, rows, packed.shape[0])
    query_out, value_out, *vector_outs, table_out = small_outs
    for tile in range(TILES):
        at = slice(TILE * tile, TILE * (tile + 1))
        query_out[:, at] = packed[tile : tile + 1, 0:TILE]
        value_out[:, at] = packed[tile : tile + 1, 2 * TILE : 3 * TILE]
    table_rows = struct((table_out.shape[0], 3 * TILE), f32)
    spots, _ = pack_rows([struct((1, 3 * TILE * TILES), f32), *vector_outs, table_rows])
    for index, row, start, at, size in spots:
        if row is None:
            table_out[...] = packed[at : at + table_rows.shape[0], 0 : table_out.shape[1]]
        elif index > 0:
            vector_outs[index - 1][:, start : start + size] = packed[at : at + 1, 0:size]


def finish(order, pieces, write, outs, small_outs):
    core, plane, _ = places()
    rows, width = pieces[0].shape
    table = struct((small_outs[-1].shape[0], width), f32)
    packed_rows = pack_rows([struct((1, width * TILES), f32), *small_outs[2:-1], table])[1]
    outs = outs + small_outs

    def call(*operands):
        return pl.pallas_call(
            functools.partial(finish_kernel, write),
            grid_spec=pltpu.PrefetchScalarGridSpec(
                num_scalar_prefetch=2,
                grid=(1,),
                in_specs=[IN_VMEM] * len(pieces),
                out_specs=[pl.BlockSpec(a.shape, lambda i, s, t: (0, 0)) for a in outs],
                scratch_shapes=[
                    pltpu.VMEM((2, 4 * (rows - 2 * packed_rows), width), f32), pltpu.VMEM((packed_rows, width), f32),
                ],
            ),
            out_shape=outs,
            compiler_params=params(),
            cost_estimate=SHORT,
        )(plane, core, *operands)

    return order(call, *pieces)


def finish_middle_kernel(plane, core, *refs):
    pieces, (up_out, down_out, proj_out) = refs[:8], refs[8:]
    size = up_out.shape[1]
    rest = pieces[0].shape[0] - size
    for other in range(4):
        for side in range(2):

            @pl.when((pl.program_id(0) == other) & (core[0] == side))
            def _():
                ups, downs = pieces[other + 4 * side], pieces[other + 4 * (1 - side)]
                up_out[...] = ups[0:size, :].astype(f32)
                down_out[...] = downs[0:size, :].astype(f32)
                at = pl.multiple_of((plane[0] ^ other) * rest, 8)
                proj_out[pl.ds(at, rest), :] = ups[size:, :].astype(f32)
                proj_out[pl.ds(at + 4 * rest, rest), :] = downs[size:, :].astype(f32)


def finish_middle(order, pieces, width, units):
    core, plane, _ = places()

    def call(*operands):
        return pl.pallas_call(
            finish_middle_kernel,
            grid_spec=pltpu.PrefetchScalarGridSpec(
                num_scalar_prefetch=2,
                grid=(4,),
                in_specs=[pl.BlockSpec(a.shape, lambda i, s, t: (0, 0), pipeline_mode=pl.Buffered(1)) for a in pieces],
                out_specs=[
                    pl.BlockSpec((width, units // 4), lambda i, s, t: (0, s[0] ^ i)),
                    pl.BlockSpec((units // 4, width), lambda i, s, t: (s[0] ^ i, 0)),
                    pl.BlockSpec((width, width), lambda i, s, t: (0, 0)),
                ],
            ),
            out_shape=[struct((width, units), f32), struct((units, width), f32), struct((width, width), f32)],
            compiler_params=params(),
            cost_estimate=SHORT,
        )(plane, core, *operands)

    return order(call, *pieces)


def moved(value, row_step, col_step):
    rows, cols = lax.axis_size("row"), lax.axis_size("col")
    pairs = [
        (r * cols + c, ((r - row_step) % rows) * cols + (c - col_step) % cols) for r in range(rows) for c in range(cols)
    ]
    return lax.ppermute(value, ("row", "col"), pairs)


def relative_index():
    spots = jnp.arange(PLACES, dtype=jnp.int32)
    prow, pcol = spots // WIN, spots % WIN
    return (prow[None, :] - prow[:, None] + WIN - 1) * (2 * WIN - 1) + (pcol[None, :] - pcol[:, None] + WIN - 1)


def by_tile(array):
    return array.reshape(3, TILES, TILE).swapaxes(0, 1).reshape(1, 3 * TILES * TILE)


def thirds(values):
    terms = []
    for _ in range(3):
        term = lax.reduce_precision(values, 8, 7)
        terms.append(term.astype(bf16))
        values = values - term
    return jnp.concatenate(terms)


def exact_dot(values, onehot, dim):
    product = lax.dot_general(thirds(values), onehot, (((1,), (dim,)), ((), ())), preferred_element_type=f32)
    first, second, third = jnp.split(product, 3)
    return first + (second + third)


def body(
    patches, region_ids, qkv_weight, query_bias, value_bias, bias_table, proj_weight, proj_bias, gain_one, shift_one,
    gain_two, shift_two, up_weight, up_bias, down_weight, down_bias, cotangent,
):
    local_rows, local_cols, width = patches.shape
    heads = bias_table.shape[1]
    hidden_units = up_weight.shape[1]
    wrows, wcols = local_rows // WIN, local_cols // WIN
    windows = wrows * wcols
    tokens = windows * PAD
    steps = wcols // GROUP
    wide = -(-local_cols // 16) * 16
    row = lambda vector: vector[None]
    core, _, _ = places()
    order = Order()

    def prepare(first, second):
        rows_block = pl.BlockSpec((SHIFT, local_cols, width), lambda i: (0, 0, 0))
        cols_block = pl.BlockSpec((local_rows, EDGE, width), lambda i: (0, 0, 0))
        corner_block = pl.BlockSpec((SHIFT, EDGE, width), lambda i: (0, 0, 0))
        return pl.pallas_call(
            prepare_kernel,
            grid=(1,),
            in_specs=[rows_block, cols_block] * 2,
            out_specs=[rows_block, cols_block, corner_block] * 2,
            out_shape=[
                struct((SHIFT, local_cols, width), bf16), struct((local_rows, EDGE, width), bf16),
                struct((SHIFT, EDGE, width), bf16),
            ] * 2,
            compiler_params=params(),
            cost_estimate=SHORT,
        )(first, first, second, second)

    edges = order(prepare, patches, cotangent)
    right, right_grad = moved(edges[1], 0, 1), moved(edges[4], 0, 1)
    below, across = moved(edges[0], 1, 0), moved(edges[2], 1, 1)
    below_grad, across_grad = moved(edges[3], 1, 0), moved(edges[5], 1, 1)
    labels = region_ids.reshape(wrows, WIN, wcols, WIN).transpose(0, 2, 1, 3).reshape(windows, PLACES)
    labels = jnp.pad(labels, ((0, 0), (0, PAD - PLACES)), constant_values=-1)
    entries = -(-bias_table.shape[0] // TILE) * TILE
    onehot = (relative_index().reshape(-1)[:, None] == jnp.arange(entries, dtype=jnp.int32)[None, :]).astype(bf16)
    table = jnp.pad(bias_table.T, ((0, 0), (0, entries - bias_table.shape[0])))
    position_bias = exact_dot(table, onehot, 1).reshape(heads, PLACES, PLACES) * LOG2E
    position_bias = jnp.pad(position_bias, ((0, 0), (0, 0), (0, PAD - PLACES)))
    position_bias = jnp.pad(position_bias, ((0, 0), (0, PAD - PLACES), (0, 0)), constant_values=far_below)
    qkv_bias = by_tile(jnp.concatenate((query_bias, jnp.zeros_like(query_bias), value_bias)))

    token_arrays = [
        struct((tokens, width), bf16), struct((tokens, width), bf16), struct((windows, PAD, 3 * width), bf16),
        struct((windows, TILES, 4 * PAD, PAD), bf16), struct((tokens, width), bf16), struct((tokens, width), f32),
        struct((tokens, width), bf16),
    ]
    made, upstream_sums = [], []
    qkv_low, proj_low = qkv_weight, proj_weight
    labels = labels[:, None, :].astype(f32)
    for index in range(wrows):
        first, last = index == 0, index == wrows - 1
        block_of = lambda array: pl.BlockSpec(
            (array.shape[0] // (wrows * steps),) + array.shape[1:],
            lambda i, n=len(array.shape), index=index: (index * steps + i,) + (0,) * (n - 1),
        )
        specs = halo_specs(2 * index + 1, last, local_cols, width)
        operands = (
            position_bias, qkv_low, qkv_bias, proj_low, row(proj_bias), row(gain_one), row(shift_one),
        )
        lows = [struct(qkv_weight.shape, bf16), struct(proj_weight.shape, bf16)] if first else []
        call = pl.pallas_call(
            functools.partial(forward_kernel, local_cols, first),
            grid=(steps,),
            in_specs=specs * 2 + [block_of(labels)] + [whole(a) for a in operands]
            + [pl.BlockSpec(memory_space=pl.ANY)] * len(made),
            out_specs=[block_of(a) for a in token_arrays]
            + [pl.BlockSpec((1, width), lambda i: (0, 0))] + [whole(a) for a in lows],
            out_shape=token_arrays + [struct((1, width), f32)] + lows,
            input_output_aliases={16 + i: i for i in range(len(made))},
            scratch_shapes=[
                pltpu.VMEM((ROWS, width), f32), pltpu.VMEM((ROWS, 3 * width), f32), pltpu.VMEM((ROWS, width), f32),
            ],
            compiler_params=params(),
            cost_estimate=SHORT,
        )
        around = (patches, below if last else patches, right, across if last else right)
        around_grad = (cotangent, below_grad if last else cotangent, right_grad, across_grad if last else right_grad)
        outs = order(call, *around, *around_grad, labels, *operands, *made)
        made, total = outs[: len(token_arrays)], outs[len(token_arrays)]
        if first:
            qkv_low, proj_low = outs[-2:]
        upstream_sums.append(total)
    inputs, normed_one, joined, probs, mixed, middle, upstream = made
    down_bias_grad = sum(upstream_sums)
    rows_of = lambda columns: pl.BlockSpec((ROWS, columns), lambda i, *_: (i, 0))
    win_of = lambda *shape: pl.BlockSpec((GROUP,) + shape, lambda i, *_: (i,) + (0,) * len(shape))
    fixed = lambda array: pl.BlockSpec(array.shape, lambda i, *_: (0,) * len(array.shape))

    def core_call(kernel, in_specs, out_specs, out_shape, scratch, aliases):
        return pl.pallas_call(
            kernel,
            grid_spec=pltpu.PrefetchScalarGridSpec(
                num_scalar_prefetch=1,
                grid=(tokens // ROWS,),
                in_specs=in_specs,
                out_specs=out_specs,
                scratch_shapes=scratch,
            ),
            out_shape=out_shape,
            input_output_aliases=aliases,
            compiler_params=params(),
            cost_estimate=SHORT,
        )

    def attention_pull(tile, count, *made):
        rows, columns, at = width // 2 * count, 3 * TILE * count, tile // count
        outs = [
            struct((tokens, 3 * width), bf16), struct((width // 2 * TILES, 3 * TILE), f32),
            struct((width // 2 * TILES, 3 * TILE), bf16), struct((1, 3 * width), f32), struct((heads, PAD, PAD), f32),
        ]
        part = heads // TILES * count
        call = core_call(
            attention_pull_kernel,
            [
                rows_of(width),
                pl.BlockSpec((GROUP, PAD, columns), lambda i, s: (i, 0, at)),
                pl.BlockSpec((GROUP, count, 4 * PAD, PAD), lambda i, s: (i, at, 0, 0)),
                pl.BlockSpec((GROUP, PAD, TILE * count), lambda i, s: (i, 0, at)),
            ]
            + [pl.BlockSpec(memory_space=pl.ANY)] * len(made),
            [
                pl.BlockSpec((ROWS, columns), lambda i, s: (i, at)),
                pl.BlockSpec((rows, 3 * TILE), lambda i, s: (at, 0)),
                pl.BlockSpec((rows, 3 * TILE), lambda i, s: (at, 0)),
                pl.BlockSpec((1, columns), lambda i, s: (0, at)),
                pl.BlockSpec((part, PAD, PAD), lambda i, s: (at, 0, 0)),
            ],
            outs,
            [
                pltpu.VMEM((ROWS, columns), f32), pltpu.VMEM((width, columns), f32),
                pltpu.VMEM((GROUP, part, PAD, PAD), f32),
            ],
            {5 + i: i for i in range(len(made))},
        )
        return order(call, core, normed_one, joined, probs, mixed_grad, *made)

    def write_qkv(total, out):
        rows = width // 2
        for side in range(2):
            for tile in range(TILES):
                for kind in range(3):
                    at = width * kind + TILE * tile
                    out[rows * side : rows * (side + 1), at : at + TILE] = (
                        total[side, rows * tile : rows * (tile + 1), TILE * kind : TILE * (kind + 1)]
                    )

    token_spec = lambda columns: pl.BlockSpec((ROWS, columns), lambda i, j, *_: (i * steps + j, 0))
    single = lambda array: pl.BlockSpec(
        array.shape, lambda *ids, n=len(array.shape): (0,) * n, pipeline_mode=pl.Buffered(1)
    )
    constant = lambda array: pl.BlockSpec(array.shape, lambda *ids, n=len(array.shape): (0,) * n)
    grid_outs = [
        struct((local_rows, local_cols, width), bf16), struct((SHIFT, local_cols + EDGE, width), bf16),
        struct((local_rows, EDGE, width), bf16),
    ]
    vector = struct((1, width), f32)

    def edge_out(above, edge):
        return moved(jnp.concatenate((above[:, local_cols:], edge[SHIFT:])), 0, -1)

    def place(grid, above, left):
        return order(
            pl.pallas_call(
                place_kernel,
                in_specs=[pl.BlockSpec(memory_space=pl.ANY), IN_VMEM, IN_VMEM],
                out_specs=pl.BlockSpec(memory_space=pl.ANY),
                out_shape=struct(grid.shape, grid.dtype),
                input_output_aliases={0: 0},
                scratch_shapes=[
                    pltpu.VMEM((SHIFT, local_cols, width), bf16), pltpu.VMEM((local_rows - SHIFT, EDGE, width), bf16),
                    pltpu.SemaphoreType.DMA((3,)),
                ],
                compiler_params=params(),
                cost_estimate=SHORT,
            ),
            grid, above, left,
        )

    shared = hidden_units + width // 2
    outs = [
        struct((shared, width), f32), struct((shared, width), bf16), struct((1, hidden_units), f32), vector, vector,
        vector,
    ]
    call = pl.pallas_call(
        middle_kernel,
        grid_spec=pltpu.PrefetchScalarGridSpec(
            num_scalar_prefetch=1,
            grid=(wrows, steps),
            in_specs=[token_spec(width)] * 3
            + [single(up_weight), single(row(up_bias)), single(down_weight)]
            + [single(a) for a in (row(down_bias), proj_low, row(gain_two), row(shift_two))],
            out_specs=[single(a) for a in grid_outs]
            + [token_spec(width), pl.BlockSpec((GROUP, PAD, width), lambda i, j, s: (i * steps + j, 0, 0))]
            + [single(a) for a in outs],
            scratch_shapes=[
                pltpu.VMEM((wcols, PAD, width), f32), pltpu.VMEM((ROWS, width), f32), pltpu.VMEM(up_weight.shape, bf16),
                pltpu.VMEM(down_weight.shape, bf16), pltpu.VMEM((2 * hidden_units, width), f32),
                pltpu.VMEM((width, width), f32),
            ],
        ),
        out_shape=grid_outs + [struct((tokens, width), f32), struct((windows, PAD, width), bf16)] + outs,
        compiler_params=params(),
            cost_estimate=SHORT,
    )
    (
        result_grid, result_below, result_edge, middle_grad, mixed_grad, kept, sent, up_bias_grad, proj_sums, gain_two_grad, shift_two_grad,
    ) = order(
        call, core, upstream, middle, mixed, up_weight, row(up_bias), down_weight, row(down_bias), proj_low,
        row(gain_two), row(shift_two),
    )
    result_above = moved(result_below, -1, 0)
    first_sum = sum_over_devices(order, kept, sent)
    next(first_sum)
    next(first_sum)
    tiles = attention_pull(0, 3)
    order.hold(result_above)
    in_flight = next(first_sum)
    result_left = edge_out(order.later(result_above), result_edge)
    joined_grad, qkv_kept, qkv_sent, qkv_sums, bias_grad = attention_pull(3, 1, *tiles)
    qkv_sent, _ = lax.optimization_barrier((qkv_sent, in_flight))
    second_sum = sum_over_devices(order, qkv_kept, qkv_sent, lambda: vectors)
    next(second_sum)
    next(first_sum)
    next(second_sum)
    call = pl.pallas_call(
        inputs_grad_kernel,
        grid=(wrows, steps),
        in_specs=[token_spec(3 * width)] + [token_spec(width)] * 2 + [single(qkv_low), single(row(gain_one))],
        out_specs=[single(a) for a in grid_outs] + [single(vector)] * 2,
        out_shape=grid_outs + [vector] * 2,
        scratch_shapes=[pltpu.VMEM((wcols, PAD, width), f32)],
        compiler_params=params(),
            cost_estimate=SHORT,
    )
    grad_grid, grad_below, grad_edge, gain_one_grad, shift_one_grad = order(
        call, joined_grad, inputs, middle_grad, qkv_low, row(gain_one)
    )
    ff_pieces = next(first_sum)
    order.hold(result_left)
    next(second_sum)
    terms = order.later(bias_grad)[:, :PLACES, :PLACES].reshape(heads, -1)
    table_grad = exact_dot(terms, onehot, 0)
    vectors = [
        qkv_sums, proj_sums, gain_one_grad, shift_one_grad, gain_two_grad, shift_two_grad, up_bias_grad, down_bias_grad,
        table_grad,
    ]
    next(second_sum)
    order.hold(ff_pieces[1])
    ff_pieces = next(first_sum)
    next(second_sum)
    first_pieces = next(first_sum)
    grad_above = moved(order.later(grad_below), -1, 0)
    up_total, down_total, proj_total = finish_middle(order, first_pieces, width, hidden_units)
    result_out = place(result_grid, result_above, result_left)
    qkv_pieces = next(second_sum)
    grad_left = edge_out(order.later(grad_above), grad_edge)
    grad_out = place(grad_grid, grad_above, grad_left)
    (qkv_total, *small) = finish(
        order, qkv_pieces, write_qkv, [struct((width, 3 * width), f32)],
        [struct((1, width), f32)] * 2 + [struct(vector.shape, f32) for vector in vectors[1:-1]] + [struct(bias_table.shape[::-1], f32)],
    )
    query_grad, value_grad, proj_sum, gain_one, shift_one, gain_two, shift_two, up_sum, down_sum = [
        vector[0] for vector in small[:-1]
    ]
    return (
        result_out, grad_out, qkv_total, query_grad, value_grad, small[-1].T, proj_total, proj_sum, gain_one, shift_one,
        gain_two, shift_two, up_total, up_sum, down_total, down_sum,
    )


def solution(mesh):
    grid = P("row", "col", None)
    return jax.shard_map(
        body,
        mesh=mesh,
        in_specs=(grid, P("row", "col")) + (P(),) * 14 + (grid,),
        out_specs=(grid, grid) + (P(),) * 14,
        check_vma=False,
    )
```

```python
import functools

import jax
import jax.numpy as jnp
from jax import lax
from jax.experimental import pallas as pl
from jax.experimental.pallas import tpu as pltpu
from jax.sharding import PartitionSpec as P

WIN = 10
SHIFT = 5
PLACES = WIN * WIN
PAD = 104
GROUP = 4
ROWS = GROUP * PAD
SLAB = 32
EDGE = 16
TILE = 128
TILES = 4

norm_eps = 1e-05
far_below = -1000000000.0
LOG2E = 1.4426950408889634
bf16 = jnp.bfloat16
f32 = jnp.float32


def dot(left, right, left_dim=1, right_dim=0):
    return lax.dot_general(
        left, right, (((left_dim,), (right_dim,)), ((), ())), preferred_element_type=f32
    )


def whole(array):
    count = len(array.shape)
    return pl.BlockSpec(array.shape, lambda *ids: (0,) * count)


SHORT = pl.CostEstimate(flops=1, bytes_accessed=1, transcendentals=0)


IN_VMEM = pl.BlockSpec(memory_space=pltpu.VMEM)


def params():
    return pltpu.CompilerParams(vmem_limit_bytes=60 * 2**20)


def norm_parts(values):
    center = values - jnp.mean(values, axis=-1, keepdims=True)
    rstd = lax.rsqrt(jnp.mean(center * center, axis=-1, keepdims=True) + norm_eps)
    return center * rstd, rstd


def norm_pull(grad, unit, rstd, gain):
    scaled = grad * gain
    return rstd * (
        scaled
        - jnp.mean(scaled, axis=-1, keepdims=True)
        - unit * jnp.mean(scaled * unit, axis=-1, keepdims=True)
    )


def head_masks():
    lane = lax.broadcasted_iota(jnp.int32, (1, 128), 1) // 32
    return [(lane == head).astype(f32).astype(bf16) for head in range(4)]


def spread_heads(tile):
    return jnp.concatenate([tile * mask for mask in head_masks()], axis=0)


def gather_heads(stacked):
    lane = lax.broadcasted_iota(jnp.int32, (PAD, 128), 1) // 32
    out = stacked[0:PAD]
    for head in range(1, 4):
        out = jnp.where(lane == head, stacked[PAD * head : PAD * (head + 1)], out)
    return out


def prepare_kernel(*refs):
    rows_out, cols_out, corner_out = refs[4:]
    for index in range(2):
        rows, cols = refs[2 * index : 2 * index + 2]
        rows_out[index] = rows[...]
        cols_out[index] = cols[...]
        corner_out[index] = cols[0:SHIFT]


def window_rows(grids, local, col):
    count, wide, width = grids[0][0].shape
    first = col * WIN + SHIFT
    start = pl.multiple_of(jnp.minimum(first // 16 * 16, wide - SLAB), 16)
    half, side = count * SLAB, count * EDGE
    cols = pl.ds(start, SLAB)
    inside = lax.broadcasted_iota(jnp.int32, (1, SLAB, width), 1) + start < local
    place = lax.broadcasted_iota(jnp.int32, (PAD, 1), 0)
    prow = (place * 205) >> 11
    pcol = place - WIN * prow + first
    target = jnp.where(pcol < local, prow * SLAB + pcol - start, 2 * half + prow * EDGE + pcol - local)
    target = jnp.where(place < PLACES, target, -1)
    lane = lax.broadcasted_iota(jnp.int32, (PAD, 2 * (half + side)), 1)
    hot = (lane == target).astype(f32).astype(bf16)
    results = []
    for upper, lower, upper_right, lower_right in grids:
        slab = jnp.concatenate(
            (
                jnp.where(inside, upper[:, cols, :], 0).reshape(half, width),
                jnp.where(inside, lower[:, cols, :], 0).reshape(half, width),
                upper_right[...].reshape(side, width),
                lower_right[...].reshape(side, width),
            ),
            axis=0,
        )
        results.append(dot(hot, slab))
    return results


def halo_specs(block_row, last, local_cols, width, index):
    wide = -(-local_cols // 16) * 16
    own = lambda at: pl.BlockSpec((SHIFT, wide, width), lambda i: (at, 0, 0))
    came = lambda columns, at: pl.BlockSpec((None, SHIFT, columns, width), lambda i: (index, at, 0, 0))
    return [
        own(block_row),
        came(wide, 0) if last else own(block_row + 1),
        came(EDGE, block_row),
        came(EDGE, 0 if last else block_row + 1),
    ]


def forward_kernel(local, first, *refs):
    sources, grad_sources, refs = refs[0:4], refs[4:8], refs[8:]
    (
        label_row, bias, qkv, qkv_bias, proj, proj_bias, gain_one, shift_one, *refs
    ) = refs
    if not first:
        refs = refs[7:]
    inputs, normed_one, joined, probs, mixed, middle, upstream, upstream_sum, *refs = refs
    part = pl.program_id(0)
    if first:
        qkv_low, proj_low, *refs = refs

        @pl.when(part == 0)
        def _():
            for tile in range(TILES):
                for kind in range(3):
                    lanes = 3 * TILE * tile + TILE * kind
                    source = qkv.shape[0] * kind + TILE * tile
                    qkv_low[:, lanes : lanes + TILE] = qkv[:, source : source + TILE].astype(bf16)
            proj_low[...] = proj[...].astype(bf16)

    else:
        qkv_low, proj_low = qkv, proj
    rows_s, joined_s, mixed_s = refs

    @pl.when(part == 0)
    def _():
        upstream_sum[...] = jnp.zeros_like(upstream_sum)

    for window in range(GROUP):
        at = slice(PAD * window, PAD * (window + 1))
        rows_s[at, :], mixed_s[at, :] = window_rows((sources, grad_sources), local, part * GROUP + window)
    upstream[...] = mixed_s[...].astype(bf16)
    upstream_sum[...] += column_sum(mixed_s[...])
    rows = rows_s[...]
    inputs[...] = rows.astype(bf16)
    unit, _ = norm_parts(rows)
    normed = (unit * gain_one[...] + shift_one[...]).astype(bf16)
    normed_one[...] = normed
    joined_s[...] = dot(normed, qkv_low[...]) + qkv_bias[...]

    for window in range(GROUP):
        at = slice(PAD * window, PAD * (window + 1))
        joined[window] = joined_s[at, :].astype(bf16)
        labels = jnp.broadcast_to(label_row[window], (PAD, PAD))
        masked = jnp.where(labels.T == labels, 0.0, far_below)
        for tile in range(TILES):
            lanes = 3 * TILE * tile
            queries = joined_s[at, lanes : lanes + TILE].astype(bf16)
            keys = joined_s[at, lanes + TILE : lanes + 2 * TILE].astype(bf16)
            values = joined_s[at, lanes + 2 * TILE : lanes + 3 * TILE].astype(bf16).T
            raw = dot(spread_heads(keys), queries, 1, 1)
            outs = []
            for head in range(4):
                here = slice(PAD * head, PAD * (head + 1))
                scores = raw[here] * (LOG2E * 32**-0.5) + (bias[4 * tile + head] + masked)
                powers = jnp.exp2(scores - jnp.max(scores, axis=0, keepdims=True))
                total = jnp.sum(powers, axis=0, keepdims=True)
                probs_low = (powers * (1.0 / total)).astype(bf16)
                probs[window, tile, here, :] = probs_low
                outs.append(dot(values[32 * head : 32 * (head + 1)], probs_low))
            mixed_s[at, TILE * tile : TILE * (tile + 1)] = jnp.concatenate(outs, axis=0).T
    mixed_low = mixed_s[...].astype(bf16)
    mixed[...] = mixed_low
    middle[...] = rows_s[...] + dot(mixed_low, proj_low[...]) + proj_bias[...]


def column_sum(values):
    return jnp.sum(values, axis=0, keepdims=True)


def store_halves(core, last, total, start, keep, send):
    half = total.shape[0] // 2
    at = slice(start, start + half)

    @pl.when(last & (core == 0))
    def _():
        keep[at, :] = total[0:half, :].astype(keep.dtype)
        send[at, :] = total[half : 2 * half, :].astype(bf16)

    @pl.when(last & (core != 0))
    def _():
        keep[at, :] = total[half : 2 * half, :].astype(keep.dtype)
        send[at, :] = total[0:half, :].astype(bf16)


def store_mixed_halves(core, last, first, second, keep, send):
    sizes = [first.shape[0] // 8, second.shape[0] // 8]

    for side in range(2):

        @pl.when(last & (core == side))
        def _():
            start = 0
            for quarter in range(4):
                for total, size in ((first, sizes[0]), (second, sizes[1])):
                    mine = (4 * side + quarter) * size
                    other = (4 * (1 - side) + quarter) * size
                    keep[start : start + size, :] = total[mine : mine + size, :].astype(keep.dtype)
                    send[start : start + size, :] = total[other : other + size, :].astype(bf16)
                    start += size


def middle_kernel(
    core, upstream, middle, mixed, up_weight, up_bias, down_weight, down_bias, proj, gain, shift,
    out, below, edge, middle_grad_out, mixed_grad, keep, send, up_bias_grad, proj_sums, gain_grad, shift_grad,
    windows_s, mixed_grad_s, up, down, ff_grad, proj_grad, normed_s, active_s, grad_s,
):
    part = pl.program_id(1)
    step = pl.program_id(0) * pl.num_programs(1) + part

    @pl.when(step == 0)
    def _():
        up[...] = up_weight[...].astype(bf16)
        down[...] = down_weight[...].astype(bf16)
        for ref in (ff_grad, proj_grad, up_bias_grad, proj_sums, gain_grad, shift_grad):
            ref[...] = jnp.zeros_like(ref)

    unit, rstd = norm_parts(middle[...])
    normed = (unit * gain[...] + shift[...]).astype(bf16)
    rows = pl.ds(pl.multiple_of(part * ROWS, 16), ROWS)
    given = upstream[rows, :]
    normed_s[rows, :] = normed
    result = middle[...] + down_bias[...]
    normed_grad = 0.0
    width, units = up.shape
    for start in range(0, units, width):
        at = slice(start, start + width)
        hidden = dot(normed, up[:, at]) + up_bias[:, at]
        under = 0.5 + 0.5 * lax.erf(hidden * (2.0**-0.5))
        active_low = (hidden * under).astype(bf16)
        slope = under + hidden * (jnp.exp2(hidden * hidden * (-0.5 * LOG2E)) * 0.3989422804014327)
        grad_low = (slope * dot(given, down[at, :], 1, 1)).astype(bf16)
        up_bias_grad[:, at] += column_sum(grad_low.astype(f32))
        active_s[rows, at] = active_low
        grad_s[rows, at] = grad_low
        result += dot(active_low, down[at, :])
        normed_grad += dot(grad_low, up[:, at], 1, 1)
    store_windows(windows_s, result, part)
    gain_grad[...] += column_sum(normed_grad * unit)
    shift_grad[...] += column_sum(normed_grad)
    middle_grad = norm_pull(normed_grad, unit, rstd, gain[...]) + given.astype(f32)
    middle_grad_out[...] = middle_grad
    branch_low = middle_grad.astype(bf16)
    proj_sums[...] += column_sum(branch_low.astype(f32))
    proj_grad[...] += dot(mixed[...], branch_low, 0, 0)
    mixed_grad_s[...] = dot(branch_low, proj[...], 1, 1)
    for window in range(GROUP):
        mixed_grad[window] = mixed_grad_s[PAD * window : PAD * (window + 1)].astype(bf16)

    @pl.when(part == pl.num_programs(1) - 1)
    def _():
        for start in range(0, units, width):
            at = slice(start, start + width)
            down_at = slice(units + start, units + start + width)
            ff_grad[at, :] += dot(normed_s[...], grad_s[:, at], 0, 0)
            ff_grad[down_at, :] += dot(active_s[:, at], upstream[...], 0, 0)

    windows_to_grid(windows_s, out, below, edge)
    last = step == pl.num_programs(0) * pl.num_programs(1) - 1
    store_mixed_halves(core[0], last, ff_grad, proj_grad, keep, send)


def attention_pull_kernel(core, normed_one, joined, probs, mixed_grad, *refs):
    joined_grad, keep, send, sums, bias_grad, joined_s, qkv_grad, bias_s = refs[-8:]

    @pl.when(pl.program_id(0) == 0)
    def _():
        for ref in (qkv_grad, sums, bias_s):
            ref[...] = jnp.zeros_like(ref)

    for tile in range(probs.shape[1]):
        lanes = 3 * TILE * tile
        for window in range(GROUP):
            at = slice(PAD * window, PAD * (window + 1))
            queries = joined[window, :, lanes : lanes + TILE]
            keys = joined[window, :, lanes + TILE : lanes + 2 * TILE]
            values = joined[window, :, lanes + 2 * TILE : lanes + 3 * TILE]
            grad = mixed_grad[window, :, TILE * tile : TILE * (tile + 1)]
            probs_grad = dot(spread_heads(values), grad, 1, 1)
            probs_low = probs[window, tile]
            parts = []
            for head in range(4):
                here = slice(PAD * head, PAD * (head + 1))
                prob = probs_low[here].astype(f32)
                product = prob * probs_grad[here]
                score_grad = product - prob * column_sum(product)
                bias_s[window, 4 * tile + head] += score_grad
                parts.append((score_grad * 32**-0.5).astype(bf16))
            draw = jnp.concatenate(parts, axis=0)
            keys = keys.T
            outs = [dot(keys[32 * head : 32 * (head + 1)], parts[head]) for head in range(4)]
            joined_s[at, lanes : lanes + TILE] = jnp.concatenate(outs, axis=0).T
            joined_s[at, lanes + TILE : lanes + 2 * TILE] = gather_heads(dot(draw, queries))
            joined_s[at, lanes + 2 * TILE : lanes + 3 * TILE] = gather_heads(dot(probs_low, grad))
    joined_low = joined_s[...].astype(bf16)
    joined_grad[...] = joined_low
    sums[...] += column_sum(joined_low.astype(f32))
    qkv_grad[...] += dot(normed_one[...], joined_low, 0, 0)
    last = pl.program_id(0) == pl.num_programs(0) - 1

    @pl.when(last)
    def _():
        for head in range(bias_grad.shape[0]):
            bias_grad[head] = (bias_s[0, head] + bias_s[1, head]) + (bias_s[2, head] + bias_s[3, head])

    for tile in range(probs.shape[1]):
        columns = qkv_grad.at[:, 3 * TILE * tile : 3 * TILE * (tile + 1)]
        half = columns.shape[0] // 2
        store_halves(core[0], last, columns, half * tile, keep, send)


def windows_to_grid(windows, out, below, edge):
    count, _, width = windows.shape
    cols = count * WIN
    window_row, last_row = pl.program_id(0), pl.num_programs(0) - 1

    @pl.when(pl.program_id(1) == pl.num_programs(1) - 1)
    def _():
        spot = lax.broadcasted_iota(jnp.int32, (cols + EDGE, 1), 0)
        col = spot - SHIFT
        window = (col * 205) >> 11
        valid = (col >= 0) & (col < cols)
        lane = lax.broadcasted_iota(jnp.int32, (cols + EDGE, count * 16), 1)
        for row in range(WIN):
            start = WIN * row // 8 * 8
            offset = WIN * row - start
            slab = windows[:, start : start + 16, :].reshape(count * 16, width).astype(bf16)
            target = jnp.where(valid, col + (16 - WIN) * window + offset, -1)
            moved_rows = dot((lane == target).astype(f32).astype(bf16), slab)
            main, side = moved_rows[0:cols].astype(bf16), moved_rows[cols : cols + EDGE].astype(bf16)
            at = WIN * window_row + row + SHIFT
            if row < WIN - SHIFT:
                out[at] = main
                edge[at] = side
            else:

                @pl.when(window_row < last_row)
                def _():
                    out[at] = main
                    edge[at] = side

                @pl.when(window_row == last_row)
                def _():
                    below[row - (WIN - SHIFT)] = moved_rows.astype(bf16)


def place_kernel(given, above, left, out, rows_s, cols_s, semaphores):
    cols, count = rows_s.shape[1], cols_s.shape[0]
    edge = out.at[pl.ds(SHIFT, count), pl.ds(0, EDGE), :]
    fetch = pltpu.make_async_copy(edge, cols_s, semaphores.at[0])
    fetch.start()
    first = lax.broadcasted_iota(jnp.int32, (1, EDGE, 1), 1) < SHIFT
    rows_s[:, 0:EDGE, :] = jnp.where(first, left[0:SHIFT], above[:, 0:EDGE, :])
    rows_s[:, EDGE:cols, :] = above[:, EDGE:cols, :]
    rows = pltpu.make_async_copy(rows_s, out.at[pl.ds(0, SHIFT)], semaphores.at[1])
    rows.start()
    fetch.wait()
    cols_s[...] = jnp.where(first, left[SHIFT : SHIFT + count], cols_s[...])
    store = pltpu.make_async_copy(cols_s, edge, semaphores.at[2])
    store.start()
    rows.wait()
    store.wait()


def store_windows(windows_s, values, part):
    for window in range(GROUP):
        windows_s[part * GROUP + window] = values[PAD * window : PAD * (window + 1)]


def inputs_grad_kernel(
    joined_grad, inputs, middle_grad, qkv, gain, out, below, edge, gain_grad, shift_grad, windows_s
):
    part = pl.program_id(1)

    @pl.when((pl.program_id(0) == 0) & (part == 0))
    def _():
        gain_grad[...] = jnp.zeros_like(gain_grad)
        shift_grad[...] = jnp.zeros_like(shift_grad)

    normed_grad = dot(joined_grad[...], qkv[...], 1, 1)
    unit, rstd = norm_parts(inputs[...].astype(f32))
    gain_grad[...] += column_sum(normed_grad * unit)
    shift_grad[...] += column_sum(normed_grad)
    store_windows(windows_s, norm_pull(normed_grad, unit, rstd, gain[...]) + middle_grad[...], part)
    windows_to_grid(windows_s, out, below, edge)


def flipped(value, row_bits, col_bits):
    rows, cols = lax.axis_size("row"), lax.axis_size("col")
    pairs = [(r * cols + c, (r ^ row_bits) * cols + (c ^ col_bits)) for r in range(rows) for c in range(cols)]
    return lax.ppermute(value, ("row", "col"), pairs)


def block(ref, index, rows):
    return ref[pl.ds(pl.multiple_of(index * rows, 8), rows), :]


def split_kernel(place, kept, got, *outs):
    total = kept[...].astype(f32) + got[...].astype(f32)
    for other in range(4):

        @pl.when(pl.program_id(0) == other)
        def _():
            outs[other][...] = total.astype(outs[other].dtype)


def split_again_kernel(place, kept, first, second, third, *refs):
    outs, total = refs[:-1], refs[-1]
    total[...] = kept[...] + first[...].astype(f32) + second[...].astype(f32) + third[...].astype(f32)
    rows = outs[0].shape[0]
    outs[0][...] = block(total, place[0], rows)
    for other in range(1, 4):
        outs[other][...] = block(total, place[0] ^ other, rows).astype(bf16)


def add_kernel(kept, first, second, third, *refs):
    out, rows = refs[-1], kept.shape[0]
    total = kept[...] + first[...].astype(f32) + second[...].astype(f32) + third[...].astype(f32)
    out[0:rows, :] = total.astype(out.dtype)


def pack_rows(vectors):
    columns, spots, at = 3 * TILE, [], 0
    for index, vector in enumerate(vectors):
        if vector.shape[0] > 1:
            at = -(-at // 8) * 8
            spots.append((index, None, 0, at, columns))
            at += vector.shape[0]
            continue
        for start in range(0, vector.shape[1], columns):
            spots.append((index, 0, start, at, min(columns, vector.shape[1] - start)))
            at += 1
    return spots, -(-at // 8) * 8


def pack(vectors, packed):
    packed[...] = jnp.zeros_like(packed)
    for index, row, start, at, size in pack_rows(vectors)[0]:
        if row is None:
            packed[at : at + vectors[index].shape[0], :] = vectors[index][...]
        else:
            packed[at : at + 1, 0:size] = vectors[index][:, start : start + size]


def pack_kernel(*refs):
    pack(refs[:-1], refs[-1])


def add_and_pack_kernel(kept, first, second, third, *refs):
    *vectors, out, packed = refs
    add_kernel(kept, first, second, third, out)
    pack(vectors, packed)
    store_pair(out, kept.shape[0], packed[...])


def store_pair(out, start, values):
    size = values.shape[0]
    high = values.astype(bf16)
    out[start : start + size, :] = high
    out[start + size : start + 2 * size, :] = (values - high.astype(f32)).astype(bf16)


def pair_sum(refs, start, size):
    total = 0.0
    for ref in refs:
        total += ref[start : start + size, :].astype(f32) + ref[start + size : start + 2 * size, :].astype(f32)
    return total


def join_kernel(place, *refs):
    pieces, out, joined_s = refs[:4], refs[4], refs[5]
    rows = joined_s.shape[0] // 4
    for other in range(4):
        at = pl.ds(pl.multiple_of((place[0] ^ other) * rows, 8), rows)
        joined_s[at, :] = pieces[other][0:rows, :].astype(f32)
    out[0 : 4 * rows, :] = joined_s[...].astype(bf16)
    extra = (pieces[0].shape[0] - rows) // 2
    if extra:
        store_pair(out, 4 * rows, pair_sum(pieces, rows, extra))


def scalar_call(kernel, scalar, *operands, outs, scratch=()):
    return pl.pallas_call(
        kernel,
        grid_spec=pltpu.PrefetchScalarGridSpec(
            num_scalar_prefetch=1,
            grid=(1,),
            in_specs=[IN_VMEM] * len(operands),
            out_specs=[IN_VMEM] * len(outs),
            scratch_shapes=list(scratch),
        ),
        out_shape=list(outs),
        compiler_params=params(),
            cost_estimate=SHORT,
    )(scalar, *operands)


def struct(shape, dtype):
    return jax.ShapeDtypeStruct(shape, dtype)


def places():
    row, col = lax.axis_index("row"), lax.axis_index("col")
    one = lambda value: jnp.reshape(value, (1,)).astype(jnp.int32)
    return one(col & 1), one(((col >> 1) & 1) | ((row & 1) << 1)), one((row >> 1) & 3)


class Order:
    def __init__(self):
        self.last = []

    def __call__(self, call, *operands):
        if self.last:
            operands, _ = lax.optimization_barrier((operands, self.last))
        results = call(*operands)
        self.last = [jax.tree.leaves(results)[0]]
        return results

    def later(self, value):
        return lax.optimization_barrier((value, self.last))[0]

    def hold(self, *values):
        self.last.extend(values)


def sum_over_devices(order, kept, sent, small_vectors=None):
    _, plane, depth = places()
    plane_flips = ((0, 2), (1, 0), (1, 2))
    depth_flips = ((2, 0), (4, 0), (6, 0))
    got = flipped(sent, 0, 1)
    rows, width = kept.shape
    quarter, small = rows // 4, rows // 16
    yield
    outs = [struct((quarter, width), f32)] + [struct((quarter, width), bf16)] * 3

    def split(*operands):
        block = pl.BlockSpec((quarter, width), lambda i, s: (s[0] ^ i, 0))
        return pl.pallas_call(
            split_kernel,
            grid_spec=pltpu.PrefetchScalarGridSpec(
                num_scalar_prefetch=1,
                grid=(4,),
                in_specs=[block] * 2,
                out_specs=[pl.BlockSpec((quarter, width), lambda i, s: (0, 0), pipeline_mode=pl.Buffered(1))] * 4,
            ),
            out_shape=outs,
            compiler_params=params(),
            cost_estimate=SHORT,
        )(plane, *operands)

    own, *sends = order(split, kept, got)
    got = [flipped(piece, *flip) for piece, flip in zip(sends, plane_flips)]
    yield
    outs = [struct((small, width), f32)] + [struct((small, width), bf16)] * 3
    call = functools.partial(
        scalar_call, split_again_kernel, depth, outs=outs, scratch=[pltpu.VMEM((quarter, width), f32)]
    )
    own, *sends = order(call, own, *got)
    got = [flipped(piece, *flip) for piece, flip in zip(sends, depth_flips)]
    yield got
    vectors = [] if small_vectors is None else small_vectors()
    packed_rows = pack_rows(vectors)[1]
    ride = 2 * packed_rows
    further = []
    bit = 8
    while bit < lax.axis_size("row"):
        further.append(bit)
        bit *= 2
    if further:
        call = pl.pallas_call(add_kernel, out_shape=struct((small, width), f32), cost_estimate=SHORT)
        done = order(call, own, *got)
        extra = []
        if vectors:
            extra = [pl.pallas_call(pack_kernel, out_shape=struct((packed_rows, width), f32))(*vectors)]
        for bit in further:
            done = done + flipped(done.astype(bf16), bit, 0).astype(f32)
            extra = [value + flipped(value, bit, 0) for value in extra]
        done = done.astype(bf16)
        for value in extra:
            high = lax.reduce_precision(value, 8, 7)
            done = jnp.concatenate((done, high.astype(bf16), (value - high).astype(bf16)))
    else:
        call = pl.pallas_call(
            add_and_pack_kernel if vectors else add_kernel,
            out_shape=struct((small + ride, width), bf16),
            in_specs=[IN_VMEM] * (4 + len(vectors)),
            out_specs=IN_VMEM,
            scratch_shapes=[pltpu.VMEM((packed_rows, width), f32)] if vectors else [],
            cost_estimate=SHORT,
        )
        done = order(call, own, *got, *vectors)
    pieces = [done] + [flipped(done, *flip) for flip in depth_flips]
    yield pieces
    call = functools.partial(
        scalar_call, join_kernel, depth, outs=[struct((quarter + ride, width), bf16)],
        scratch=[pltpu.VMEM((quarter, width), f32)],
    )
    (mine,) = order(call, *pieces)
    if vectors:
        mine = [mine] + [flipped(mine, *flip) for flip in plane_flips]
    else:
        mine = [mine] + [flipped(mine, *flip) for flip in plane_flips[:2]]
        yield mine
        mine.append(flipped(order.later(mine[2]), *plane_flips[0]))
    yield mine
    pieces = mine + [flipped(piece if vectors else order.later(piece), 0, 1) for piece in mine]
    yield pieces


def finish_kernel(write, plane, core, *refs):
    pieces, out, small_outs, (total, packed) = refs[:8], refs[8], refs[9:-2], refs[-2:]
    rows = total.shape[1] // 4
    for other in range(4):
        at = pl.ds(pl.multiple_of((plane[0] ^ other) * rows, 8), rows)
        total[core[0], at, :] = pieces[other][0:rows, :].astype(f32)
        total[1 - core[0], at, :] = pieces[4 + other][0:rows, :].astype(f32)
    write(total, out)
    packed[...] = pair_sum(pieces, rows, packed.shape[0])
    query_out, value_out, *vector_outs, table_out = small_outs
    for tile in range(TILES):
        at = slice(TILE * tile, TILE * (tile + 1))
        query_out[:, at] = packed[tile : tile + 1, 0:TILE]
        value_out[:, at] = packed[tile : tile + 1, 2 * TILE : 3 * TILE]
    table_rows = struct((table_out.shape[0], 3 * TILE), f32)
    spots, _ = pack_rows([struct((1, 3 * TILE * TILES), f32), *vector_outs, table_rows])
    for index, row, start, at, size in spots:
        if row is None:
            table_out[...] = packed[at : at + table_rows.shape[0], 0 : table_out.shape[1]]
        elif index > 0:
            vector_outs[index - 1][:, start : start + size] = packed[at : at + 1, 0:size]


def finish(order, pieces, write, outs, small_outs):
    core, plane, _ = places()
    rows, width = pieces[0].shape
    table = struct((small_outs[-1].shape[0], width), f32)
    packed_rows = pack_rows([struct((1, width * TILES), f32), *small_outs[2:-1], table])[1]
    outs = outs + small_outs

    def call(*operands):
        return pl.pallas_call(
            functools.partial(finish_kernel, write),
            grid_spec=pltpu.PrefetchScalarGridSpec(
                num_scalar_prefetch=2,
                grid=(1,),
                in_specs=[IN_VMEM] * len(pieces),
                out_specs=[pl.BlockSpec(a.shape, lambda i, s, t: (0, 0)) for a in outs],
                scratch_shapes=[
                    pltpu.VMEM((2, 4 * (rows - 2 * packed_rows), width), f32), pltpu.VMEM((packed_rows, width), f32),
                ],
            ),
            out_shape=outs,
            compiler_params=params(),
            cost_estimate=SHORT,
        )(plane, core, *operands)

    return order(call, *pieces)


def finish_middle_kernel(plane, core, *refs):
    pieces, (up_out, down_out, proj_out) = refs[:8], refs[8:]
    size = up_out.shape[1]
    rest = pieces[0].shape[0] - size
    for other in range(4):
        for side in range(2):

            @pl.when((pl.program_id(0) == other) & (core[0] == side))
            def _():
                ups, downs = pieces[other + 4 * side], pieces[other + 4 * (1 - side)]
                up_out[...] = ups[0:size, :].astype(f32)
                down_out[...] = downs[0:size, :].astype(f32)
                at = pl.multiple_of((plane[0] ^ other) * rest, 8)
                proj_out[pl.ds(at, rest), :] = ups[size:, :].astype(f32)
                proj_out[pl.ds(at + 4 * rest, rest), :] = downs[size:, :].astype(f32)


def finish_middle(order, pieces, width, units):
    core, plane, _ = places()

    def call(*operands):
        return pl.pallas_call(
            finish_middle_kernel,
            grid_spec=pltpu.PrefetchScalarGridSpec(
                num_scalar_prefetch=2,
                grid=(4,),
                in_specs=[pl.BlockSpec(a.shape, lambda i, s, t: (0, 0), pipeline_mode=pl.Buffered(1)) for a in pieces],
                out_specs=[
                    pl.BlockSpec((width, units // 4), lambda i, s, t: (0, s[0] ^ i)),
                    pl.BlockSpec((units // 4, width), lambda i, s, t: (s[0] ^ i, 0)),
                    pl.BlockSpec((width, width), lambda i, s, t: (0, 0)),
                ],
            ),
            out_shape=[struct((width, units), f32), struct((units, width), f32), struct((width, width), f32)],
            compiler_params=params(),
            cost_estimate=SHORT,
        )(plane, core, *operands)

    return order(call, *pieces)


def moved(value, row_step, col_step):
    rows, cols = lax.axis_size("row"), lax.axis_size("col")
    pairs = [
        (r * cols + c, ((r - row_step) % rows) * cols + (c - col_step) % cols) for r in range(rows) for c in range(cols)
    ]
    return lax.ppermute(value, ("row", "col"), pairs)


def relative_index():
    spots = jnp.arange(PLACES, dtype=jnp.int32)
    prow, pcol = spots // WIN, spots % WIN
    return (prow[None, :] - prow[:, None] + WIN - 1) * (2 * WIN - 1) + (pcol[None, :] - pcol[:, None] + WIN - 1)


def by_tile(array):
    return array.reshape(3, TILES, TILE).swapaxes(0, 1).reshape(1, 3 * TILES * TILE)


def thirds(values):
    terms = []
    for _ in range(3):
        term = lax.reduce_precision(values, 8, 7)
        terms.append(term.astype(bf16))
        values = values - term
    return jnp.concatenate(terms)


def exact_dot(values, onehot, dim):
    product = lax.dot_general(thirds(values), onehot, (((1,), (dim,)), ((), ())), preferred_element_type=f32)
    first, second, third = jnp.split(product, 3)
    return first + (second + third)


def body(
    patches, region_ids, qkv_weight, query_bias, value_bias, bias_table, proj_weight, proj_bias, gain_one, shift_one,
    gain_two, shift_two, up_weight, up_bias, down_weight, down_bias, cotangent,
):
    local_rows, local_cols, width = patches.shape
    heads = bias_table.shape[1]
    hidden_units = up_weight.shape[1]
    wrows, wcols = local_rows // WIN, local_cols // WIN
    windows = wrows * wcols
    tokens = windows * PAD
    steps = wcols // GROUP
    wide = -(-local_cols // 16) * 16
    row = lambda vector: vector[None]
    core, _, _ = places()
    order = Order()

    def prepare(first, second):
        rows_block = pl.BlockSpec((SHIFT, local_cols, width), lambda i: (0, 0, 0))
        cols_block = pl.BlockSpec((local_rows, EDGE, width), lambda i: (0, 0, 0))
        shapes = [(SHIFT, local_cols, width), (local_rows, EDGE, width), (SHIFT, EDGE, width)]
        return pl.pallas_call(
            prepare_kernel,
            grid=(1,),
            in_specs=[rows_block, cols_block] * 2,
            out_specs=[
                pl.BlockSpec((2,) + shape, lambda i: (0, 0, 0, 0)) for shape in shapes
            ],
            out_shape=[struct((2,) + shape, bf16) for shape in shapes],
            compiler_params=params(),
            cost_estimate=SHORT,
        )(first, first, second, second)

    edges = order(prepare, patches, cotangent)
    right, below, across = moved(edges[1], 0, 1), moved(edges[0], 1, 0), moved(edges[2], 1, 1)
    labels = region_ids.reshape(wrows, WIN, wcols, WIN).transpose(0, 2, 1, 3).reshape(windows, PLACES)
    labels = jnp.pad(labels, ((0, 0), (0, PAD - PLACES)), constant_values=-1)
    entries = -(-bias_table.shape[0] // TILE) * TILE
    onehot = (relative_index().reshape(-1)[:, None] == jnp.arange(entries, dtype=jnp.int32)[None, :]).astype(bf16)
    table = jnp.pad(bias_table.T, ((0, 0), (0, entries - bias_table.shape[0])))
    position_bias = exact_dot(table, onehot, 1).reshape(heads, PLACES, PLACES) * LOG2E
    position_bias = jnp.pad(position_bias, ((0, 0), (0, 0), (0, PAD - PLACES)))
    position_bias = jnp.pad(position_bias, ((0, 0), (0, PAD - PLACES), (0, 0)), constant_values=far_below)
    qkv_bias = by_tile(jnp.concatenate((query_bias, jnp.zeros_like(query_bias), value_bias)))

    token_arrays = [
        struct((tokens, width), bf16), struct((tokens, width), bf16), struct((windows, PAD, 3 * width), bf16),
        struct((windows, TILES, 4 * PAD, PAD), bf16), struct((tokens, width), bf16), struct((tokens, width), f32),
        struct((tokens, width), bf16),
    ]
    made, upstream_sums = [], []
    qkv_low, proj_low = qkv_weight, proj_weight
    labels = labels[:, None, :].astype(f32)
    for index in range(wrows):
        first, last = index == 0, index == wrows - 1
        block_of = lambda array: pl.BlockSpec(
            (array.shape[0] // (wrows * steps),) + array.shape[1:],
            lambda i, n=len(array.shape), index=index: (index * steps + i,) + (0,) * (n - 1),
        )
        specs = [
            spec for grid in range(2) for spec in halo_specs(2 * index + 1, last, local_cols, width, grid)
        ]
        operands = (
            position_bias, qkv_low, qkv_bias, proj_low, row(proj_bias), row(gain_one), row(shift_one),
        )
        lows = [struct(qkv_weight.shape, bf16), struct(proj_weight.shape, bf16)] if first else []
        call = pl.pallas_call(
            functools.partial(forward_kernel, local_cols, first),
            grid=(steps,),
            in_specs=specs + [block_of(labels)] + [whole(a) for a in operands]
            + [pl.BlockSpec(memory_space=pl.ANY)] * len(made),
            out_specs=[block_of(a) for a in token_arrays]
            + [pl.BlockSpec((1, width), lambda i: (0, 0))] + [whole(a) for a in lows],
            out_shape=token_arrays + [struct((1, width), f32)] + lows,
            input_output_aliases={16 + i: i for i in range(len(made))},
            scratch_shapes=[
                pltpu.VMEM((ROWS, width), f32), pltpu.VMEM((ROWS, 3 * width), f32), pltpu.VMEM((ROWS, width), f32),
            ],
            compiler_params=params(),
            cost_estimate=SHORT,
        )
        around = (patches, below if last else patches, right, across if last else right)
        around_grad = (cotangent, below if last else cotangent, right, across if last else right)
        outs = order(call, *around, *around_grad, labels, *operands, *made)
        made, total = outs[: len(token_arrays)], outs[len(token_arrays)]
        if first:
            qkv_low, proj_low = outs[-2:]
        upstream_sums.append(total)
    inputs, normed_one, joined, probs, mixed, middle, upstream = made
    down_bias_grad = sum(upstream_sums)
    rows_of = lambda columns: pl.BlockSpec((ROWS, columns), lambda i, *_: (i, 0))
    win_of = lambda *shape: pl.BlockSpec((GROUP,) + shape, lambda i, *_: (i,) + (0,) * len(shape))
    fixed = lambda array: pl.BlockSpec(array.shape, lambda i, *_: (0,) * len(array.shape))

    def core_call(kernel, in_specs, out_specs, out_shape, scratch, aliases):
        return pl.pallas_call(
            kernel,
            grid_spec=pltpu.PrefetchScalarGridSpec(
                num_scalar_prefetch=1,
                grid=(tokens // ROWS,),
                in_specs=in_specs,
                out_specs=out_specs,
                scratch_shapes=scratch,
            ),
            out_shape=out_shape,
            input_output_aliases=aliases,
            compiler_params=params(),
            cost_estimate=SHORT,
        )

    def attention_pull(tile, count, *made):
        rows, columns, at = width // 2 * count, 3 * TILE * count, tile // count
        outs = [
            struct((tokens, 3 * width), bf16), struct((width // 2 * TILES, 3 * TILE), bf16),
            struct((width // 2 * TILES, 3 * TILE), bf16), struct((1, 3 * width), f32), struct((heads, PAD, PAD), f32),
        ]
        part = heads // TILES * count
        call = core_call(
            attention_pull_kernel,
            [
                rows_of(width),
                pl.BlockSpec((GROUP, PAD, columns), lambda i, s: (i, 0, at)),
                pl.BlockSpec((GROUP, count, 4 * PAD, PAD), lambda i, s: (i, at, 0, 0)),
                pl.BlockSpec((GROUP, PAD, TILE * count), lambda i, s: (i, 0, at)),
            ]
            + [pl.BlockSpec(memory_space=pl.ANY)] * len(made),
            [
                pl.BlockSpec((ROWS, columns), lambda i, s: (i, at)),
                pl.BlockSpec((rows, 3 * TILE), lambda i, s: (at, 0)),
                pl.BlockSpec((rows, 3 * TILE), lambda i, s: (at, 0)),
                pl.BlockSpec((1, columns), lambda i, s: (0, at)),
                pl.BlockSpec((part, PAD, PAD), lambda i, s: (at, 0, 0)),
            ],
            outs,
            [
                pltpu.VMEM((ROWS, columns), f32), pltpu.VMEM((width, columns), f32),
                pltpu.VMEM((GROUP, part, PAD, PAD), f32),
            ],
            {5 + i: i for i in range(len(made))},
        )
        return order(call, core, normed_one, joined, probs, mixed_grad, *made)

    def write_qkv(total, out):
        rows = width // 2
        for side in range(2):
            for tile in range(TILES):
                for kind in range(3):
                    at = width * kind + TILE * tile
                    out[rows * side : rows * (side + 1), at : at + TILE] = (
                        total[side, rows * tile : rows * (tile + 1), TILE * kind : TILE * (kind + 1)]
                    )

    token_spec = lambda columns: pl.BlockSpec((ROWS, columns), lambda i, j, *_: (i * steps + j, 0))
    single = lambda array: pl.BlockSpec(
        array.shape, lambda *ids, n=len(array.shape): (0,) * n, pipeline_mode=pl.Buffered(1)
    )
    constant = lambda array: pl.BlockSpec(array.shape, lambda *ids, n=len(array.shape): (0,) * n)
    grid_outs = [
        struct((local_rows, local_cols, width), bf16), struct((SHIFT, local_cols + EDGE, width), bf16),
        struct((local_rows, EDGE, width), bf16),
    ]
    vector = struct((1, width), f32)

    def edge_out(above, edge):
        return moved(jnp.concatenate((above[:, local_cols:], edge[SHIFT:])), 0, -1)

    def place(grid, above, left):
        return order(
            pl.pallas_call(
                place_kernel,
                in_specs=[pl.BlockSpec(memory_space=pl.ANY), IN_VMEM, IN_VMEM],
                out_specs=pl.BlockSpec(memory_space=pl.ANY),
                out_shape=struct(grid.shape, grid.dtype),
                input_output_aliases={0: 0},
                scratch_shapes=[
                    pltpu.VMEM((SHIFT, local_cols, width), bf16), pltpu.VMEM((local_rows - SHIFT, EDGE, width), bf16),
                    pltpu.SemaphoreType.DMA((3,)),
                ],
                compiler_params=params(),
                cost_estimate=SHORT,
            ),
            grid, above, left,
        )

    shared = hidden_units + width // 2
    outs = [
        struct((shared, width), bf16), struct((shared, width), bf16), struct((1, hidden_units), f32), vector, vector,
        vector,
    ]
    call = pl.pallas_call(
        middle_kernel,
        grid_spec=pltpu.PrefetchScalarGridSpec(
            num_scalar_prefetch=1,
            grid=(wrows, steps),
            in_specs=[pl.BlockSpec((wcols * PAD, width), lambda i, j, s: (i, 0))] + [token_spec(width)] * 2
            + [single(up_weight), single(row(up_bias)), single(down_weight)]
            + [single(a) for a in (row(down_bias), proj_low, row(gain_two), row(shift_two))],
            out_specs=[single(a) for a in grid_outs]
            + [token_spec(width), pl.BlockSpec((GROUP, PAD, width), lambda i, j, s: (i * steps + j, 0, 0))]
            + [single(a) for a in outs],
            scratch_shapes=[
                pltpu.VMEM((wcols, PAD, width), f32), pltpu.VMEM((ROWS, width), f32), pltpu.VMEM(up_weight.shape, bf16),
                pltpu.VMEM(down_weight.shape, bf16), pltpu.VMEM((2 * hidden_units, width), f32),
                pltpu.VMEM((width, width), f32), pltpu.VMEM((wcols * PAD, width), bf16),
                pltpu.VMEM((wcols * PAD, hidden_units), bf16), pltpu.VMEM((wcols * PAD, hidden_units), bf16),
            ],
        ),
        out_shape=grid_outs + [struct((tokens, width), f32), struct((windows, PAD, width), bf16)] + outs,
        compiler_params=params(),
            cost_estimate=SHORT,
    )
    (
        result_grid, result_below, result_edge, middle_grad, mixed_grad, kept, sent, up_bias_grad, proj_sums, gain_two_grad, shift_two_grad,
    ) = order(
        call, core, upstream, middle, mixed, up_weight, row(up_bias), down_weight, row(down_bias), proj_low,
        row(gain_two), row(shift_two),
    )
    result_above = moved(result_below, -1, 0)
    first_sum = sum_over_devices(order, kept, sent)
    next(first_sum)
    next(first_sum)
    tiles = attention_pull(0, 3)
    order.hold(result_above)
    in_flight = next(first_sum)
    result_left = edge_out(order.later(result_above), result_edge)
    joined_grad, qkv_kept, qkv_sent, qkv_sums, bias_grad = attention_pull(3, 1, *tiles)
    qkv_sent, _ = lax.optimization_barrier((qkv_sent, in_flight))
    second_sum = sum_over_devices(order, qkv_kept, qkv_sent, lambda: vectors)
    next(second_sum)
    next(first_sum)
    next(second_sum)
    call = pl.pallas_call(
        inputs_grad_kernel,
        grid=(wrows, steps),
        in_specs=[token_spec(3 * width)] + [token_spec(width)] * 2 + [single(qkv_low), single(row(gain_one))],
        out_specs=[single(a) for a in grid_outs] + [single(vector)] * 2,
        out_shape=grid_outs + [vector] * 2,
        scratch_shapes=[pltpu.VMEM((wcols, PAD, width), f32)],
        compiler_params=params(),
            cost_estimate=SHORT,
    )
    grad_grid, grad_below, grad_edge, gain_one_grad, shift_one_grad = order(
        call, joined_grad, inputs, middle_grad, qkv_low, row(gain_one)
    )
    ff_pieces = next(first_sum)
    order.hold(result_left)
    next(second_sum)
    terms = order.later(bias_grad)[:, :PLACES, :PLACES].reshape(heads, -1)
    table_grad = exact_dot(terms, onehot, 0)
    vectors = [
        qkv_sums, proj_sums, gain_one_grad, shift_one_grad, gain_two_grad, shift_two_grad, up_bias_grad, down_bias_grad,
        table_grad,
    ]
    next(second_sum)
    order.hold(ff_pieces[2])
    ff_pieces = next(first_sum)
    next(second_sum)
    first_pieces = next(first_sum)
    grad_above = moved(order.later(grad_below), -1, 0)
    up_total, down_total, proj_total = finish_middle(order, first_pieces, width, hidden_units)
    result_out = place(result_grid, result_above, result_left)
    qkv_pieces = next(second_sum)
    grad_left = edge_out(order.later(grad_above), grad_edge)
    grad_out = place(grad_grid, grad_above, grad_left)
    (qkv_total, *small) = finish(
        order, qkv_pieces, write_qkv, [struct((width, 3 * width), f32)],
        [struct((1, width), f32)] * 2 + [struct(vector.shape, f32) for vector in vectors[1:-1]] + [struct(bias_table.shape[::-1], f32)],
    )
    query_grad, value_grad, proj_sum, gain_one, shift_one, gain_two, shift_two, up_sum, down_sum = [
        vector[0] for vector in small[:-1]
    ]
    return (
        result_out, grad_out, qkv_total, query_grad, value_grad, small[-1].T, proj_total, proj_sum, gain_one, shift_one,
        gain_two, shift_two, up_total, up_sum, down_total, down_sum,
    )


def solution(mesh):
    grid = P("row", "col", None)
    return jax.shard_map(
        body,
        mesh=mesh,
        in_specs=(grid, P("row", "col")) + (P(),) * 14 + (grid,),
        out_specs=(grid, grid) + (P(),) * 14,
        check_vma=False,
    )
```

```python
import functools

import jax
import jax.numpy as jnp
from jax import lax
from jax.experimental import pallas as pl
from jax.experimental.pallas import tpu as pltpu
from jax.sharding import PartitionSpec as P

WIN = 10
SHIFT = 5
PLACES = WIN * WIN
PAD = 104
GROUP = 4
ROWS = GROUP * PAD
SLAB = 32
EDGE = 16
TILE = 128
TILES = 4

norm_eps = 1e-05
far_below = -1000000000.0
LOG2E = 1.4426950408889634
bf16 = jnp.bfloat16
f32 = jnp.float32


def dot(left, right, left_dim=1, right_dim=0):
    return lax.dot_general(
        left, right, (((left_dim,), (right_dim,)), ((), ())), preferred_element_type=f32
    )


def whole(array):
    count = len(array.shape)
    return pl.BlockSpec(array.shape, lambda *ids: (0,) * count)


SHORT = pl.CostEstimate(flops=1, bytes_accessed=1, transcendentals=0)


IN_VMEM = pl.BlockSpec(memory_space=pltpu.VMEM)


def params():
    return pltpu.CompilerParams(vmem_limit_bytes=60 * 2**20)


def norm_parts(values):
    center = values - jnp.mean(values, axis=-1, keepdims=True)
    rstd = lax.rsqrt(jnp.mean(center * center, axis=-1, keepdims=True) + norm_eps)
    return center * rstd, rstd


def norm_pull(grad, unit, rstd, gain):
    scaled = grad * gain
    return rstd * (
        scaled
        - jnp.mean(scaled, axis=-1, keepdims=True)
        - unit * jnp.mean(scaled * unit, axis=-1, keepdims=True)
    )


def head_masks():
    lane = lax.broadcasted_iota(jnp.int32, (1, 128), 1) // 32
    return [(lane == head).astype(f32).astype(bf16) for head in range(4)]


def spread_heads(tile):
    return jnp.concatenate([tile * mask for mask in head_masks()], axis=0)


def gather_heads(stacked):
    lane = lax.broadcasted_iota(jnp.int32, (PAD, 128), 1) // 32
    out = stacked[0:PAD]
    for head in range(1, 4):
        out = jnp.where(lane == head, stacked[PAD * head : PAD * (head + 1)], out)
    return out


def prepare_kernel(*refs):
    rows_out, cols_out, corner_out = refs[4:]
    for index in range(2):
        rows, cols = refs[2 * index : 2 * index + 2]
        rows_out[index] = rows[...]
        cols_out[index] = cols[...]
        corner_out[index] = cols[0:SHIFT]


def window_rows(grids, local, col):
    count, wide, width = grids[0][0].shape
    first = col * WIN + SHIFT
    start = pl.multiple_of(jnp.minimum(first // 16 * 16, wide - SLAB), 16)
    half, side = count * SLAB, count * EDGE
    cols = pl.ds(start, SLAB)
    inside = lax.broadcasted_iota(jnp.int32, (1, SLAB, width), 1) + start < local
    place = lax.broadcasted_iota(jnp.int32, (PAD, 1), 0)
    prow = (place * 205) >> 11
    pcol = place - WIN * prow + first
    target = jnp.where(pcol < local, prow * SLAB + pcol - start, 2 * half + prow * EDGE + pcol - local)
    target = jnp.where(place < PLACES, target, -1)
    lane = lax.broadcasted_iota(jnp.int32, (PAD, 2 * (half + side)), 1)
    hot = (lane == target).astype(f32).astype(bf16)
    results = []
    for upper, lower, upper_right, lower_right in grids:
        slab = jnp.concatenate(
            (
                jnp.where(inside, upper[:, cols, :], 0).reshape(half, width),
                jnp.where(inside, lower[:, cols, :], 0).reshape(half, width),
                upper_right[...].reshape(side, width),
                lower_right[...].reshape(side, width),
            ),
            axis=0,
        )
        results.append(dot(hot, slab))
    return results


def halo_specs(block_row, last, local_cols, width, index):
    wide = -(-local_cols // 16) * 16
    own = lambda at: pl.BlockSpec((SHIFT, wide, width), lambda i: (at, 0, 0))
    came = lambda columns, at: pl.BlockSpec((None, SHIFT, columns, width), lambda i: (index, at, 0, 0))
    return [
        own(block_row),
        came(wide, 0) if last else own(block_row + 1),
        came(EDGE, block_row),
        came(EDGE, 0 if last else block_row + 1),
    ]


def forward_kernel(local, first, *refs):
    sources, grad_sources, refs = refs[0:4], refs[4:8], refs[8:]
    (
        label_row, bias, qkv, qkv_bias, proj, proj_bias, gain_one, shift_one, *refs
    ) = refs
    if not first:
        refs = refs[7:]
    inputs, normed_one, joined, probs, mixed, middle, upstream, upstream_sum, *refs = refs
    part = pl.program_id(0)
    if first:
        qkv_low, proj_low, *refs = refs

        @pl.when(part == 0)
        def _():
            for tile in range(TILES):
                for kind in range(3):
                    lanes = 3 * TILE * tile + TILE * kind
                    source = qkv.shape[0] * kind + TILE * tile
                    qkv_low[:, lanes : lanes + TILE] = qkv[:, source : source + TILE].astype(bf16)
            proj_low[...] = proj[...].astype(bf16)

    else:
        qkv_low, proj_low = qkv, proj
    rows_s, joined_s, mixed_s = refs

    @pl.when(part == 0)
    def _():
        upstream_sum[...] = jnp.zeros_like(upstream_sum)

    for window in range(GROUP):
        at = slice(PAD * window, PAD * (window + 1))
        rows_s[at, :], mixed_s[at, :] = window_rows((sources, grad_sources), local, part * GROUP + window)
    upstream[...] = mixed_s[...].astype(bf16)
    upstream_sum[...] += column_sum(mixed_s[...])
    rows = rows_s[...]
    inputs[...] = rows.astype(bf16)
    unit, _ = norm_parts(rows)
    normed = (unit * gain_one[...] + shift_one[...]).astype(bf16)
    normed_one[...] = normed
    joined_s[...] = dot(normed, qkv_low[...]) + qkv_bias[...]

    for window in range(GROUP):
        at = slice(PAD * window, PAD * (window + 1))
        joined[window] = joined_s[at, :].astype(bf16)
        labels = jnp.broadcast_to(label_row[window], (PAD, PAD))
        masked = jnp.where(labels.T == labels, 0.0, far_below)
        for tile in range(TILES):
            lanes = 3 * TILE * tile
            queries = joined_s[at, lanes : lanes + TILE].astype(bf16)
            keys = joined_s[at, lanes + TILE : lanes + 2 * TILE].astype(bf16)
            values = joined_s[at, lanes + 2 * TILE : lanes + 3 * TILE].astype(bf16).T
            raw = dot(spread_heads(keys), queries, 1, 1)
            outs = []
            for head in range(4):
                here = slice(PAD * head, PAD * (head + 1))
                scores = raw[here] * (LOG2E * 32**-0.5) + (bias[4 * tile + head] + masked)
                powers = jnp.exp2(scores - jnp.max(scores, axis=0, keepdims=True))
                total = jnp.sum(powers, axis=0, keepdims=True)
                probs_low = (powers * (1.0 / total)).astype(bf16)
                probs[window, tile, here, :] = probs_low
                outs.append(dot(values[32 * head : 32 * (head + 1)], probs_low))
            mixed_s[at, TILE * tile : TILE * (tile + 1)] = jnp.concatenate(outs, axis=0).T
    mixed_low = mixed_s[...].astype(bf16)
    mixed[...] = mixed_low
    middle[...] = rows_s[...] + dot(mixed_low, proj_low[...]) + proj_bias[...]


def column_sum(values):
    return jnp.sum(values, axis=0, keepdims=True)


def store_halves(core, last, total, start, keep, send):
    half = total.shape[0] // 2
    at = slice(start, start + half)

    @pl.when(last & (core == 0))
    def _():
        keep[at, :] = total[0:half, :].astype(keep.dtype)
        send[at, :] = total[half : 2 * half, :].astype(bf16)

    @pl.when(last & (core != 0))
    def _():
        keep[at, :] = total[half : 2 * half, :].astype(keep.dtype)
        send[at, :] = total[0:half, :].astype(bf16)


def store_mixed_halves(core, last, first, second, keep, send):
    sizes = [first.shape[0] // 8, second.shape[0] // 8]

    for side in range(2):

        @pl.when(last & (core == side))
        def _():
            start = 0
            for quarter in range(4):
                for total, size in ((first, sizes[0]), (second, sizes[1])):
                    mine = (4 * side + quarter) * size
                    other = (4 * (1 - side) + quarter) * size
                    keep[start : start + size, :] = total[mine : mine + size, :].astype(keep.dtype)
                    send[start : start + size, :] = total[other : other + size, :].astype(bf16)
                    start += size


def middle_kernel(
    core, upstream, middle, mixed, up_weight, up_bias, down_weight, down_bias, proj, gain, shift,
    out, below, edge, middle_grad_out, mixed_grad, keep, send, up_bias_grad, proj_sums, gain_grad, shift_grad,
    windows_s, mixed_grad_s, up, down, ff_grad, proj_grad, normed_s, active_s, grad_s,
):
    part = pl.program_id(1)
    step = pl.program_id(0) * pl.num_programs(1) + part

    @pl.when(step == 0)
    def _():
        up[...] = up_weight[...].astype(bf16)
        down[...] = down_weight[...].astype(bf16)
        for ref in (ff_grad, proj_grad, up_bias_grad, proj_sums, gain_grad, shift_grad):
            ref[...] = jnp.zeros_like(ref)

    unit, rstd = norm_parts(middle[...])
    normed = (unit * gain[...] + shift[...]).astype(bf16)
    rows = pl.ds(pl.multiple_of(part * ROWS, 16), ROWS)
    given = upstream[rows, :]
    normed_s[rows, :] = normed
    result = middle[...] + down_bias[...]
    normed_grad = 0.0
    width, units = up.shape
    for start in range(0, units, width):
        at = slice(start, start + width)
        hidden = dot(normed, up[:, at]) + up_bias[:, at]
        under = 0.5 + 0.5 * lax.erf(hidden * (2.0**-0.5))
        active_low = (hidden * under).astype(bf16)
        slope = under + hidden * (jnp.exp2(hidden * hidden * (-0.5 * LOG2E)) * 0.3989422804014327)
        grad_low = (slope * dot(given, down[at, :], 1, 1)).astype(bf16)
        up_bias_grad[:, at] += column_sum(grad_low.astype(f32))
        active_s[rows, at] = active_low
        grad_s[rows, at] = grad_low
        result += dot(active_low, down[at, :])
        normed_grad += dot(grad_low, up[:, at], 1, 1)
    store_windows(windows_s, result, part)
    gain_grad[...] += column_sum(normed_grad * unit)
    shift_grad[...] += column_sum(normed_grad)
    middle_grad = norm_pull(normed_grad, unit, rstd, gain[...]) + given.astype(f32)
    middle_grad_out[...] = middle_grad
    branch_low = middle_grad.astype(bf16)
    proj_sums[...] += column_sum(branch_low.astype(f32))
    proj_grad[...] += dot(mixed[...], branch_low, 0, 0)
    mixed_grad_s[...] = dot(branch_low, proj[...], 1, 1)
    for window in range(GROUP):
        mixed_grad[window] = mixed_grad_s[PAD * window : PAD * (window + 1)].astype(bf16)

    @pl.when(part == pl.num_programs(1) - 1)
    def _():
        for start in range(0, units, width):
            at = slice(start, start + width)
            down_at = slice(units + start, units + start + width)
            ff_grad[at, :] += dot(normed_s[...], grad_s[:, at], 0, 0)
            ff_grad[down_at, :] += dot(active_s[:, at], upstream[...], 0, 0)

    windows_to_grid(windows_s, out, below, edge)
    last = step == pl.num_programs(0) * pl.num_programs(1) - 1
    store_mixed_halves(core[0], last, ff_grad, proj_grad, keep, send)


def attention_pull_kernel(core, normed_one, joined, probs, mixed_grad, *refs):
    joined_grad, keep, send, sums, bias_grad, joined_s, qkv_grad, bias_s = refs[-8:]

    @pl.when(pl.program_id(0) == 0)
    def _():
        for ref in (qkv_grad, sums, bias_s):
            ref[...] = jnp.zeros_like(ref)

    for tile in range(probs.shape[1]):
        lanes = 3 * TILE * tile
        for window in range(GROUP):
            at = slice(PAD * window, PAD * (window + 1))
            queries = joined[window, :, lanes : lanes + TILE]
            keys = joined[window, :, lanes + TILE : lanes + 2 * TILE]
            values = joined[window, :, lanes + 2 * TILE : lanes + 3 * TILE]
            grad = mixed_grad[window, :, TILE * tile : TILE * (tile + 1)]
            probs_grad = dot(spread_heads(values), grad, 1, 1)
            probs_low = probs[window, tile]
            parts = []
            for head in range(4):
                here = slice(PAD * head, PAD * (head + 1))
                prob = probs_low[here].astype(f32)
                product = prob * probs_grad[here]
                score_grad = product - prob * column_sum(product)
                bias_s[window, 4 * tile + head] += score_grad
                parts.append((score_grad * 32**-0.5).astype(bf16))
            draw = jnp.concatenate(parts, axis=0)
            keys = keys.T
            outs = [dot(keys[32 * head : 32 * (head + 1)], parts[head]) for head in range(4)]
            joined_s[at, lanes : lanes + TILE] = jnp.concatenate(outs, axis=0).T
            joined_s[at, lanes + TILE : lanes + 2 * TILE] = gather_heads(dot(draw, queries))
            joined_s[at, lanes + 2 * TILE : lanes + 3 * TILE] = gather_heads(dot(probs_low, grad))
    joined_low = joined_s[...].astype(bf16)
    joined_grad[...] = joined_low
    sums[...] += column_sum(joined_low.astype(f32))
    qkv_grad[...] += dot(normed_one[...], joined_low, 0, 0)
    last = pl.program_id(0) == pl.num_programs(0) - 1

    @pl.when(last)
    def _():
        for head in range(bias_grad.shape[0]):
            bias_grad[head] = (bias_s[0, head] + bias_s[1, head]) + (bias_s[2, head] + bias_s[3, head])

    for tile in range(probs.shape[1]):
        columns = qkv_grad.at[:, 3 * TILE * tile : 3 * TILE * (tile + 1)]
        half = columns.shape[0] // 2
        store_halves(core[0], last, columns, half * tile, keep, send)


def windows_to_grid(windows, out, below, edge):
    count, _, width = windows.shape
    cols = count * WIN
    window_row, last_row = pl.program_id(0), pl.num_programs(0) - 1

    @pl.when(pl.program_id(1) == pl.num_programs(1) - 1)
    def _():
        spot = lax.broadcasted_iota(jnp.int32, (cols + EDGE, 1), 0)
        col = spot - SHIFT
        window = (col * 205) >> 11
        valid = (col >= 0) & (col < cols)
        lane = lax.broadcasted_iota(jnp.int32, (cols + EDGE, count * 16), 1)
        for row in range(WIN):
            start = WIN * row // 8 * 8
            offset = WIN * row - start
            slab = windows[:, start : start + 16, :].reshape(count * 16, width).astype(bf16)
            target = jnp.where(valid, col + (16 - WIN) * window + offset, -1)
            moved_rows = dot((lane == target).astype(f32).astype(bf16), slab)
            main, side = moved_rows[0:cols].astype(bf16), moved_rows[cols : cols + EDGE].astype(bf16)
            at = WIN * window_row + row + SHIFT
            if row < WIN - SHIFT:
                out[at] = main
                edge[at] = side
            else:

                @pl.when(window_row < last_row)
                def _():
                    out[at] = main
                    edge[at] = side

                @pl.when(window_row == last_row)
                def _():
                    below[row - (WIN - SHIFT)] = moved_rows.astype(bf16)


def place_kernel(given, above, left, out, rows_s, cols_s, semaphores):
    cols, count = rows_s.shape[1], cols_s.shape[0]
    edge = out.at[pl.ds(SHIFT, count), pl.ds(0, EDGE), :]
    fetch = pltpu.make_async_copy(edge, cols_s, semaphores.at[0])
    fetch.start()
    first = lax.broadcasted_iota(jnp.int32, (1, EDGE, 1), 1) < SHIFT
    rows_s[:, 0:EDGE, :] = jnp.where(first, left[0:SHIFT], above[:, 0:EDGE, :])
    rows_s[:, EDGE:cols, :] = above[:, EDGE:cols, :]
    rows = pltpu.make_async_copy(rows_s, out.at[pl.ds(0, SHIFT)], semaphores.at[1])
    rows.start()
    fetch.wait()
    cols_s[...] = jnp.where(first, left[SHIFT : SHIFT + count], cols_s[...])
    store = pltpu.make_async_copy(cols_s, edge, semaphores.at[2])
    store.start()
    rows.wait()
    store.wait()


def store_windows(windows_s, values, part):
    for window in range(GROUP):
        windows_s[part * GROUP + window] = values[PAD * window : PAD * (window + 1)]


def inputs_grad_kernel(
    joined_grad, inputs, middle_grad, qkv, gain, out, below, edge, gain_grad, shift_grad, windows_s
):
    part = pl.program_id(1)

    @pl.when((pl.program_id(0) == 0) & (part == 0))
    def _():
        gain_grad[...] = jnp.zeros_like(gain_grad)
        shift_grad[...] = jnp.zeros_like(shift_grad)

    normed_grad = dot(joined_grad[...], qkv[...], 1, 1)
    unit, rstd = norm_parts(inputs[...].astype(f32))
    gain_grad[...] += column_sum(normed_grad * unit)
    shift_grad[...] += column_sum(normed_grad)
    store_windows(windows_s, norm_pull(normed_grad, unit, rstd, gain[...]) + middle_grad[...], part)
    windows_to_grid(windows_s, out, below, edge)


def flipped(value, row_bits, col_bits):
    rows, cols = lax.axis_size("row"), lax.axis_size("col")
    pairs = [(r * cols + c, (r ^ row_bits) * cols + (c ^ col_bits)) for r in range(rows) for c in range(cols)]
    return lax.ppermute(value, ("row", "col"), pairs)


def block(ref, index, rows):
    return ref[pl.ds(pl.multiple_of(index * rows, 8), rows), :]


def split_kernel(place, kept, got, *outs):
    total = kept[...].astype(f32) + got[...].astype(f32)
    half = total.shape[0]
    for step in range(8):

        @pl.when(pl.program_id(0) == step)
        def _():
            out, start = outs[step // 2], half * (step % 2)
            out[start : start + half, :] = total.astype(out.dtype)


def split_again_kernel(place, kept, first, second, third, *refs):
    outs, total = refs[:-1], refs[-1]
    total[...] = kept[...] + first[...].astype(f32) + second[...].astype(f32) + third[...].astype(f32)
    rows = outs[0].shape[0]
    outs[0][...] = block(total, place[0], rows)
    for other in range(1, 4):
        outs[other][...] = block(total, place[0] ^ other, rows).astype(bf16)


def add_kernel(kept, first, second, third, *refs):
    out, rows = refs[-1], kept.shape[0]
    total = kept[...] + first[...].astype(f32) + second[...].astype(f32) + third[...].astype(f32)
    out[0:rows, :] = total.astype(out.dtype)


def pack_rows(vectors):
    columns, spots, at = 3 * TILE, [], 0
    for index, vector in enumerate(vectors):
        if vector.shape[0] > 1:
            at = -(-at // 8) * 8
            spots.append((index, None, 0, at, columns))
            at += vector.shape[0]
            continue
        for start in range(0, vector.shape[1], columns):
            spots.append((index, 0, start, at, min(columns, vector.shape[1] - start)))
            at += 1
    return spots, -(-at // 8) * 8


def pack(vectors, packed):
    packed[...] = jnp.zeros_like(packed)
    for index, row, start, at, size in pack_rows(vectors)[0]:
        if row is None:
            packed[at : at + vectors[index].shape[0], :] = vectors[index][...]
        else:
            packed[at : at + 1, 0:size] = vectors[index][:, start : start + size]


def pack_kernel(*refs):
    pack(refs[:-1], refs[-1])


def add_and_pack_kernel(kept, first, second, third, *refs):
    *vectors, out, packed = refs
    add_kernel(kept, first, second, third, out)
    pack(vectors, packed)
    store_pair(out, kept.shape[0], packed[...])


def store_pair(out, start, values):
    size = values.shape[0]
    high = values.astype(bf16)
    out[start : start + size, :] = high
    out[start + size : start + 2 * size, :] = (values - high.astype(f32)).astype(bf16)


def pair_sum(refs, start, size):
    total = 0.0
    for ref in refs:
        total += ref[start : start + size, :].astype(f32) + ref[start + size : start + 2 * size, :].astype(f32)
    return total


def join_kernel(place, *refs):
    pieces, out, joined_s = refs[:4], refs[4], refs[5]
    rows = joined_s.shape[0] // 4
    for other in range(4):
        at = pl.ds(pl.multiple_of((place[0] ^ other) * rows, 8), rows)
        joined_s[at, :] = pieces[other][0:rows, :].astype(f32)
    out[0 : 4 * rows, :] = joined_s[...].astype(bf16)
    extra = (pieces[0].shape[0] - rows) // 2
    if extra:
        store_pair(out, 4 * rows, pair_sum(pieces, rows, extra))


def scalar_call(kernel, scalar, *operands, outs, scratch=()):
    return pl.pallas_call(
        kernel,
        grid_spec=pltpu.PrefetchScalarGridSpec(
            num_scalar_prefetch=1,
            grid=(1,),
            in_specs=[IN_VMEM] * len(operands),
            out_specs=[IN_VMEM] * len(outs),
            scratch_shapes=list(scratch),
        ),
        out_shape=list(outs),
        compiler_params=params(),
            cost_estimate=SHORT,
    )(scalar, *operands)


def struct(shape, dtype):
    return jax.ShapeDtypeStruct(shape, dtype)


def places():
    row, col = lax.axis_index("row"), lax.axis_index("col")
    one = lambda value: jnp.reshape(value, (1,)).astype(jnp.int32)
    return one(col & 1), one(((col >> 1) & 1) | ((row & 1) << 1)), one((row >> 1) & 3)


class Order:
    def __init__(self):
        self.last = []

    def __call__(self, call, *operands):
        if self.last:
            operands, _ = lax.optimization_barrier((operands, self.last))
        results = call(*operands)
        self.last = [jax.tree.leaves(results)[0]]
        return results

    def later(self, value):
        return lax.optimization_barrier((value, self.last))[0]

    def hold(self, *values):
        self.last.extend(values)


def sum_over_devices(order, kept, sent, small_vectors=None):
    _, plane, depth = places()
    plane_flips = ((0, 2), (1, 0), (1, 2))
    depth_flips = ((2, 0), (4, 0), (6, 0))
    got = flipped(sent, 0, 1)
    rows, width = kept.shape
    quarter, small = rows // 4, rows // 16
    yield
    outs = [struct((quarter, width), f32)] + [struct((quarter, width), bf16)] * 3

    def split(*operands):
        block = pl.BlockSpec((quarter // 2, width), lambda i, s: (2 * (s[0] ^ (i // 2)) + i % 2, 0))
        return pl.pallas_call(
            split_kernel,
            grid_spec=pltpu.PrefetchScalarGridSpec(
                num_scalar_prefetch=1,
                grid=(8,),
                in_specs=[block] * 2,
                out_specs=[pl.BlockSpec((quarter, width), lambda i, s: (0, 0), pipeline_mode=pl.Buffered(1))] * 4,
            ),
            out_shape=outs,
            compiler_params=params(),
            cost_estimate=SHORT,
        )(plane, *operands)

    own, *sends = order(split, kept, got)
    got = [flipped(piece, *flip) for piece, flip in zip(sends, plane_flips)]
    yield
    outs = [struct((small, width), f32)] + [struct((small, width), bf16)] * 3
    call = functools.partial(
        scalar_call, split_again_kernel, depth, outs=outs, scratch=[pltpu.VMEM((quarter, width), f32)]
    )
    own, *sends = order(call, own, *got)
    got = [flipped(piece, *flip) for piece, flip in zip(sends, depth_flips)]
    yield got
    vectors = [] if small_vectors is None else small_vectors()
    packed_rows = pack_rows(vectors)[1]
    ride = 2 * packed_rows
    further = []
    bit = 8
    while bit < lax.axis_size("row"):
        further.append(bit)
        bit *= 2
    if further:
        call = pl.pallas_call(add_kernel, out_shape=struct((small, width), f32), cost_estimate=SHORT)
        done = order(call, own, *got)
        extra = []
        if vectors:
            extra = [pl.pallas_call(pack_kernel, out_shape=struct((packed_rows, width), f32))(*vectors)]
        for bit in further:
            done = done + flipped(done.astype(bf16), bit, 0).astype(f32)
            extra = [value + flipped(value, bit, 0) for value in extra]
        done = done.astype(bf16)
        for value in extra:
            high = lax.reduce_precision(value, 8, 7)
            done = jnp.concatenate((done, high.astype(bf16), (value - high).astype(bf16)))
    else:
        call = pl.pallas_call(
            add_and_pack_kernel if vectors else add_kernel,
            out_shape=struct((small + ride, width), bf16),
            in_specs=[IN_VMEM] * (4 + len(vectors)),
            out_specs=IN_VMEM,
            scratch_shapes=[pltpu.VMEM((packed_rows, width), f32)] if vectors else [],
            cost_estimate=SHORT,
        )
        done = order(call, own, *got, *vectors)
    pieces = [done] + [flipped(done, *flip) for flip in depth_flips]
    yield pieces
    call = functools.partial(
        scalar_call, join_kernel, depth, outs=[struct((quarter + ride, width), bf16)],
        scratch=[pltpu.VMEM((quarter, width), f32)],
    )
    (mine,) = order(call, *pieces)
    if vectors:
        mine = [mine] + [flipped(mine, *flip) for flip in plane_flips]
    else:
        mine = [mine] + [flipped(mine, *flip) for flip in plane_flips[:2]]
        yield mine
        mine.append(flipped(order.later(mine[2]), *plane_flips[0]))
    yield mine
    pieces = mine + [flipped(piece if vectors else order.later(piece), 0, 1) for piece in mine]
    yield pieces


def finish_kernel(write, plane, core, *refs):
    pieces, out, small_outs, (total, packed) = refs[:8], refs[8], refs[9:-2], refs[-2:]
    rows = total.shape[1] // 4
    for other in range(4):
        at = pl.ds(pl.multiple_of((plane[0] ^ other) * rows, 8), rows)
        total[core[0], at, :] = pieces[other][0:rows, :].astype(f32)
        total[1 - core[0], at, :] = pieces[4 + other][0:rows, :].astype(f32)
    write(total, out)
    packed[...] = pair_sum(pieces, rows, packed.shape[0])
    query_out, value_out, *vector_outs, table_out = small_outs
    for tile in range(TILES):
        at = slice(TILE * tile, TILE * (tile + 1))
        query_out[:, at] = packed[tile : tile + 1, 0:TILE]
        value_out[:, at] = packed[tile : tile + 1, 2 * TILE : 3 * TILE]
    table_rows = struct((table_out.shape[0], 3 * TILE), f32)
    spots, _ = pack_rows([struct((1, 3 * TILE * TILES), f32), *vector_outs, table_rows])
    for index, row, start, at, size in spots:
        if row is None:
            table_out[...] = packed[at : at + table_rows.shape[0], 0 : table_out.shape[1]]
        elif index > 0:
            vector_outs[index - 1][:, start : start + size] = packed[at : at + 1, 0:size]


def finish(order, pieces, write, outs, small_outs):
    core, plane, _ = places()
    rows, width = pieces[0].shape
    table = struct((small_outs[-1].shape[0], width), f32)
    packed_rows = pack_rows([struct((1, width * TILES), f32), *small_outs[2:-1], table])[1]
    outs = outs + small_outs

    def call(*operands):
        return pl.pallas_call(
            functools.partial(finish_kernel, write),
            grid_spec=pltpu.PrefetchScalarGridSpec(
                num_scalar_prefetch=2,
                grid=(1,),
                in_specs=[IN_VMEM] * len(pieces),
                out_specs=[pl.BlockSpec(a.shape, lambda i, s, t: (0, 0)) for a in outs],
                scratch_shapes=[
                    pltpu.VMEM((2, 4 * (rows - 2 * packed_rows), width), f32), pltpu.VMEM((packed_rows, width), f32),
                ],
            ),
            out_shape=outs,
            compiler_params=params(),
            cost_estimate=SHORT,
        )(plane, core, *operands)

    return order(call, *pieces)


def finish_middle_kernel(plane, core, *refs):
    pieces, (up_out, down_out, proj_out) = refs[:8], refs[8:]
    size = up_out.shape[1]
    rest = pieces[0].shape[0] - size
    for other in range(4):
        for side in range(2):

            @pl.when((pl.program_id(0) == other) & (core[0] == side))
            def _():
                ups, downs = pieces[other + 4 * side], pieces[other + 4 * (1 - side)]
                up_out[...] = ups[0:size, :].astype(f32)
                down_out[...] = downs[0:size, :].astype(f32)
                at = pl.multiple_of((plane[0] ^ other) * rest, 8)
                proj_out[pl.ds(at, rest), :] = ups[size:, :].astype(f32)
                proj_out[pl.ds(at + 4 * rest, rest), :] = downs[size:, :].astype(f32)


def finish_middle(order, pieces, width, units):
    core, plane, _ = places()

    def call(*operands):
        return pl.pallas_call(
            finish_middle_kernel,
            grid_spec=pltpu.PrefetchScalarGridSpec(
                num_scalar_prefetch=2,
                grid=(4,),
                in_specs=[pl.BlockSpec(a.shape, lambda i, s, t: (0, 0), pipeline_mode=pl.Buffered(1)) for a in pieces],
                out_specs=[
                    pl.BlockSpec((width, units // 4), lambda i, s, t: (0, s[0] ^ i)),
                    pl.BlockSpec((units // 4, width), lambda i, s, t: (s[0] ^ i, 0)),
                    pl.BlockSpec((width, width), lambda i, s, t: (0, 0)),
                ],
            ),
            out_shape=[struct((width, units), f32), struct((units, width), f32), struct((width, width), f32)],
            compiler_params=params(),
            cost_estimate=SHORT,
        )(plane, core, *operands)

    return order(call, *pieces)


def moved(value, row_step, col_step):
    rows, cols = lax.axis_size("row"), lax.axis_size("col")
    pairs = [
        (r * cols + c, ((r - row_step) % rows) * cols + (c - col_step) % cols) for r in range(rows) for c in range(cols)
    ]
    return lax.ppermute(value, ("row", "col"), pairs)


def relative_index():
    spots = jnp.arange(PLACES, dtype=jnp.int32)
    prow, pcol = spots // WIN, spots % WIN
    return (prow[None, :] - prow[:, None] + WIN - 1) * (2 * WIN - 1) + (pcol[None, :] - pcol[:, None] + WIN - 1)


def by_tile(array):
    return array.reshape(3, TILES, TILE).swapaxes(0, 1).reshape(1, 3 * TILES * TILE)


def thirds(values):
    terms = []
    for _ in range(3):
        term = lax.reduce_precision(values, 8, 7)
        terms.append(term.astype(bf16))
        values = values - term
    return jnp.concatenate(terms)


def exact_dot(values, onehot, dim):
    product = lax.dot_general(thirds(values), onehot, (((1,), (dim,)), ((), ())), preferred_element_type=f32)
    first, second, third = jnp.split(product, 3)
    return first + (second + third)


def body(
    patches, region_ids, qkv_weight, query_bias, value_bias, bias_table, proj_weight, proj_bias, gain_one, shift_one,
    gain_two, shift_two, up_weight, up_bias, down_weight, down_bias, cotangent,
):
    local_rows, local_cols, width = patches.shape
    heads = bias_table.shape[1]
    hidden_units = up_weight.shape[1]
    wrows, wcols = local_rows // WIN, local_cols // WIN
    windows = wrows * wcols
    tokens = windows * PAD
    steps = wcols // GROUP
    wide = -(-local_cols // 16) * 16
    row = lambda vector: vector[None]
    core, _, _ = places()
    order = Order()

    def prepare(first, second):
        rows_block = pl.BlockSpec((SHIFT, local_cols, width), lambda i: (0, 0, 0))
        cols_block = pl.BlockSpec((local_rows, EDGE, width), lambda i: (0, 0, 0))
        shapes = [(SHIFT, local_cols, width), (local_rows, EDGE, width), (SHIFT, EDGE, width)]
        return pl.pallas_call(
            prepare_kernel,
            grid=(1,),
            in_specs=[rows_block, cols_block] * 2,
            out_specs=[
                pl.BlockSpec((2,) + shape, lambda i: (0, 0, 0, 0)) for shape in shapes
            ],
            out_shape=[struct((2,) + shape, bf16) for shape in shapes],
            compiler_params=params(),
            cost_estimate=SHORT,
        )(first, first, second, second)

    edges = order(prepare, patches, cotangent)
    right, below, across = moved(edges[1], 0, 1), moved(edges[0], 1, 0), moved(edges[2], 1, 1)
    labels = region_ids.reshape(wrows, WIN, wcols, WIN).transpose(0, 2, 1, 3).reshape(windows, PLACES)
    labels = jnp.pad(labels, ((0, 0), (0, PAD - PLACES)), constant_values=-1)
    entries = -(-bias_table.shape[0] // TILE) * TILE
    onehot = (relative_index().reshape(-1)[:, None] == jnp.arange(entries, dtype=jnp.int32)[None, :]).astype(bf16)
    table = jnp.pad(bias_table.T, ((0, 0), (0, entries - bias_table.shape[0])))
    position_bias = exact_dot(table, onehot, 1).reshape(heads, PLACES, PLACES) * LOG2E
    position_bias = jnp.pad(position_bias, ((0, 0), (0, 0), (0, PAD - PLACES)))
    position_bias = jnp.pad(position_bias, ((0, 0), (0, PAD - PLACES), (0, 0)), constant_values=far_below)
    qkv_bias = by_tile(jnp.concatenate((query_bias, jnp.zeros_like(query_bias), value_bias)))

    token_arrays = [
        struct((tokens, width), bf16), struct((tokens, width), bf16), struct((windows, PAD, 3 * width), bf16),
        struct((windows, TILES, 4 * PAD, PAD), bf16), struct((tokens, width), bf16), struct((tokens, width), f32),
        struct((tokens, width), bf16),
    ]
    made, upstream_sums = [], []
    qkv_low, proj_low = qkv_weight, proj_weight
    labels = labels[:, None, :].astype(f32)
    for index in range(wrows):
        first, last = index == 0, index == wrows - 1
        block_of = lambda array: pl.BlockSpec(
            (array.shape[0] // (wrows * steps),) + array.shape[1:],
            lambda i, n=len(array.shape), index=index: (index * steps + i,) + (0,) * (n - 1),
        )
        specs = [
            spec for grid in range(2) for spec in halo_specs(2 * index + 1, last, local_cols, width, grid)
        ]
        operands = (
            position_bias, qkv_low, qkv_bias, proj_low, row(proj_bias), row(gain_one), row(shift_one),
        )
        lows = [struct(qkv_weight.shape, bf16), struct(proj_weight.shape, bf16)] if first else []
        call = pl.pallas_call(
            functools.partial(forward_kernel, local_cols, first),
            grid=(steps,),
            in_specs=specs + [block_of(labels)] + [whole(a) for a in operands]
            + [pl.BlockSpec(memory_space=pl.ANY)] * len(made),
            out_specs=[block_of(a) for a in token_arrays]
            + [pl.BlockSpec((1, width), lambda i: (0, 0))] + [whole(a) for a in lows],
            out_shape=token_arrays + [struct((1, width), f32)] + lows,
            input_output_aliases={16 + i: i for i in range(len(made))},
            scratch_shapes=[
                pltpu.VMEM((ROWS, width), f32), pltpu.VMEM((ROWS, 3 * width), f32), pltpu.VMEM((ROWS, width), f32),
            ],
            compiler_params=params(),
            cost_estimate=SHORT,
        )
        around = (patches, below if last else patches, right, across if last else right)
        around_grad = (cotangent, below if last else cotangent, right, across if last else right)
        outs = order(call, *around, *around_grad, labels, *operands, *made)
        made, total = outs[: len(token_arrays)], outs[len(token_arrays)]
        if first:
            qkv_low, proj_low = outs[-2:]
        upstream_sums.append(total)
    inputs, normed_one, joined, probs, mixed, middle, upstream = made
    down_bias_grad = sum(upstream_sums)
    rows_of = lambda columns: pl.BlockSpec((ROWS, columns), lambda i, *_: (i, 0))
    win_of = lambda *shape: pl.BlockSpec((GROUP,) + shape, lambda i, *_: (i,) + (0,) * len(shape))
    fixed = lambda array: pl.BlockSpec(array.shape, lambda i, *_: (0,) * len(array.shape))

    def core_call(kernel, in_specs, out_specs, out_shape, scratch, aliases):
        return pl.pallas_call(
            kernel,
            grid_spec=pltpu.PrefetchScalarGridSpec(
                num_scalar_prefetch=1,
                grid=(tokens // ROWS,),
                in_specs=in_specs,
                out_specs=out_specs,
                scratch_shapes=scratch,
            ),
            out_shape=out_shape,
            input_output_aliases=aliases,
            compiler_params=params(),
            cost_estimate=SHORT,
        )

    def attention_pull(tile, count, *made):
        rows, columns, at = width // 2 * count, 3 * TILE * count, tile // count
        outs = [
            struct((tokens, 3 * width), bf16), struct((width // 2 * TILES, 3 * TILE), bf16),
            struct((width // 2 * TILES, 3 * TILE), bf16), struct((1, 3 * width), f32), struct((heads, PAD, PAD), f32),
        ]
        part = heads // TILES * count
        call = core_call(
            attention_pull_kernel,
            [
                rows_of(width),
                pl.BlockSpec((GROUP, PAD, columns), lambda i, s: (i, 0, at)),
                pl.BlockSpec((GROUP, count, 4 * PAD, PAD), lambda i, s: (i, at, 0, 0)),
                pl.BlockSpec((GROUP, PAD, TILE * count), lambda i, s: (i, 0, at)),
            ]
            + [pl.BlockSpec(memory_space=pl.ANY)] * len(made),
            [
                pl.BlockSpec((ROWS, columns), lambda i, s: (i, at)),
                pl.BlockSpec((rows, 3 * TILE), lambda i, s: (at, 0)),
                pl.BlockSpec((rows, 3 * TILE), lambda i, s: (at, 0)),
                pl.BlockSpec((1, columns), lambda i, s: (0, at)),
                pl.BlockSpec((part, PAD, PAD), lambda i, s: (at, 0, 0)),
            ],
            outs,
            [
                pltpu.VMEM((ROWS, columns), f32), pltpu.VMEM((width, columns), f32),
                pltpu.VMEM((GROUP, part, PAD, PAD), f32),
            ],
            {5 + i: i for i in range(len(made))},
        )
        return order(call, core, normed_one, joined, probs, mixed_grad, *made)

    def write_qkv(total, out):
        rows = width // 2
        for side in range(2):
            for tile in range(TILES):
                for kind in range(3):
                    at = width * kind + TILE * tile
                    out[rows * side : rows * (side + 1), at : at + TILE] = (
                        total[side, rows * tile : rows * (tile + 1), TILE * kind : TILE * (kind + 1)]
                    )

    token_spec = lambda columns: pl.BlockSpec((ROWS, columns), lambda i, j, *_: (i * steps + j, 0))
    single = lambda array: pl.BlockSpec(
        array.shape, lambda *ids, n=len(array.shape): (0,) * n, pipeline_mode=pl.Buffered(1)
    )
    constant = lambda array: pl.BlockSpec(array.shape, lambda *ids, n=len(array.shape): (0,) * n)
    grid_outs = [
        struct((local_rows, local_cols, width), bf16), struct((SHIFT, local_cols + EDGE, width), bf16),
        struct((local_rows, EDGE, width), bf16),
    ]
    vector = struct((1, width), f32)

    def edge_out(above, edge):
        return moved(jnp.concatenate((above[:, local_cols:], edge[SHIFT:])), 0, -1)

    def place(grid, above, left):
        return order(
            pl.pallas_call(
                place_kernel,
                in_specs=[pl.BlockSpec(memory_space=pl.ANY), IN_VMEM, IN_VMEM],
                out_specs=pl.BlockSpec(memory_space=pl.ANY),
                out_shape=struct(grid.shape, grid.dtype),
                input_output_aliases={0: 0},
                scratch_shapes=[
                    pltpu.VMEM((SHIFT, local_cols, width), bf16), pltpu.VMEM((local_rows - SHIFT, EDGE, width), bf16),
                    pltpu.SemaphoreType.DMA((3,)),
                ],
                compiler_params=params(),
                cost_estimate=SHORT,
            ),
            grid, above, left,
        )

    shared = hidden_units + width // 2
    outs = [
        struct((shared, width), bf16), struct((shared, width), bf16), struct((1, hidden_units), f32), vector, vector,
        vector,
    ]
    call = pl.pallas_call(
        middle_kernel,
        grid_spec=pltpu.PrefetchScalarGridSpec(
            num_scalar_prefetch=1,
            grid=(wrows, steps),
            in_specs=[pl.BlockSpec((wcols * PAD, width), lambda i, j, s: (i, 0))] + [token_spec(width)] * 2
            + [single(up_weight), single(row(up_bias)), single(down_weight)]
            + [single(a) for a in (row(down_bias), proj_low, row(gain_two), row(shift_two))],
            out_specs=[single(a) for a in grid_outs]
            + [token_spec(width), pl.BlockSpec((GROUP, PAD, width), lambda i, j, s: (i * steps + j, 0, 0))]
            + [single(a) for a in outs],
            scratch_shapes=[
                pltpu.VMEM((wcols, PAD, width), f32), pltpu.VMEM((ROWS, width), f32), pltpu.VMEM(up_weight.shape, bf16),
                pltpu.VMEM(down_weight.shape, bf16), pltpu.VMEM((2 * hidden_units, width), f32),
                pltpu.VMEM((width, width), f32), pltpu.VMEM((wcols * PAD, width), bf16),
                pltpu.VMEM((wcols * PAD, hidden_units), bf16), pltpu.VMEM((wcols * PAD, hidden_units), bf16),
            ],
        ),
        out_shape=grid_outs + [struct((tokens, width), f32), struct((windows, PAD, width), bf16)] + outs,
        compiler_params=params(),
            cost_estimate=SHORT,
    )
    (
        result_grid, result_below, result_edge, middle_grad, mixed_grad, kept, sent, up_bias_grad, proj_sums, gain_two_grad, shift_two_grad,
    ) = order(
        call, core, upstream, middle, mixed, up_weight, row(up_bias), down_weight, row(down_bias), proj_low,
        row(gain_two), row(shift_two),
    )
    result_above = moved(result_below, -1, 0)
    first_sum = sum_over_devices(order, kept, sent)
    next(first_sum)
    next(first_sum)
    tiles = attention_pull(0, 3)
    order.hold(result_above)
    in_flight = next(first_sum)
    result_left = edge_out(order.later(result_above), result_edge)
    joined_grad, qkv_kept, qkv_sent, qkv_sums, bias_grad = attention_pull(3, 1, *tiles)
    qkv_sent, _ = lax.optimization_barrier((qkv_sent, in_flight))
    second_sum = sum_over_devices(order, qkv_kept, qkv_sent, lambda: vectors)
    next(second_sum)
    next(first_sum)
    next(second_sum)
    call = pl.pallas_call(
        inputs_grad_kernel,
        grid=(wrows, steps),
        in_specs=[token_spec(3 * width)] + [token_spec(width)] * 2 + [single(qkv_low), single(row(gain_one))],
        out_specs=[single(a) for a in grid_outs] + [single(vector)] * 2,
        out_shape=grid_outs + [vector] * 2,
        scratch_shapes=[pltpu.VMEM((wcols, PAD, width), f32)],
        compiler_params=params(),
            cost_estimate=SHORT,
    )
    grad_grid, grad_below, grad_edge, gain_one_grad, shift_one_grad = order(
        call, joined_grad, inputs, middle_grad, qkv_low, row(gain_one)
    )
    ff_pieces = next(first_sum)
    order.hold(result_left)
    next(second_sum)
    terms = order.later(bias_grad)[:, :PLACES, :PLACES].reshape(heads, -1)
    table_grad = exact_dot(terms, onehot, 0)
    vectors = [
        qkv_sums, proj_sums, gain_one_grad, shift_one_grad, gain_two_grad, shift_two_grad, up_bias_grad, down_bias_grad,
        table_grad,
    ]
    next(second_sum)
    order.hold(ff_pieces[2])
    ff_pieces = next(first_sum)
    next(second_sum)
    first_pieces = next(first_sum)
    grad_above = moved(order.later(grad_below), -1, 0)
    up_total, down_total, proj_total = finish_middle(order, first_pieces, width, hidden_units)
    result_out = place(result_grid, result_above, result_left)
    qkv_pieces = next(second_sum)
    grad_left = edge_out(order.later(grad_above), grad_edge)
    grad_out = place(grad_grid, grad_above, grad_left)
    (qkv_total, *small) = finish(
        order, qkv_pieces, write_qkv, [struct((width, 3 * width), f32)],
        [struct((1, width), f32)] * 2 + [struct(vector.shape, f32) for vector in vectors[1:-1]] + [struct(bias_table.shape[::-1], f32)],
    )
    query_grad, value_grad, proj_sum, gain_one, shift_one, gain_two, shift_two, up_sum, down_sum = [
        vector[0] for vector in small[:-1]
    ]
    return (
        result_out, grad_out, qkv_total, query_grad, value_grad, small[-1].T, proj_total, proj_sum, gain_one, shift_one,
        gain_two, shift_two, up_total, up_sum, down_total, down_sum,
    )


def solution(mesh):
    grid = P("row", "col", None)
    return jax.shard_map(
        body,
        mesh=mesh,
        in_specs=(grid, P("row", "col")) + (P(),) * 14 + (grid,),
        out_specs=(grid, grid) + (P(),) * 14,
        check_vma=False,
    )
```
